32 devices in a mesh: runs: 2 (over x), gx: 16 (over z, y, core).
Axes of the slice: x: 2, y: 2, z: 4, core: 2. Of those that a mesh axis runs over, the one named last changes fastest.
Arguments:
- inputs: bfloat16 [1024, 6144], P('runs', 'gx'), parts along dimension 0, may hold values from -6 to 6
- out_grad: bfloat16 [1024, 6144], P('runs', 'gx'), parts along dimension 0, may hold values from -1.5 to 1.5
- w_qkv: bfloat16 [6144, 3, 8192], P(None, None, 'gx'), may hold values from -0.109375 to 0.109375
- w_out: bfloat16 [8192, 6144], P('gx'), may hold values from -0.0625 to 0.0625
- saved_qkv: bfloat16 [1024, 3, 8192], P('runs', None, 'gx'), parts along dimension 0, may hold values from -30 to 30
- positions: int32 [1024], P('runs'), parts along dimension 0, may hold values from 0 to 511, as said below
Outputs:
- input_grad: bfloat16 [1024, 6144], P('runs', 'gx'), parts along dimension 0
- grad_w_qkv: bfloat16 [12288, 3, 8192], P('runs', None, 'gx'), parts along dimension 0
- grad_w_out: bfloat16 [16384, 6144], P(('runs', 'gx')), parts along dimension 0
The draws below stay inside these ranges and needn't reach their ends.
There are 2 independent parts, one for each index of `runs`. The reference program is written for one: setup_inputs(seed, part) draws one part's arguments, and reference() takes and returns one part's arrays. A program takes and returns all parts, laid end to end along the dimension named above; an argument that names none is the same for every part. Nothing has to cross between parts.
Inputs may be any that keep to these rules, and one draw needn't show every extreme that they name: `positions`: each of 0 to 511 appears once.
All inputs are finite; a program needn't handle non-finite values.
Results may differ from the reference program's by a relative error of at most 0.018.
Values may be sent and summed in bfloat16 or wider, within the bound.
No kernel may reach another device: no remote copies, remote signals or barrier semaphores. Data moves between devices by JAX's collectives and lax.ppermute only.
A program may use at most 192 MiB of HBM per device.

```python
import math
import jax
import jax.numpy as jnp
from jax import lax

D = 6144
HEADS = 64
HD = 128
SEQ = 512


def token_order(key):
    return jax.random.permutation(jax.random.fold_in(key, 7), SEQ).astype(jnp.int32)


def draw_positions(key, part):
    return token_order(key)


def draw_saved_qkv(key, part):
    key = jax.random.fold_in(key, 2)
    columns = HEADS * HD
    result = jax.random.normal(jax.random.fold_in(key, 1), (SEQ, 3, columns), jnp.float32)
    return jnp.clip(result, -30.0, 30.0).astype(jnp.bfloat16)


def strengthened(values, stream_key, source, target, parts, factor):
    def block_of(position):
        return (jnp.arange(values.shape[position]) // (values.shape[position] // parts)).reshape((-1,) + (1,) * (values.ndim - 1 - position))

    first = jax.random.permutation(stream_key, parts)[block_of(target)]
    second = (block_of(target) + parts // 2) % parts
    return jnp.where((block_of(source) == first) | (block_of(source) == second), factor * values, values)


def steps_of(stream_key, extent, cuts, low, high):
    level = 1.0
    for position, shards_of in cuts:
        heights = jax.random.uniform(jax.random.fold_in(jax.random.fold_in(stream_key, 6), position), (shards_of,), jnp.float32, low / len(cuts), high / len(cuts))
        level = level * jnp.repeat(jnp.exp(heights), extent[position] // shards_of).reshape((-1,) + (1,) * (len(extent) - 1 - position))
    return level


def normal_values(stream_key, extent, scale, limit, split=(), kind=jnp.bfloat16):
    gain = steps_of(stream_key, extent, split, -0.22, 0.18) if split else 1.0
    entries = jax.random.normal(stream_key, extent, jnp.float32) * scale * gain
    return jnp.minimum(jnp.maximum(entries, -limit), limit).astype(kind)


def noise_with(rng, dims, deviation, bound, shards, heavy, held_as=jnp.bfloat16):
    entries = deviation * jax.random.normal(rng, dims, jnp.float32)
    if shards:
        entries = entries * steps_of(rng, dims, shards, -0.22, 0.18)
    return jnp.clip(strengthened(entries, jax.random.fold_in(rng, 3), *heavy), -bound, bound).astype(held_as)


def setup_inputs(seed: int = 0, part: int = 0) -> dict:
    seeds = jax.random.split(jax.random.key(seed), 7)
    own_keys = jax.random.split(jax.random.fold_in(seeds[6], part), 7)
    inputs = normal_values(own_keys[0], (SEQ, D), 1.0, 6.0, ((1, 16),))
    out_grad = normal_values(own_keys[1], (SEQ, D), 0.25, 1.5, ((1, 16),))
    w_qkv = noise_with(seeds[2], (D, 3, HEADS * HD), D ** -0.5, 0.109375, ((2, 16),), (2, 0, 16, 2.0))
    w_out = normal_values(seeds[3], (HEADS * HD, D), (HEADS * HD) ** -0.5, 0.0625, ((0, 16),))
    saved_qkv = draw_saved_qkv(jax.random.fold_in(jax.random.fold_in(seeds[6], part), 71), part)
    positions = draw_positions(jax.random.fold_in(jax.random.fold_in(seeds[6], part), 71), part)
    return {"inputs": inputs, "out_grad": out_grad, "w_qkv": w_qkv, "w_out": w_out, "saved_qkv": saved_qkv, "positions": positions}


def reference(inputs, out_grad, w_qkv, w_out, saved_qkv, positions):
    seq_len = saved_qkv.shape[0]
    columns = saved_qkv.shape[2]
    heads_here = columns // HD
    factor = 1.0 / math.sqrt(HD)
    queries = saved_qkv[:, 0].reshape(seq_len, heads_here, HD).astype(jnp.float32)
    keys = saved_qkv[:, 1].reshape(seq_len, heads_here, HD).astype(jnp.float32)
    values = saved_qkv[:, 2].reshape(seq_len, heads_here, HD).astype(jnp.float32)
    scores = jnp.einsum('qhd,khd->hqk', queries, keys) * factor
    visible = positions[None, :] <= positions[:, None]
    scores = jnp.where(visible[None], scores, jnp.float32(-1e+30))
    highest = lax.optimization_barrier(jnp.max(scores, axis=-1, keepdims=True))
    expd = jnp.exp(scores - highest)
    attn = expd / lax.optimization_barrier(jnp.sum(expd, axis=-1, keepdims=True))
    attn_b = attn.astype(jnp.bfloat16)
    attended = jnp.einsum('hqk,khd->qhd', attn_b.astype(jnp.float32), values).astype(jnp.bfloat16)
    grad_out_h = jnp.dot(out_grad, w_out.T, preferred_element_type=jnp.float32).astype(jnp.bfloat16)
    grad_w_out = jnp.dot(attended.reshape(seq_len, columns).T, out_grad, preferred_element_type=jnp.float32).astype(jnp.bfloat16)
    grad_heads = grad_out_h.reshape(seq_len, heads_here, HD).astype(jnp.float32)
    grad_attn = jnp.einsum('qhd,khd->hqk', grad_heads, values)
    row_dot = lax.optimization_barrier(jnp.sum(grad_heads * attended.astype(jnp.float32), axis=-1)).T[:, :, None]
    grad_scores = (attn * (grad_attn - row_dot) * factor).astype(jnp.bfloat16).astype(jnp.float32)
    grad_q = jnp.einsum('hqk,khd->qhd', grad_scores, keys).astype(jnp.bfloat16)
    grad_k = jnp.einsum('hqk,qhd->khd', grad_scores, queries).astype(jnp.bfloat16)
    grad_v = jnp.einsum('hqk,qhd->khd', attn_b.astype(jnp.float32), grad_heads).astype(jnp.bfloat16)
    grad_qkv = jnp.stack([grad_q, grad_k, grad_v], axis=1).reshape(seq_len, 3 * columns)
    grad_w_qkv = jnp.dot(inputs.T, grad_qkv, preferred_element_type=jnp.float32).astype(jnp.bfloat16)
    grad_w_qkv = grad_w_qkv.reshape(inputs.shape[1], 3, columns)
    input_grad = jnp.dot(grad_qkv, w_qkv.reshape(inputs.shape[1], 3 * columns).T, preferred_element_type=jnp.float32).astype(jnp.bfloat16)
    return (input_grad, grad_w_qkv, grad_w_out)
```

```python
import functools
import math

import jax
import jax.numpy as jnp
from jax import lax
from jax.experimental import pallas as pl
from jax.experimental.pallas import tpu as pltpu
from jax.sharding import PartitionSpec as P

HD = 128
FACTOR = 1.0 / math.sqrt(HD)
MIB = 1 << 20
NT = (((1,), (1,)), ((), ()))
TN = (((0,), (0,)), ((), ()))


def dot(a, b, dims=(((1,), (0,)), ((), ()))):
    return lax.dot_general(a, b, dims, preferred_element_type=jnp.float32)


def params(mib):
    return pltpu.CompilerParams(vmem_limit_bytes=mib * MIB)


def cost(flops, nbytes, transcendentals=0):
    return pl.CostEstimate(flops=flops, bytes_accessed=nbytes, transcendentals=transcendentals)


def attend_kernel(col_ref, row_ref, qkv_ref, attn_ref, out_ref, out_t_ref):
    scores = dot(qkv_ref[0], qkv_ref[1], NT) * FACTOR
    scores = jnp.where(row_ref[...] <= col_ref[...], scores, -1e30)
    expd = jnp.exp(scores - jnp.max(scores, axis=1, keepdims=True))
    attn = (expd / jnp.sum(expd, axis=1, keepdims=True)).astype(jnp.bfloat16)
    attn_ref[0] = attn
    attended = dot(attn, qkv_ref[2])
    out_ref[...] = attended.astype(jnp.bfloat16)
    out_t_ref[...] = attended.T.astype(jnp.bfloat16)


def attend(positions, qkv):
    _, seq, columns = qkv.shape
    heads = columns // HD
    return pl.pallas_call(
        attend_kernel,
        grid=(heads,),
        in_specs=[
            pl.BlockSpec((seq, 1), lambda h: (0, 0)),
            pl.BlockSpec((1, seq), lambda h: (0, 0)),
            pl.BlockSpec((3, seq, HD), lambda h: (0, 0, h)),
        ],
        out_specs=[
            pl.BlockSpec((1, seq, seq), lambda h: (h, 0, 0)),
            pl.BlockSpec((seq, HD), lambda h: (0, h)),
            pl.BlockSpec((HD, seq), lambda h: (h, 0)),
        ],
        out_shape=[
            jax.ShapeDtypeStruct((heads, seq, seq), jnp.bfloat16),
            jax.ShapeDtypeStruct((seq, columns), jnp.bfloat16),
            jax.ShapeDtypeStruct((columns, seq), jnp.bfloat16),
        ],
        compiler_params=params(24),
        cost_estimate=cost(4 * seq * seq * columns, 5 * MIB, heads * seq * seq),
    )(positions[:, None], positions[None, :], qkv)


def attend_back_kernel(qkv_ref, attn_ref, attended_ref, grad_ref, out_ref):
    grad = grad_ref[...]
    attn = attn_ref[0]
    row_dot = jnp.sum(
        grad.astype(jnp.float32) * attended_ref[...].astype(jnp.float32), axis=1, keepdims=True
    )
    grad_attn = dot(grad, qkv_ref[2], NT)
    grad_scores = (attn.astype(jnp.float32) * (grad_attn - row_dot) * FACTOR).astype(jnp.bfloat16)
    out_ref[0] = dot(grad_scores, qkv_ref[1]).astype(jnp.bfloat16)
    out_ref[1] = dot(grad_scores, qkv_ref[0], TN).astype(jnp.bfloat16)
    out_ref[2] = dot(attn, grad, TN).astype(jnp.bfloat16)


def attend_back(qkv, attn, attended, grad):
    _, seq, columns = qkv.shape
    planes = pl.BlockSpec((3, seq, HD), lambda h: (0, 0, h))
    one = pl.BlockSpec((seq, HD), lambda h: (0, h))
    return pl.pallas_call(
        attend_back_kernel,
        grid=(columns // HD,),
        in_specs=[planes, pl.BlockSpec((1, seq, seq), lambda h: (h, 0, 0)), one, one],
        out_specs=planes,
        out_shape=jax.ShapeDtypeStruct(qkv.shape, jnp.bfloat16),
        compiler_params=params(24),
        cost_estimate=cost(8 * seq * seq * columns, 6 * MIB),
    )(qkv, attn, attended, grad)


def block_refs(refs):
    found = []
    for ref in refs:
        found += [ref] if len(ref.shape) == 2 else [ref.at[i] for i in range(ref.shape[0])]
    return found


def count_blocks(blocks):
    return sum(1 if b.ndim == 2 else b.shape[0] for b in blocks)


def features(index_ref, i, width):
    return pl.ds(pl.multiple_of(index_ref[i] * width, 128), width)


def grad_heads_kernel(index_ref, w_ref, *refs):
    *blocks, out_ref, total = refs
    for i, block in enumerate(block_refs(blocks)):
        width = block.shape[1]
        term = dot(block[...], w_ref[:, features(index_ref, i, width)], NT)
        if i == 0:
            total[...] = term
        else:
            total[...] += term
    out_ref[...] = total[...].astype(jnp.bfloat16)


def grad_heads(index, w_out, blocks):
    columns, width = w_out.shape
    seq = blocks[0].shape[-2]
    vmem = pl.BlockSpec(memory_space=pltpu.VMEM)
    return pl.pallas_call(
        grad_heads_kernel,
        in_specs=[pl.BlockSpec(memory_space=pltpu.SMEM)] + [vmem] * (1 + len(blocks)),
        out_specs=vmem,
        out_shape=jax.ShapeDtypeStruct((seq, columns), jnp.bfloat16),
        scratch_shapes=[pltpu.VMEM((seq, columns), jnp.float32)],
        compiler_params=params(32),
        cost_estimate=cost(2 * seq * columns * width, 13 * MIB),
    )(index, w_out, *blocks)


def weight_out_kernel(index_ref, left_ref, *refs):
    *blocks, out_ref, held, sems = refs
    copies = []
    for i, block in enumerate(block_refs(blocks)):
        width = block.shape[1]
        if i >= 2:
            copies[i - 2].wait()
        held[i % 2] = dot(left_ref[...], block[...]).astype(jnp.bfloat16)
        copy = pltpu.make_async_copy(
            held.at[i % 2], out_ref.at[:, features(index_ref, i, width)], sems.at[i % 2]
        )
        copy.start()
        copies.append(copy)
    for copy in copies[-2:]:
        copy.wait()


def weight_out(index, attended_t, blocks):
    columns, seq = attended_t.shape
    part = blocks[0].shape[-1]
    width = part * count_blocks(blocks)
    vmem = pl.BlockSpec(memory_space=pltpu.VMEM)
    return pl.pallas_call(
        weight_out_kernel,
        in_specs=[pl.BlockSpec(memory_space=pltpu.SMEM)] + [vmem] * (1 + len(blocks)),
        out_specs=pl.BlockSpec(memory_space=pl.ANY),
        out_shape=jax.ShapeDtypeStruct((columns, width), jnp.bfloat16),
        scratch_shapes=[pltpu.VMEM((2, columns, part), jnp.bfloat16), pltpu.SemaphoreType.DMA((2,))],
        compiler_params=params(24),
        cost_estimate=cost(2 * seq * columns * width, 13 * MIB),
    )(index, attended_t, *blocks)


def weight_qkv_kernel(index_ref, grad_ref, *refs):
    *blocks, out_ref, held, sems = refs
    copies = []
    for i, block in enumerate(block_refs(blocks)):
        width = block.shape[1]
        if i >= 2:
            copies[i - 2].wait()
        turned = block[...].T
        for slot in range(3):
            held[i % 2, slot] = dot(turned, grad_ref[slot]).astype(jnp.bfloat16)
        copy = pltpu.make_async_copy(
            held.at[i % 2], out_ref.at[:, features(index_ref, i, width)], sems.at[i % 2]
        )
        copy.start()
        copies.append(copy)
    for copy in copies[-2:]:
        copy.wait()


def weight_qkv(index, grad, blocks):
    _, seq, columns = grad.shape
    part = blocks[0].shape[-1]
    width = part * count_blocks(blocks)
    vmem = pl.BlockSpec(memory_space=pltpu.VMEM)
    return pl.pallas_call(
        weight_qkv_kernel,
        in_specs=[pl.BlockSpec(memory_space=pltpu.SMEM)] + [vmem] * (1 + len(blocks)),
        out_specs=pl.BlockSpec(memory_space=pl.ANY),
        out_shape=jax.ShapeDtypeStruct((3, width, columns), jnp.bfloat16),
        scratch_shapes=[
            pltpu.VMEM((2, 3, part, columns), jnp.bfloat16),
            pltpu.SemaphoreType.DMA((2,)),
        ],
        compiler_params=params(32),
        cost_estimate=cost(6 * seq * columns * width, 26 * MIB),
    )(index, grad, *blocks)


def terms_kernel(index_ref, grad_ref, w_ref, out_ref):
    total = dot(grad_ref[0], w_ref[0], NT)
    total += dot(grad_ref[1], w_ref[1], NT)
    total += dot(grad_ref[2], w_ref[2], NT)
    out_ref[0] = total.astype(jnp.bfloat16)


def terms(index, grad, w, part):
    _, seq, columns = grad.shape
    count = index.shape[0]
    return pl.pallas_call(
        terms_kernel,
        grid_spec=pltpu.PrefetchScalarGridSpec(
            num_scalar_prefetch=1,
            grid=(count,),
            in_specs=[
                pl.BlockSpec((3, seq, columns), lambda i, index: (0, 0, 0)),
                pl.BlockSpec((3, part, columns), lambda i, index: (0, index[i], 0)),
            ],
            out_specs=pl.BlockSpec((1, seq, part), lambda i, index: (i, 0, 0)),
        ),
        out_shape=jax.ShapeDtypeStruct((count, seq, part), jnp.bfloat16),
        compiler_params=params(24),
        cost_estimate=cost(6 * seq * columns * part * count, 2 * MIB * count),
    )(index, grad, w)


def plain(n, inputs, out_grad, w_qkv, w_out, saved_qkv, positions):
    full_in = lax.all_gather(inputs, "gx", axis=1, tiled=True)
    full_grad = lax.all_gather(out_grad, "gx", axis=1, tiled=True)
    qkv = saved_qkv.transpose(1, 0, 2)
    attn, attended, _ = attend(positions, qkv)
    grad_h = dot(full_grad, w_out, NT).astype(jnp.bfloat16)
    grad_w_out = dot(attended, full_grad, TN).astype(jnp.bfloat16)
    grad = attend_back(qkv, attn, attended, grad_h)
    grad_w_qkv = jnp.stack([dot(full_in, grad[k], TN).astype(jnp.bfloat16) for k in range(3)], 1)
    partial = sum(dot(grad[k], w_qkv[:, k], NT) for k in range(3))
    input_grad = lax.psum_scatter(partial, "gx", scatter_dimension=1, tiled=True)
    return input_grad.astype(jnp.bfloat16), grad_w_qkv, grad_w_out


def on_device(n, inputs, out_grad, w_qkv, w_out, saved_qkv, positions):
    part = inputs.shape[1]
    if part % 128:
        return plain(n, inputs, out_grad, w_qkv, w_out, saved_qkv, positions)
    same_core = [list(range(core, n, 2)) for core in range(2)]
    swap = [(i, i ^ 1) for i in range(n)]
    core = lax.axis_index("gx") % 2
    evens = jnp.arange(0, n, 2, dtype=jnp.int32)
    index = jnp.concatenate([evens + core, evens + 1 - core])

    def gathered(x):
        mine = lax.all_gather(x, "gx", axis=0, axis_index_groups=same_core)
        return mine, lax.ppermute(mine, "gx", swap)

    grad_blocks = gathered(out_grad)
    in_blocks = gathered(inputs)
    qkv = saved_qkv.transpose(1, 0, 2)
    w = w_qkv.transpose(1, 0, 2)
    attn, attended, attended_t = attend(positions, qkv)
    grad_h = grad_heads(index, w_out, grad_blocks)
    grad = attend_back(qkv, attn, attended, grad_h)
    theirs = terms(index[n // 2 :], grad, w, part)
    mine = terms(index[: n // 2], grad, w, part)
    both = mine + lax.ppermute(theirs, "gx", swap)
    input_grad = lax.psum_scatter(
        both, "gx", scatter_dimension=0, axis_index_groups=same_core, tiled=False
    )
    grad_w_qkv = weight_qkv(index, grad, in_blocks).transpose(1, 0, 2)
    grad_w_out = weight_out(index, attended_t, grad_blocks)
    return input_grad.astype(jnp.bfloat16), grad_w_qkv, grad_w_out


def solution(mesh):
    placed = (
        P("runs", "gx"),
        P("runs", "gx"),
        P(None, None, "gx"),
        P("gx", None),
        P("runs", None, "gx"),
        P("runs"),
    )
    return jax.shard_map(
        functools.partial(on_device, mesh.shape["gx"]),
        mesh=mesh,
        in_specs=placed,
        out_specs=(P("runs", "gx"), P("runs", None, "gx"), P(("runs", "gx"), None)),
        check_vma=False,
    )
```

```python
import functools
import math

import jax
import jax.numpy as jnp
from jax import lax
from jax.experimental import pallas as pl
from jax.experimental.pallas import tpu as pltpu
from jax.sharding import PartitionSpec as P

HD = 128
FACTOR = 1.0 / math.sqrt(HD)
MIB = 1 << 20
NT = (((1,), (1,)), ((), ()))
TN = (((0,), (0,)), ((), ()))


def dot(a, b, dims=(((1,), (0,)), ((), ()))):
    return lax.dot_general(a, b, dims, preferred_element_type=jnp.float32)


def params(mib):
    return pltpu.CompilerParams(vmem_limit_bytes=mib * MIB)


def cost(flops, nbytes, transcendentals=0):
    return pl.CostEstimate(flops=flops, bytes_accessed=nbytes, transcendentals=transcendentals)


def attend_kernel(col_ref, row_ref, qkv_ref, attn_ref, out_ref, out_t_ref):
    scores = dot(qkv_ref[0], qkv_ref[1], NT) * FACTOR
    scores = jnp.where(row_ref[...] <= col_ref[...], scores, -1e30)
    expd = jnp.exp(scores - jnp.max(scores, axis=1, keepdims=True))
    attn = (expd / jnp.sum(expd, axis=1, keepdims=True)).astype(jnp.bfloat16)
    attn_ref[0] = attn
    attended = dot(attn, qkv_ref[2])
    out_ref[...] = attended.astype(jnp.bfloat16)
    out_t_ref[...] = attended.T.astype(jnp.bfloat16)


def attend(positions, qkv):
    _, seq, columns = qkv.shape
    heads = columns // HD
    return pl.pallas_call(
        attend_kernel,
        grid=(heads,),
        in_specs=[
            pl.BlockSpec((seq, 1), lambda h: (0, 0)),
            pl.BlockSpec((1, seq), lambda h: (0, 0)),
            pl.BlockSpec((3, seq, HD), lambda h: (0, 0, h)),
        ],
        out_specs=[
            pl.BlockSpec((1, seq, seq), lambda h: (h, 0, 0)),
            pl.BlockSpec((seq, HD), lambda h: (0, h)),
            pl.BlockSpec((HD, seq), lambda h: (h, 0)),
        ],
        out_shape=[
            jax.ShapeDtypeStruct((heads, seq, seq), jnp.bfloat16),
            jax.ShapeDtypeStruct((seq, columns), jnp.bfloat16),
            jax.ShapeDtypeStruct((columns, seq), jnp.bfloat16),
        ],
        compiler_params=params(24),
        cost_estimate=cost(4 * seq * seq * columns, 5 * MIB, heads * seq * seq),
    )(positions[:, None], positions[None, :], qkv)


def attend_back_kernel(qkv_ref, attn_ref, attended_ref, grad_ref, out_ref):
    grad = grad_ref[...]
    attn = attn_ref[0]
    row_dot = jnp.sum(
        grad.astype(jnp.float32) * attended_ref[...].astype(jnp.float32), axis=1, keepdims=True
    )
    grad_attn = dot(grad, qkv_ref[2], NT)
    grad_scores = (attn.astype(jnp.float32) * (grad_attn - row_dot) * FACTOR).astype(jnp.bfloat16)
    out_ref[0] = dot(grad_scores, qkv_ref[1]).astype(jnp.bfloat16)
    out_ref[1] = dot(grad_scores, qkv_ref[0], TN).astype(jnp.bfloat16)
    out_ref[2] = dot(attn, grad, TN).astype(jnp.bfloat16)


def attend_back(qkv, attn, attended, grad):
    _, seq, columns = qkv.shape
    planes = pl.BlockSpec((3, seq, HD), lambda h: (0, 0, h))
    one = pl.BlockSpec((seq, HD), lambda h: (0, h))
    return pl.pallas_call(
        attend_back_kernel,
        grid=(columns // HD,),
        in_specs=[planes, pl.BlockSpec((1, seq, seq), lambda h: (h, 0, 0)), one, one],
        out_specs=planes,
        out_shape=jax.ShapeDtypeStruct(qkv.shape, jnp.bfloat16),
        compiler_params=params(24),
        cost_estimate=cost(8 * seq * seq * columns, 6 * MIB),
    )(qkv, attn, attended, grad)


def features(index_ref, i, width):
    return pl.ds(pl.multiple_of(index_ref[i] * width, 128), width)


def grad_heads_kernel(count, first, last, index_ref, *refs):
    blocks, weights, rest = refs[:count], refs[count : 2 * count], refs[2 * count :]
    total = None if first else rest[0][...]
    for block, weight in zip(blocks, weights):
        term = dot(block[...], weight[...], NT)
        total = term if total is None else total + term
    rest[-1][...] = total.astype(jnp.bfloat16) if last else total


def grad_heads(index, w_out, blocks, total=None, last=False):
    columns = w_out.shape[0]
    seq, part = blocks[0].shape
    count = len(blocks)

    def weight(i):
        return pl.BlockSpec((columns, part), lambda step, index: (0, index[i]))

    block = pl.BlockSpec((seq, part), lambda step, index: (0, 0))
    whole = pl.BlockSpec((seq, columns), lambda step, index: (0, 0))
    first = total is None
    return pl.pallas_call(
        functools.partial(grad_heads_kernel, count, first, last),
        grid_spec=pltpu.PrefetchScalarGridSpec(
            num_scalar_prefetch=1,
            grid=(1,),
            in_specs=[block] * count + [weight(i) for i in range(count)] + [whole] * (not first),
            out_specs=whole,
        ),
        out_shape=jax.ShapeDtypeStruct((seq, columns), jnp.bfloat16 if last else jnp.float32),
        compiler_params=params(40),
        cost_estimate=cost(2 * seq * columns * part * count, MIB * count),
    )(index, *blocks, *[w_out] * count, *([] if first else [total]))


SLOTS = 4


def weight_kernel(count, turn, index_ref, left_ref, *refs):
    blocks, (out_ref, held, sems) = refs[:count], refs[-3:]
    copies = []
    for i, block in enumerate(blocks):
        width = block.shape[1]
        slot = i % SLOTS
        if i >= SLOTS:
            copies[i - SLOTS].wait()
        if turn:
            turned = block[...].T
            for k in range(3):
                held[slot, k] = dot(turned, left_ref[k]).astype(jnp.bfloat16)
        else:
            held[slot] = dot(left_ref[...], block[...]).astype(jnp.bfloat16)
        copy = pltpu.make_async_copy(
            held.at[slot], out_ref.at[:, features(index_ref, i, width)], sems.at[slot]
        )
        copy.start()
        copies.append(copy)
    for copy in copies[-SLOTS:]:
        copy.wait()


def weight_grad(index, left, blocks, shape, into=None):
    turn = left.ndim == 3
    seq, part = blocks[0].shape
    count = len(blocks)
    held = (3, part, left.shape[2]) if turn else (left.shape[0], part)
    vmem = pl.BlockSpec(memory_space=pltpu.VMEM)
    rest = pl.BlockSpec(memory_space=pl.ANY)
    size = math.prod(held)
    return pl.pallas_call(
        functools.partial(weight_kernel, count, turn),
        in_specs=[pl.BlockSpec(memory_space=pltpu.SMEM)]
        + [vmem] * (1 + count)
        + [rest] * (into is not None),
        out_specs=rest,
        out_shape=jax.ShapeDtypeStruct(shape, jnp.bfloat16),
        scratch_shapes=[
            pltpu.VMEM((SLOTS, *held), jnp.bfloat16),
            pltpu.SemaphoreType.DMA((SLOTS,)),
        ],
        input_output_aliases={} if into is None else {2 + count: 0},
        compiler_params=params(40),
        cost_estimate=cost(2 * seq * size * count, 3 * size * count),
    )(index, left, *blocks, *([] if into is None else [into]))


def terms_kernel(index_ref, core_ref, grad_ref, w_ref, theirs_ref, mine_ref):
    total = dot(grad_ref[0], w_ref[0], NT)
    total += dot(grad_ref[1], w_ref[1], NT)
    total += dot(grad_ref[2], w_ref[2], NT)
    total = total.astype(jnp.bfloat16)
    part = total.shape[1] // 2

    @pl.when(core_ref[0] == 0)
    def _():
        mine_ref[0] = total[:, :part]
        theirs_ref[0] = total[:, part:]

    @pl.when(core_ref[0] == 1)
    def _():
        mine_ref[0] = total[:, part:]
        theirs_ref[0] = total[:, :part]


def terms(chips, core, grad, w, part):
    _, seq, columns = grad.shape
    count = chips.shape[0]
    out = pl.BlockSpec((1, seq, part), lambda i, chips, core: (i, 0, 0))
    shape = jax.ShapeDtypeStruct((count, seq, part), jnp.bfloat16)
    return pl.pallas_call(
        terms_kernel,
        grid_spec=pltpu.PrefetchScalarGridSpec(
            num_scalar_prefetch=2,
            grid=(count,),
            in_specs=[
                pl.BlockSpec((3, seq, columns), lambda i, chips, core: (0, 0, 0)),
                pl.BlockSpec((3, 2 * part, columns), lambda i, chips, core: (0, chips[i], 0)),
            ],
            out_specs=[out, out],
        ),
        out_shape=[shape, shape],
        compiler_params=params(48),
        cost_estimate=cost(12 * seq * columns * part * count, 5 * MIB * count),
    )(chips, core, grad, w)


def plain(n, inputs, out_grad, w_qkv, w_out, saved_qkv, positions):
    full_in = lax.all_gather(inputs, "gx", axis=1, tiled=True)
    full_grad = lax.all_gather(out_grad, "gx", axis=1, tiled=True)
    qkv = saved_qkv.transpose(1, 0, 2)
    attn, attended, _ = attend(positions, qkv)
    grad_h = dot(full_grad, w_out, NT).astype(jnp.bfloat16)
    grad_w_out = dot(attended, full_grad, TN).astype(jnp.bfloat16)
    grad = attend_back(qkv, attn, attended, grad_h)
    grad_w_qkv = jnp.stack([dot(full_in, grad[k], TN).astype(jnp.bfloat16) for k in range(3)], 1)
    partial = sum(dot(grad[k], w_qkv[:, k], NT) for k in range(3))
    input_grad = lax.psum_scatter(partial, "gx", scatter_dimension=1, tiled=True)
    return input_grad.astype(jnp.bfloat16), grad_w_qkv, grad_w_out


def ring_order(chips):
    if chips == 8:
        return [0, 2, 4, 6, 7, 5, 3, 1]
    return list(range(chips))


def on_device(n, inputs, out_grad, w_qkv, w_out, saved_qkv, positions):
    seq, part = inputs.shape
    if part % 128 or n != 16:
        return plain(n, inputs, out_grad, w_qkv, w_out, saved_qkv, positions)
    chips, half = n // 2, seq // 2
    far = chips // 2
    order = ring_order(chips)
    after = {order[i]: order[(i + 1) % chips] for i in range(chips)}
    ahead = [(2 * c + k, 2 * after[c] + k) for c in order for k in range(2)]
    back = [(j, i) for i, j in ahead]
    swap = [(i, i ^ 1) for i in range(n)]
    here = [[order[(order.index(i // 2) + k) % chips] for k in range(chips)] for i in range(n)]

    me = lax.axis_index("gx")
    core = me % 2
    chip_at = lax.dynamic_slice(jnp.array(here, jnp.int32), (me, 0), (1, chips))[0]
    core_ref = core.astype(jnp.int32)[None]

    def send(x, perm):
        return lax.ppermute(x, "gx", perm)

    def index_of(offsets):
        at = jnp.stack([chip_at[k % chips] for k in offsets])
        return jnp.concatenate([2 * at + core, 2 * at + 1 - core]).astype(jnp.int32)

    def gathered(x):
        parts = [((0,), [x, send(x, swap)])]
        right = left = x
        for step in range(1, far):
            right, left = send(right, ahead), send(left, back)
            parts.append(((-step, step), [right, left, send(right, swap), send(left, swap)]))
        last = jnp.concatenate([send(right[:half], ahead), send(left[half:], back)])
        parts.append(((far,), [last, send(last, swap)]))
        return parts

    qkv = saved_qkv.transpose(1, 0, 2)
    w = w_qkv.transpose(1, 0, 2)
    grad_parts = gathered(out_grad)
    inputs, _ = lax.optimization_barrier((inputs, grad_parts[far - 1][1][:2]))
    in_parts = gathered(inputs)

    attn, attended, attended_t = attend(positions, qkv)

    def joined(parts):
        offsets = [k for ks, _ in parts for k in ks]
        own = [b for ks, bs in parts for b in bs[: len(ks)]]
        other = [b for ks, bs in parts for b in bs[len(ks) :]]
        return index_of(offsets), own + other

    grad_h = None
    for some in (grad_parts[:2], grad_parts[2:3], grad_parts[3:4], grad_parts[4:]):
        index, blocks = joined(some)
        grad_h = grad_heads(index, w_out, blocks, grad_h, some[-1][0] == (far,))
    grad = attend_back(qkv, attn, attended, grad_h)

    def summed(offsets):
        at = jnp.stack([chip_at[k % chips] for k in offsets]).astype(jnp.int32)
        theirs, mine = terms(at, core_ref, grad, w, part)
        return mine.astype(jnp.float32) + send(theirs, swap).astype(jnp.float32)

    low = summed((far,))[0].astype(jnp.bfloat16)
    right, left = send(low[:half], ahead), send(low[half:], back)
    for step in range(far - 1, 0, -1):
        total = summed((step, -step))
        if step == far - 1:
            right = jnp.pad(right, ((0, half), (0, 0)))
            left = jnp.pad(left, ((half, 0), (0, 0)))
        right = send((total[0] + right.astype(jnp.float32)).astype(jnp.bfloat16), ahead)
        left = send((total[1] + left.astype(jnp.float32)).astype(jnp.bfloat16), back)
    input_grad = summed((0,))[0] + right.astype(jnp.float32) + left.astype(jnp.float32)

    def weight_of(left_side, parts, shape):
        result = None
        for some in (parts[:2], parts[2:3], parts[3:4], parts[4:]):
            index, blocks = joined(some)
            result = weight_grad(index, left_side, blocks, shape, result)
        return result

    grad_w_out = weight_of(attended_t, grad_parts, w_out.shape)
    grad_w_qkv = weight_of(grad, in_parts, w.shape).transpose(1, 0, 2)
    return input_grad.astype(jnp.bfloat16), grad_w_qkv, grad_w_out


def solution(mesh):
    placed = (
        P("runs", "gx"),
        P("runs", "gx"),
        P(None, None, "gx"),
        P("gx", None),
        P("runs", None, "gx"),
        P("runs"),
    )
    return jax.shard_map(
        functools.partial(on_device, mesh.shape["gx"]),
        mesh=mesh,
        in_specs=placed,
        out_specs=(P("runs", "gx"), P("runs", None, "gx"), P(("runs", "gx"), None)),
        check_vma=False,
    )
```

```python
import functools
import math

import jax
import jax.numpy as jnp
from jax import lax
from jax.experimental import pallas as pl
from jax.experimental.pallas import tpu as pltpu
from jax.sharding import PartitionSpec as P

HD = 128
FACTOR = 1.0 / math.sqrt(HD)
MIB = 1 << 20
NT = (((1,), (1,)), ((), ()))
TN = (((0,), (0,)), ((), ()))


def dot(a, b, dims=(((1,), (0,)), ((), ()))):
    return lax.dot_general(a, b, dims, preferred_element_type=jnp.float32)


def params(mib):
    return pltpu.CompilerParams(vmem_limit_bytes=mib * MIB)


def cost(flops, nbytes, transcendentals=0):
    flops, nbytes = flops // 4096, nbytes // 4096
    return pl.CostEstimate(flops=flops, bytes_accessed=nbytes, transcendentals=transcendentals)


def attend_kernel(col_ref, row_ref, qkv_ref, attn_ref, out_ref, out_t_ref):
    scores = dot(qkv_ref[0], qkv_ref[1], NT) * FACTOR
    scores = jnp.where(row_ref[...] <= col_ref[...], scores, -1e30)
    expd = jnp.exp(scores - jnp.max(scores, axis=1, keepdims=True))
    attn = (expd / jnp.sum(expd, axis=1, keepdims=True)).astype(jnp.bfloat16)
    attn_ref[0] = attn
    attended = dot(attn, qkv_ref[2])
    out_ref[...] = attended.astype(jnp.bfloat16)
    out_t_ref[...] = attended.T.astype(jnp.bfloat16)


def attend(positions, qkv):
    _, seq, columns = qkv.shape
    heads = columns // HD
    return pl.pallas_call(
        attend_kernel,
        grid=(heads,),
        in_specs=[
            pl.BlockSpec((seq, 1), lambda h: (0, 0)),
            pl.BlockSpec((1, seq), lambda h: (0, 0)),
            pl.BlockSpec((3, seq, HD), lambda h: (0, 0, h)),
        ],
        out_specs=[
            pl.BlockSpec((1, seq, seq), lambda h: (h, 0, 0)),
            pl.BlockSpec((seq, HD), lambda h: (0, h)),
            pl.BlockSpec((HD, seq), lambda h: (h, 0)),
        ],
        out_shape=[
            jax.ShapeDtypeStruct((heads, seq, seq), jnp.bfloat16),
            jax.ShapeDtypeStruct((seq, columns), jnp.bfloat16),
            jax.ShapeDtypeStruct((columns, seq), jnp.bfloat16),
        ],
        compiler_params=params(24),
        cost_estimate=cost(4 * seq * seq * columns, 5 * MIB, heads * seq * seq),
    )(positions[:, None], positions[None, :], qkv)


def attend_back_kernel(qkv_ref, attn_ref, attended_ref, grad_ref, out_ref):
    grad = grad_ref[...]
    attn = attn_ref[0]
    row_dot = jnp.sum(
        grad.astype(jnp.float32) * attended_ref[...].astype(jnp.float32), axis=1, keepdims=True
    )
    grad_attn = dot(grad, qkv_ref[2], NT)
    grad_scores = (attn.astype(jnp.float32) * (grad_attn - row_dot) * FACTOR).astype(jnp.bfloat16)
    out_ref[0] = dot(grad_scores, qkv_ref[1]).astype(jnp.bfloat16)
    out_ref[1] = dot(grad_scores, qkv_ref[0], TN).astype(jnp.bfloat16)
    out_ref[2] = dot(attn, grad, TN).astype(jnp.bfloat16)


def attend_back(qkv, attn, attended, grad):
    _, seq, columns = qkv.shape
    planes = pl.BlockSpec((3, seq, HD), lambda h: (0, 0, h))
    one = pl.BlockSpec((seq, HD), lambda h: (0, h))
    return pl.pallas_call(
        attend_back_kernel,
        grid=(columns // HD,),
        in_specs=[planes, pl.BlockSpec((1, seq, seq), lambda h: (h, 0, 0)), one, one],
        out_specs=planes,
        out_shape=jax.ShapeDtypeStruct(qkv.shape, jnp.bfloat16),
        compiler_params=params(24),
        cost_estimate=cost(8 * seq * seq * columns, 6 * MIB),
    )(qkv, attn, attended, grad)


def grad_heads_kernel(count, first, last, plan_ref, *refs):
    blocks, weights, rest = refs[:count], refs[count : 2 * count], refs[2 * count :]
    out_ref, total = rest[-2:]
    for i, (block, weight) in enumerate(zip(blocks, weights)):
        term = dot(block[...], weight[...], NT)
        if i:
            total[...] += term
        else:
            total[...] = term if first else rest[0][...] + term
    out_ref[...] = total[...].astype(jnp.bfloat16) if last else total[...]


def grad_heads(plan, w_out, blocks, total=None, last=False):
    columns = w_out.shape[0]
    seq, part = blocks[0][1].shape
    count = len(blocks)

    def weight(place):
        return pl.BlockSpec((columns, part), lambda step, plan: (0, plan[place]))

    def whole(shape):
        return pl.BlockSpec(shape, lambda step, plan: (0, 0))

    first = total is None
    return pl.pallas_call(
        functools.partial(grad_heads_kernel, count, first, last),
        grid_spec=pltpu.PrefetchScalarGridSpec(
            num_scalar_prefetch=1,
            grid=(1,),
            in_specs=[whole((seq, part))] * count
            + [weight(place) for place, _ in blocks]
            + [whole((seq, columns))] * (not first),
            out_specs=whole((seq, columns)),
            scratch_shapes=[pltpu.VMEM((seq, columns), jnp.float32)],
        ),
        out_shape=jax.ShapeDtypeStruct((seq, columns), jnp.bfloat16 if last else jnp.float32),
        compiler_params=params(40),
        cost_estimate=cost(2 * seq * columns * part * count, MIB * count),
    )(plan, *[block for _, block in blocks], *[w_out] * count, *([] if first else [total]))


SLOTS = 4


def weight_kernel(places, turn, plan_ref, left_ref, *refs):
    out_ref, held, sems = refs[-3:]
    copies = []
    for i, (place, block) in enumerate(zip(places, refs)):
        width = block.shape[1]
        slot = i % SLOTS
        if i >= SLOTS:
            copies[i - SLOTS].wait()
        if turn:
            turned = block[...].T
            for k in range(3):
                held[slot, k] = dot(turned, left_ref[k]).astype(jnp.bfloat16)
        else:
            held[slot] = dot(left_ref[...], block[...]).astype(jnp.bfloat16)
        start = pl.multiple_of(plan_ref[place] * width, 128)
        copy = pltpu.make_async_copy(
            held.at[slot], out_ref.at[:, pl.ds(start, width)], sems.at[slot]
        )
        copy.start()
        copies.append(copy)
    for copy in copies[-SLOTS:]:
        copy.wait()


def weight_grad(plan, left, blocks, shape, into=None):
    turn = left.ndim == 3
    seq, part = blocks[0][1].shape
    count = len(blocks)
    held = (3, part, left.shape[2]) if turn else (left.shape[0], part)
    vmem = pl.BlockSpec(memory_space=pltpu.VMEM)
    rest = pl.BlockSpec(memory_space=pl.ANY)
    size = math.prod(held) * count
    return pl.pallas_call(
        functools.partial(weight_kernel, [place for place, _ in blocks], turn),
        in_specs=[pl.BlockSpec(memory_space=pltpu.SMEM)]
        + [vmem] * (1 + count)
        + [rest] * (into is not None),
        out_specs=rest,
        out_shape=jax.ShapeDtypeStruct(shape, jnp.bfloat16),
        scratch_shapes=[
            pltpu.VMEM((SLOTS, *held), jnp.bfloat16),
            pltpu.SemaphoreType.DMA((SLOTS,)),
        ],
        input_output_aliases={} if into is None else {2 + count: 0},
        compiler_params=params(40),
        cost_estimate=cost(2 * seq * size, 3 * size),
    )(plan, left, *[block for _, block in blocks], *([] if into is None else [into]))


def terms_kernel(plan_ref, grad_ref, w_ref, *out_refs):
    total = dot(grad_ref[0], w_ref[0], NT)
    total += dot(grad_ref[1], w_ref[1], NT)
    total += dot(grad_ref[2], w_ref[2], NT)
    total = total.astype(jnp.bfloat16)
    part = total.shape[1] // 2
    step = pl.program_id(0)
    for i, out_ref in enumerate(out_refs):
        core = plan_ref[0] if i == len(out_refs) - 1 else 1 - plan_ref[0]

        @pl.when((step == i) & (core == 0))
        def _():
            out_ref[0] = total[:, part:]
            out_ref[1] = total[:, :part]

        @pl.when((step == i) & (core == 1))
        def _():
            out_ref[0] = total[:, :part]
            out_ref[1] = total[:, part:]


def terms(plan, place, count, grad, w, part):
    _, seq, columns = grad.shape
    out = pl.BlockSpec((2, seq, part), lambda i, plan: (0, 0, 0))
    shape = jax.ShapeDtypeStruct((2, seq, part), jnp.bfloat16)
    return pl.pallas_call(
        terms_kernel,
        grid_spec=pltpu.PrefetchScalarGridSpec(
            num_scalar_prefetch=1,
            grid=(count,),
            in_specs=[
                pl.BlockSpec((3, seq, columns), lambda i, plan: (0, 0, 0)),
                pl.BlockSpec((3, 2 * part, columns), lambda i, plan: (0, plan[place + i], 0)),
            ],
            out_specs=[out] * count,
        ),
        out_shape=[shape] * count,
        compiler_params=params(48),
        cost_estimate=cost(12 * seq * columns * part * count, 5 * MIB * count),
    )(plan, grad, w)


def plain(n, inputs, out_grad, w_qkv, w_out, saved_qkv, positions):
    full_in = lax.all_gather(inputs, "gx", axis=1, tiled=True)
    full_grad = lax.all_gather(out_grad, "gx", axis=1, tiled=True)
    qkv = saved_qkv.transpose(1, 0, 2)
    attn, attended, _ = attend(positions, qkv)
    grad_h = dot(full_grad, w_out, NT).astype(jnp.bfloat16)
    grad_w_out = dot(attended, full_grad, TN).astype(jnp.bfloat16)
    grad = attend_back(qkv, attn, attended, grad_h)
    grad_w_qkv = jnp.stack([dot(full_in, grad[k], TN).astype(jnp.bfloat16) for k in range(3)], 1)
    partial = sum(dot(grad[k], w_qkv[:, k], NT) for k in range(3))
    input_grad = lax.psum_scatter(partial, "gx", scatter_dimension=1, tiled=True)
    return input_grad.astype(jnp.bfloat16), grad_w_qkv, grad_w_out


def ring_order(chips):
    if chips == 8:
        return [0, 2, 4, 6, 7, 5, 3, 1]
    return list(range(chips))


def plan_of(order, device):
    chips = len(order)
    at = order.index(device // 2)
    core = device % 2

    def chip(offset):
        return order[(at + offset) % chips]

    blocks = [2 * chip(0) + core, 2 * chip(0) + 1 - core]
    for step in range(1, chips // 2):
        behind, ahead = (-step, step) if core == 0 else (step, -step)
        blocks += [2 * chip(behind) + core, 2 * chip(behind) + 1 - core]
        blocks += [2 * chip(ahead) + 1 - core, 2 * chip(ahead) + core]
    blocks += [2 * chip(chips // 2) + core, 2 * chip(chips // 2) + 1 - core]
    summed = [chip(chips // 2)]
    for step in range(chips // 2 - 1, 0, -1):
        ahead = step if core == 0 else -step
        summed += [chip(-ahead), chip(ahead)]
    return [core] + blocks + summed + [chip(0)]


def after(x, *others):
    return lax.optimization_barrier((x, *others))[0]


def together(*arrays):
    return lax.optimization_barrier(arrays)


def f32(x):
    return x.astype(jnp.float32)


def on_device(n, inputs, out_grad, w_qkv, w_out, saved_qkv, positions):
    part = inputs.shape[1]
    if part % 128 or n != 16:
        return plain(n, inputs, out_grad, w_qkv, w_out, saved_qkv, positions)
    order = ring_order(n // 2)
    chips = range(n // 2)
    ring = [(2 * order[i], 2 * order[i - 1]) for i in chips]
    ring = [(j, i) for i, j in ring] + [(i + 1, j + 1) for i, j in ring]
    swap = [(i, i ^ 1) for i in range(n)]
    plans = [plan_of(order, i) for i in range(n)]
    size = len(plans[0])
    plan = lax.dynamic_slice(
        jnp.array(sum(plans, []), jnp.int32), (lax.axis_index("gx") * size,), (size,)
    )

    def send(x):
        return lax.ppermute(x, "gx", ring)

    def swapped(x):
        return lax.ppermute(x, "gx", swap)

    def blocks(step, *arrays):
        first = 1 if step == 0 else 4 * step - 1
        return [(first + i, array) for i, array in enumerate(arrays)]

    def grad_out(index, some, into=None):
        return weight_grad(index, attended_t, some, w_out.shape, into)

    def grad_qkv(index, some, into=None):
        return weight_grad(index, grad, some, w.shape, into)

    qkv = saved_qkv.transpose(1, 0, 2)
    w = w_qkv.transpose(1, 0, 2)

    a1 = send(out_grad)
    other = swapped(out_grad)
    b1 = send(other)
    attn, attended, attended_t = attend(positions, qkv)

    a1 = after(a1, attended)
    a2, a1x = send(a1), swapped(a1)
    g0 = blocks(0, out_grad, other)
    grad_h = grad_heads(after(plan, a1), w_out, g0)

    b1 = after(b1, grad_h)
    b2, b1x = send(b1), swapped(b1)
    out = grad_out(after(plan, b1), g0)

    a2 = after(a2, out)
    a3, a2x = send(a2), swapped(a2)
    g1 = blocks(1, a1, b1, a1x, b1x)
    grad_h = grad_heads(after(plan, a2), w_out, g1, grad_h)

    b2 = after(b2, grad_h)
    b3, b2x = send(b2), swapped(b2)
    out = grad_out(after(plan, b2), g1, out)

    a3 = after(a3, out)
    a4, a3x = send(a3), swapped(a3)
    g2 = blocks(2, a2, b2, a2x, b2x)
    grad_h = grad_heads(after(plan, a3), w_out, g2, grad_h)

    b3 = after(b3, grad_h)
    b3x = swapped(b3)
    inputs = after(inputs, b3)
    other = swapped(inputs)
    i1 = send(inputs)
    out = grad_out(after(plan, b3), g2, out)

    out, other, a3x, b3x, plan = together(out, other, a3x, b3x, plan)
    j1 = send(other)
    f0 = blocks(0, inputs, other)
    g3 = blocks(3, a3, b3, a3x, b3x)
    grad_h = grad_heads(plan, w_out, g3, grad_h)

    grad_h, a4, plan = together(grad_h, a4, plan)
    a4x = swapped(a4)
    out = grad_out(plan, g3, out)

    out, a4x, i1, plan = together(out, a4x, i1, plan)
    i2, i1x = send(i1), swapped(i1)
    g4 = blocks(4, a4, a4x)
    grad_h = grad_heads(plan, w_out, g4, grad_h, last=True)
    grad = attend_back(qkv, attn, attended, grad_h)

    grad, j1, plan = together(grad, j1, plan)
    j2, j1x = send(j1), swapped(j1)
    (t4,) = terms(plan, 17, 1, grad, w, part)

    t4, i2, plan = together(t4, i2, plan)
    theirs = swapped(t4[0])
    i3, i2x = send(i2), swapped(i2)
    out = grad_out(plan, g4, out)

    out, theirs, j2, plan = together(out, theirs, j2, plan)
    m4 = send((f32(t4[1]) + f32(theirs)).astype(jnp.bfloat16))
    j3, j2x = send(j2), swapped(j2)
    theirs, t3 = terms(plan, 18, 2, grad, w, part)

    theirs, t3, m4, i3, plan = together(theirs, t3, m4, i3, plan)
    theirs = swapped(theirs)
    i4, i3x = send(i3), swapped(i3)
    weight = grad_qkv(plan, f0)

    weight, theirs, j3, plan = together(weight, theirs, j3, plan)
    o3 = send((f32(t3[0]) + f32(theirs[0])).astype(jnp.bfloat16))
    theirs2, t2 = terms(plan, 20, 2, grad, w, part)

    theirs2, t2, o3, i4, plan = together(theirs2, t2, o3, i4, plan)
    m3 = send((f32(t3[1]) + f32(theirs[1]) + f32(m4)).astype(jnp.bfloat16))
    theirs = swapped(theirs2)
    j3x = swapped(j3)
    i4x = swapped(i4)
    weight = grad_qkv(plan, blocks(1, i1, j1, i1x, j1x), weight)

    weight, theirs, m3, plan = together(weight, theirs, m3, plan)
    o2 = send((f32(t2[0]) + f32(theirs[0]) + f32(o3)).astype(jnp.bfloat16))
    theirs1, t1 = terms(plan, 22, 2, grad, w, part)

    theirs1, t1, o2, plan = together(theirs1, t1, o2, plan)
    m2 = send((f32(t2[1]) + f32(theirs[1]) + f32(m3)).astype(jnp.bfloat16))
    theirs = swapped(theirs1)
    weight = grad_qkv(plan, blocks(2, i2, j2, i2x, j2x), weight)

    weight, theirs, m2, plan = together(weight, theirs, m2, plan)
    o1 = send((f32(t1[0]) + f32(theirs[0]) + f32(o2)).astype(jnp.bfloat16))
    (t0,) = terms(plan, 24, 1, grad, w, part)
    weight = grad_qkv(plan, blocks(4, i4, i4x), weight)

    weight, t0, o1, plan = together(weight, t0, o1, plan)
    m1 = send((f32(t1[1]) + f32(theirs[1]) + f32(m2)).astype(jnp.bfloat16))
    theirs = swapped((f32(t0[0]) + f32(o1)).astype(jnp.bfloat16))
    weight = grad_qkv(plan, blocks(3, i3, j3, i3x, j3x), weight)

    weight, theirs, m1 = together(weight, theirs, m1)
    input_grad = f32(t0[1]) + f32(m1) + f32(theirs)
    return input_grad.astype(jnp.bfloat16), weight.transpose(1, 0, 2), out


def solution(mesh):
    placed = (
        P("runs", "gx"),
        P("runs", "gx"),
        P(None, None, "gx"),
        P("gx", None),
        P("runs", None, "gx"),
        P("runs"),
    )
    return jax.shard_map(
        functools.partial(on_device, mesh.shape["gx"]),
        mesh=mesh,
        in_specs=placed,
        out_specs=(P("runs", "gx"), P("runs", None, "gx"), P(("runs", "gx"), None)),
        check_vma=False,
    )
```

```python
import functools
import math

import jax
import jax.numpy as jnp
from jax import lax
from jax.experimental import pallas as pl
from jax.experimental.pallas import tpu as pltpu
from jax.sharding import PartitionSpec as P

HD = 128
FACTOR = 1.0 / math.sqrt(HD)
MIB = 1 << 20
NT = (((1,), (1,)), ((), ()))
TN = (((0,), (0,)), ((), ()))


def dot(a, b, dims=(((1,), (0,)), ((), ()))):
    return lax.dot_general(a, b, dims, preferred_element_type=jnp.float32)


def params(mib):
    return pltpu.CompilerParams(vmem_limit_bytes=mib * MIB)


def cost(flops, nbytes, transcendentals=0):
    flops, nbytes = flops // 4096, nbytes // 4096
    return pl.CostEstimate(flops=flops, bytes_accessed=nbytes, transcendentals=transcendentals)


def attend_kernel(row_ref, qkv_ref, attn_ref, out_ref, out_t_ref):
    row = row_ref[...]
    column = jnp.broadcast_to(row, (HD, row.shape[1])).T[:, :1]
    scores = dot(qkv_ref[0], qkv_ref[1], NT) * FACTOR
    scores = jnp.where(row <= column, scores, -1e30)
    expd = jnp.exp(scores - jnp.max(scores, axis=1, keepdims=True))
    attn = (expd / jnp.sum(expd, axis=1, keepdims=True)).astype(jnp.bfloat16)
    attn_ref[0] = attn
    attended = dot(attn, qkv_ref[2])
    out_ref[...] = attended.astype(jnp.bfloat16)
    out_t_ref[...] = attended.T.astype(jnp.bfloat16)


def attend(positions, qkv):
    _, seq, columns = qkv.shape
    heads = columns // HD
    return pl.pallas_call(
        attend_kernel,
        grid=(heads,),
        in_specs=[
            pl.BlockSpec((1, seq), lambda h: (0, 0)),
            pl.BlockSpec((3, seq, HD), lambda h: (0, 0, h)),
        ],
        out_specs=[
            pl.BlockSpec((1, seq, seq), lambda h: (h, 0, 0)),
            pl.BlockSpec((seq, HD), lambda h: (0, h)),
            pl.BlockSpec((HD, seq), lambda h: (h, 0)),
        ],
        out_shape=[
            jax.ShapeDtypeStruct((heads, seq, seq), jnp.bfloat16),
            jax.ShapeDtypeStruct((seq, columns), jnp.bfloat16),
            jax.ShapeDtypeStruct((columns, seq), jnp.bfloat16),
        ],
        compiler_params=params(60),
        cost_estimate=cost(4 * seq * seq * columns, 5 * MIB, heads * seq * seq),
    )(positions[None, :], qkv)


def attend_back_kernel(qkv_ref, attn_ref, attended_ref, grad_ref, out_ref):
    grad = grad_ref[...]
    attn = attn_ref[0]
    row_dot = jnp.sum(
        grad.astype(jnp.float32) * attended_ref[...].astype(jnp.float32), axis=1, keepdims=True
    )
    grad_attn = dot(grad, qkv_ref[2], NT)
    grad_scores = (attn.astype(jnp.float32) * (grad_attn - row_dot) * FACTOR).astype(jnp.bfloat16)
    out_ref[0] = dot(grad_scores, qkv_ref[1]).astype(jnp.bfloat16)
    out_ref[1] = dot(grad_scores, qkv_ref[0], TN).astype(jnp.bfloat16)
    out_ref[2] = dot(attn, grad, TN).astype(jnp.bfloat16)


def attend_back(qkv, attn, attended, grad):
    _, seq, columns = qkv.shape
    planes = pl.BlockSpec((3, seq, HD), lambda h: (0, 0, h))
    one = pl.BlockSpec((seq, HD), lambda h: (0, h))
    return pl.pallas_call(
        attend_back_kernel,
        grid=(columns // HD,),
        in_specs=[planes, pl.BlockSpec((1, seq, seq), lambda h: (h, 0, 0)), one, one],
        out_specs=planes,
        out_shape=jax.ShapeDtypeStruct(qkv.shape, jnp.bfloat16),
        compiler_params=params(24),
        cost_estimate=cost(8 * seq * seq * columns, 6 * MIB),
    )(qkv, attn, attended, grad)


REST = pl.BlockSpec(memory_space=pl.ANY)
SCALARS = pl.BlockSpec(memory_space=pltpu.SMEM)


def single(places, refs):
    found = []
    for place, ref in zip(places, refs):
        if len(ref.shape) == 2:
            found.append((place, ref))
        else:
            found += [(place + i, ref.at[i]) for i in range(ref.shape[0])]
    return found


def count_of(blocks):
    return sum(1 if array.ndim == 2 else array.shape[0] for _, array in blocks)


def started(source, target, sem):
    copy = pltpu.make_async_copy(source, target, sem)
    copy.start()
    return copy


def columns_of(plan_ref, place, part):
    return pl.ds(pl.multiple_of(plan_ref[place] * part, 128), part)


def grad_heads_kernel(places, first, last, plan_ref, w_ref, *refs):
    total_ref, out_ref, held, weights, sems, weight_sems, total = refs[len(places) :]
    part = held.shape[2]
    copies = []
    for i, (place, block) in enumerate(single(places, refs)):
        weight = w_ref.at[:, columns_of(plan_ref, place, part)]
        copies.append(
            (
                started(block, held.at[i], sems.at[i]),
                started(weight, weights.at[i], weight_sems.at[i]),
            )
        )
    for i, (block, weight) in enumerate(copies):
        block.wait()
        weight.wait()
        term = dot(held[i], weights[i], NT)
        if i:
            total[...] += term
        else:
            total[...] = term if first else total_ref[...] + term
    out_ref[...] = total[...].astype(jnp.bfloat16) if last else total[...]


def grad_heads(plan, w_out, blocks, total=None, last=False):
    columns = w_out.shape[0]
    seq, part = blocks[0][1].shape[-2:]
    count = count_of(blocks)
    vmem = pl.BlockSpec(memory_space=pltpu.VMEM)
    first = total is None
    return pl.pallas_call(
        functools.partial(grad_heads_kernel, [place for place, _ in blocks], first, last),
        in_specs=[SCALARS, REST] + [REST] * len(blocks) + [REST if first else vmem],
        out_specs=vmem,
        out_shape=jax.ShapeDtypeStruct((seq, columns), jnp.bfloat16 if last else jnp.float32),
        scratch_shapes=[
            pltpu.VMEM((count, seq, part), jnp.bfloat16),
            pltpu.VMEM((count, columns, part), jnp.bfloat16),
            pltpu.SemaphoreType.DMA((count,)),
            pltpu.SemaphoreType.DMA((count,)),
            pltpu.VMEM((seq, columns), jnp.float32),
        ],
        compiler_params=params(48),
        cost_estimate=cost(2 * seq * columns * part * count, MIB * count),
    )(plan, w_out, *[array for _, array in blocks], plan if first else total)


SLOTS = 4


def weight_kernel(places, turn, plan_ref, left_ref, *refs):
    out_ref, inside, sems, held, out_sems = refs[-5:]
    found = single(places, refs)
    part = inside.shape[2]
    copies = [started(block, inside.at[i], sems.at[i]) for i, (_, block) in enumerate(found)]
    written = []
    for i, (place, _) in enumerate(found):
        slot = i % SLOTS
        copies[i].wait()
        if i >= SLOTS:
            written[i - SLOTS].wait()
        if turn:
            turned = inside[i].T
            for k in range(3):
                held[slot, k] = dot(turned, left_ref[k]).astype(jnp.bfloat16)
        else:
            held[slot] = dot(left_ref[...], inside[i]).astype(jnp.bfloat16)
        target = out_ref.at[:, columns_of(plan_ref, place, part)]
        written.append(started(held.at[slot], target, out_sems.at[slot]))
    for copy in written[-SLOTS:]:
        copy.wait()


def weight_grad(plan, left, blocks, shape, into=None):
    turn = left.ndim == 3
    seq, part = blocks[0][1].shape[-2:]
    count = count_of(blocks)
    held = (3, part, left.shape[2]) if turn else (left.shape[0], part)
    size = math.prod(held) * count
    return pl.pallas_call(
        functools.partial(weight_kernel, [place for place, _ in blocks], turn),
        in_specs=[SCALARS, pl.BlockSpec(memory_space=pltpu.VMEM)]
        + [REST] * (len(blocks) + (into is not None)),
        out_specs=REST,
        out_shape=jax.ShapeDtypeStruct(shape, jnp.bfloat16),
        scratch_shapes=[
            pltpu.VMEM((count, seq, part), jnp.bfloat16),
            pltpu.SemaphoreType.DMA((count,)),
            pltpu.VMEM((SLOTS, *held), jnp.bfloat16),
            pltpu.SemaphoreType.DMA((SLOTS,)),
        ],
        input_output_aliases={} if into is None else {2 + len(blocks): 0},
        compiler_params=params(32),
        cost_estimate=cost(2 * seq * size, 3 * size),
    )(plan, left, *[array for _, array in blocks], *([] if into is None else [into]))


def terms_kernel(place, plan_ref, grad_ref, w_ref, *refs):
    grads, weights, held, grad_sems, sems, out_sems = refs[-6:]
    outs = refs[:-6]
    rows = weights.shape[2]
    copies = []
    for i in range(len(outs)):
        block = pl.ds(pl.multiple_of(plan_ref[place + i] * rows, 128), rows)
        for k in range(3):
            if i == 0:
                copies.append([started(grad_ref.at[k], grads.at[k], grad_sems.at[k])])
            else:
                copies.append([])
            source = w_ref.at[k, block]
            copies[-1].append(started(source, weights.at[i, k], sems.at[i, k]))
    written = []
    for i, out_ref in enumerate(outs):
        total = None
        for k in range(3):
            for copy in copies[3 * i + k]:
                copy.wait()
            term = dot(grads[k], weights[i, k], NT)
            total = term if total is None else total + term
        core = plan_ref[0] if i == len(outs) - 1 else 1 - plan_ref[0]
        held[i, 1 - core] = total[:, : rows // 2].astype(jnp.bfloat16)
        held[i, core] = total[:, rows // 2 :].astype(jnp.bfloat16)
        written.append(started(held.at[i], out_ref, out_sems.at[i]))
    for copy in written:
        copy.wait()


def terms(plan, place, count, grad, w, part):
    _, seq, columns = grad.shape
    shape = jax.ShapeDtypeStruct((2, seq, part), jnp.bfloat16)
    return pl.pallas_call(
        functools.partial(terms_kernel, place),
        in_specs=[SCALARS, REST, REST],
        out_specs=[REST] * count,
        out_shape=[shape] * count,
        scratch_shapes=[
            pltpu.VMEM(grad.shape, jnp.bfloat16),
            pltpu.VMEM((count, 3, 2 * part, columns), jnp.bfloat16),
            pltpu.VMEM((count, 2, seq, part), jnp.bfloat16),
            pltpu.SemaphoreType.DMA((3,)),
            pltpu.SemaphoreType.DMA((count, 3)),
            pltpu.SemaphoreType.DMA((count,)),
        ],
        compiler_params=params(48),
        cost_estimate=cost(12 * seq * columns * part * count, 5 * MIB * count),
    )(plan, grad, w)


def plain(n, inputs, out_grad, w_qkv, w_out, saved_qkv, positions):
    full_in = lax.all_gather(inputs, "gx", axis=1, tiled=True)
    full_grad = lax.all_gather(out_grad, "gx", axis=1, tiled=True)
    qkv = saved_qkv.transpose(1, 0, 2)
    attn, attended, _ = attend(positions, qkv)
    grad_h = dot(full_grad, w_out, NT).astype(jnp.bfloat16)
    grad_w_out = dot(attended, full_grad, TN).astype(jnp.bfloat16)
    grad = attend_back(qkv, attn, attended, grad_h)
    grad_w_qkv = jnp.stack([dot(full_in, grad[k], TN).astype(jnp.bfloat16) for k in range(3)], 1)
    partial = sum(dot(grad[k], w_qkv[:, k], NT) for k in range(3))
    input_grad = lax.psum_scatter(partial, "gx", scatter_dimension=1, tiled=True)
    return input_grad.astype(jnp.bfloat16), grad_w_qkv, grad_w_out


def ring_order(chips):
    if chips == 8:
        return [0, 2, 4, 6, 7, 5, 3, 1]
    return list(range(chips))


def plan_of(order, device):
    chips = len(order)
    at = order.index(device // 2)
    core = device % 2

    def chip(offset):
        return order[(at + offset) % chips]

    blocks = [2 * chip(0) + core, 2 * chip(0) + 1 - core]
    for step in range(1, chips // 2):
        behind, ahead = (-step, step) if core == 0 else (step, -step)
        blocks += [2 * chip(behind) + core, 2 * chip(behind) + 1 - core]
        blocks += [2 * chip(ahead) + 1 - core, 2 * chip(ahead) + core]
    blocks += [2 * chip(chips // 2) + core, 2 * chip(chips // 2) + 1 - core]
    summed = [chip(chips // 2)]
    for step in range(chips // 2 - 1, 0, -1):
        ahead = step if core == 0 else -step
        summed += [chip(-ahead), chip(ahead)]
    return [core] + blocks + summed + [chip(0)]


def after(x, *others):
    return lax.optimization_barrier((x, *others))[0]


def together(*arrays):
    return lax.optimization_barrier(arrays)


def f32(x):
    return x.astype(jnp.float32)


def on_device(n, inputs, out_grad, w_qkv, w_out, saved_qkv, positions):
    part = inputs.shape[1]
    if part % 128 or n != 16:
        return plain(n, inputs, out_grad, w_qkv, w_out, saved_qkv, positions)
    order = ring_order(n // 2)
    chips = range(n // 2)
    ring = [(2 * order[i], 2 * order[i - 1]) for i in chips]
    ring = [(j, i) for i, j in ring] + [(i + 1, j + 1) for i, j in ring]
    swap = [(i, i ^ 1) for i in range(n)]
    plans = [plan_of(order, i) for i in range(n)]
    size = len(plans[0])
    plan = lax.dynamic_slice(
        jnp.array(sum(plans, []), jnp.int32), (lax.axis_index("gx") * size,), (size,)
    )

    def send(x):
        return lax.ppermute(x, "gx", ring)

    def swapped(x):
        return lax.ppermute(x, "gx", swap)

    def blocks(step, *arrays):
        found, place = [], 1 if step == 0 else 4 * step - 1
        for array in arrays:
            found.append((place, array))
            place += 1 if array.ndim == 2 else array.shape[0]
        return found

    def grad_qkv(index, some, into=None):
        return weight_grad(index, grad, some, w.shape, into)

    def total(*values):
        return sum(f32(value) for value in values[1:]) + f32(values[0])

    def rounded_total(*values):
        return total(*values).astype(jnp.bfloat16)

    qkv = saved_qkv.transpose(1, 0, 2)
    w = w_qkv.transpose(1, 0, 2)

    a1 = send(out_grad)
    other = swapped(out_grad)
    b1 = send(other)
    attn, attended, attended_t = attend(positions, qkv)

    def grad_out_heads(index, some, so_far=None, last=False):
        return grad_heads(index, w_out, some, so_far, last)

    def grad_out(index, some, into=None):
        return weight_grad(index, attended_t, some, w_out.shape, into)

    a1 = after(a1, attended)
    a2, a1x = send(a1), swapped(a1)
    g0 = blocks(0, out_grad, other)
    grad_h = grad_out_heads(after(plan, a1), g0)

    b1 = after(b1, grad_h)
    b2, b1x = send(b1), swapped(b1)
    out = grad_out(after(plan, b1), g0)

    a2 = after(a2, out)
    a3, a2x = send(a2), swapped(a2)
    g1 = blocks(1, a1, b1, a1x, b1x)
    grad_h = grad_out_heads(after(plan, a2), g1, grad_h)

    b2 = after(b2, grad_h)
    b3, b2x = send(b2), swapped(b2)
    out = grad_out(after(plan, b2), g1, out)

    a3 = after(a3, out)
    a4, a3x = send(a3), swapped(a3)
    g2 = blocks(2, a2, b2, a2x, b2x)
    grad_h = grad_out_heads(after(plan, a3), g2, grad_h)

    b3, grad_h, plan = together(b3, grad_h, plan)
    b3x = swapped(b3)
    inputs = after(inputs, b3)
    other = swapped(inputs)
    out = grad_out(plan, g2, out)

    out, other, a3x, b3x, plan = together(out, other, a3x, b3x, plan)
    i0 = jnp.stack([inputs, other])
    i1 = send(i0)
    g3 = blocks(3, a3, b3, a3x, b3x)
    grad_h = grad_out_heads(plan, g3, grad_h)

    grad_h, a4, plan = together(grad_h, a4, plan)
    a4x = swapped(a4)
    out = grad_out(plan, g3, out)

    out, a4x, plan = together(out, a4x, plan)
    g4 = blocks(4, a4, a4x)
    grad_h = grad_out_heads(plan, g4, grad_h, last=True)
    grad = attend_back(qkv, attn, attended, grad_h)
    (t4,) = terms(plan, 17, 1, grad, w, part)

    t4, i1, plan = together(t4, i1, plan)
    theirs = swapped(t4[0])
    i2, i1x = send(i1), swapped(i1)
    weight = grad_qkv(plan, blocks(0, i0))

    weight, theirs, plan = together(weight, theirs, plan)
    m4 = send(rounded_total(t4[1], theirs))
    theirs, t3 = terms(plan, 18, 2, grad, w, part)

    theirs, t3, m4, plan = together(theirs, t3, m4, plan)
    theirs = swapped(theirs)
    out = grad_out(plan, g4, out)

    out, theirs, i2, plan = together(out, theirs, i2, plan)
    o3 = send(rounded_total(t3[0], theirs[0]))
    m3 = send(rounded_total(t3[1], theirs[1], m4))
    i3, i2x = send(i2), swapped(i2)
    theirs, t2 = terms(plan, 20, 2, grad, w, part)

    theirs, t2, i1x, plan = together(theirs, t2, i1x, plan)
    theirs = swapped(theirs)
    weight = grad_qkv(plan, blocks(1, i1, i1x), weight)

    weight, theirs, o3, m3, i3, plan = together(weight, theirs, o3, m3, i3, plan)
    o2 = send(rounded_total(t2[0], theirs[0], o3))
    m2 = send(rounded_total(t2[1], theirs[1], m3))
    i4, i3x = send(i3[0]), swapped(i3)
    theirs, t1 = terms(plan, 22, 2, grad, w, part)

    theirs, t1, i2x, plan = together(theirs, t1, i2x, plan)
    theirs = swapped(theirs)
    weight = grad_qkv(plan, blocks(2, i2, i2x), weight)

    weight, theirs, o2, m2, i4, plan = together(weight, theirs, o2, m2, i4, plan)
    o1 = send(rounded_total(t1[0], theirs[0], o2))
    m1 = send(rounded_total(t1[1], theirs[1], m2))
    i4x = swapped(i4)
    (t0,) = terms(plan, 24, 1, grad, w, part)

    t0, i3x, plan = together(t0, i3x, plan)
    weight = grad_qkv(plan, blocks(3, i3, i3x), weight)

    weight, o1, i4x, plan = together(weight, o1, i4x, plan)
    theirs = swapped(rounded_total(t0[0], o1))
    weight = grad_qkv(plan, blocks(4, i4, i4x), weight)

    weight, theirs, m1 = together(weight, theirs, m1)
    return rounded_total(t0[1], m1, theirs), weight.transpose(1, 0, 2), out


def solution(mesh):
    placed = (
        P("runs", "gx"),
        P("runs", "gx"),
        P(None, None, "gx"),
        P("gx", None),
        P("runs", None, "gx"),
        P("runs"),
    )
    return jax.shard_map(
        functools.partial(on_device, mesh.shape["gx"]),
        mesh=mesh,
        in_specs=placed,
        out_specs=(P("runs", "gx"), P("runs", None, "gx"), P(("runs", "gx"), None)),
        check_vma=False,
    )
```

```python
import functools
import math

import jax
import jax.numpy as jnp
from jax import lax
from jax.experimental import pallas as pl
from jax.experimental.pallas import tpu as pltpu
from jax.sharding import PartitionSpec as P

HD = 128
FACTOR = 1.0 / math.sqrt(HD)
MIB = 1 << 20
NT = (((1,), (1,)), ((), ()))
TN = (((0,), (0,)), ((), ()))


def dot(a, b, dims=(((1,), (0,)), ((), ()))):
    return lax.dot_general(a, b, dims, preferred_element_type=jnp.float32)


def params(mib):
    return pltpu.CompilerParams(vmem_limit_bytes=mib * MIB)


def cost(flops, nbytes, transcendentals=0):
    flops, nbytes = flops // 4096, nbytes // 4096
    return pl.CostEstimate(flops=flops, bytes_accessed=nbytes, transcendentals=transcendentals)


def attend_kernel(row_ref, qkv_ref, attn_ref, out_ref, out_t_ref, column):
    row = row_ref[...]

    @pl.when(pl.program_id(0) == 0)
    def _():
        column[...] = jnp.broadcast_to(row, (HD, row.shape[1])).T

    scores = dot(qkv_ref[0], qkv_ref[1], NT) * FACTOR
    scores = jnp.where(row <= column[:, :1], scores, -1e30)
    expd = jnp.exp(scores - jnp.max(scores, axis=1, keepdims=True))
    attn = (expd / jnp.sum(expd, axis=1, keepdims=True)).astype(jnp.bfloat16)
    attn_ref[0] = attn
    attended = dot(attn, qkv_ref[2])
    out_ref[...] = attended.astype(jnp.bfloat16)
    out_t_ref[...] = attended.T.astype(jnp.bfloat16)


def attend(positions, qkv):
    _, seq, columns = qkv.shape
    heads = columns // HD
    return pl.pallas_call(
        attend_kernel,
        grid=(heads,),
        in_specs=[
            pl.BlockSpec((1, seq), lambda h: (0, 0)),
            pl.BlockSpec((3, seq, HD), lambda h: (0, 0, h)),
        ],
        out_specs=[
            pl.BlockSpec((1, seq, seq), lambda h: (h, 0, 0)),
            pl.BlockSpec((seq, HD), lambda h: (0, h)),
            pl.BlockSpec((HD, seq), lambda h: (h, 0)),
        ],
        out_shape=[
            jax.ShapeDtypeStruct((heads, seq, seq), jnp.bfloat16),
            jax.ShapeDtypeStruct((seq, columns), jnp.bfloat16),
            jax.ShapeDtypeStruct((columns, seq), jnp.bfloat16),
        ],
        scratch_shapes=[pltpu.VMEM((seq, HD), jnp.int32)],
        compiler_params=params(60),
        cost_estimate=cost(4 * seq * seq * columns, 5 * MIB, heads * seq * seq),
    )(positions[None, :], qkv)


def attend_back_kernel(qkv_ref, attn_ref, attended_ref, grad_ref, out_ref):
    grad = grad_ref[...]
    attn = attn_ref[0]
    row_dot = jnp.sum(
        grad.astype(jnp.float32) * attended_ref[...].astype(jnp.float32), axis=1, keepdims=True
    )
    grad_attn = dot(grad, qkv_ref[2], NT)
    grad_scores = (attn.astype(jnp.float32) * (grad_attn - row_dot) * FACTOR).astype(jnp.bfloat16)
    out_ref[0] = dot(grad_scores, qkv_ref[1]).astype(jnp.bfloat16)
    out_ref[1] = dot(grad_scores, qkv_ref[0], TN).astype(jnp.bfloat16)
    out_ref[2] = dot(attn, grad, TN).astype(jnp.bfloat16)


def attend_back(qkv, attn, attended, grad):
    _, seq, columns = qkv.shape
    planes = pl.BlockSpec((3, seq, HD), lambda h: (0, 0, h))
    one = pl.BlockSpec((seq, HD), lambda h: (0, h))
    return pl.pallas_call(
        attend_back_kernel,
        grid=(columns // HD,),
        in_specs=[planes, pl.BlockSpec((1, seq, seq), lambda h: (h, 0, 0)), one, one],
        out_specs=planes,
        out_shape=jax.ShapeDtypeStruct(qkv.shape, jnp.bfloat16),
        compiler_params=params(24),
        cost_estimate=cost(8 * seq * seq * columns, 6 * MIB),
    )(qkv, attn, attended, grad)


def grad_heads_kernel(count, first, last, plan_ref, *refs):
    blocks, weights, rest = refs[:count], refs[count : 2 * count], refs[2 * count :]
    out_ref, total = rest[-2:]
    for i, (block, weight) in enumerate(zip(blocks, weights)):
        term = dot(block[...], weight[...], NT)
        if i:
            total[...] += term
        else:
            total[...] = term if first else rest[0][...] + term
    out_ref[...] = total[...].astype(jnp.bfloat16) if last else total[...]


def grad_heads(plan, w_out, blocks, total=None, last=False):
    columns = w_out.shape[0]
    seq, part = blocks[0][1].shape
    count = len(blocks)

    def weight(place):
        return pl.BlockSpec((columns, part), lambda step, plan: (0, plan[place]))

    def whole(shape):
        return pl.BlockSpec(shape, lambda step, plan: (0, 0))

    first = total is None
    return pl.pallas_call(
        functools.partial(grad_heads_kernel, count, first, last),
        grid_spec=pltpu.PrefetchScalarGridSpec(
            num_scalar_prefetch=1,
            grid=(1,),
            in_specs=[whole((seq, part))] * count
            + [weight(place) for place, _ in blocks]
            + [whole((seq, columns))] * (not first),
            out_specs=whole((seq, columns)),
            scratch_shapes=[pltpu.VMEM((seq, columns), jnp.float32)],
        ),
        out_shape=jax.ShapeDtypeStruct((seq, columns), jnp.bfloat16 if last else jnp.float32),
        compiler_params=params(48),
        cost_estimate=cost(2 * seq * columns * part * count, MIB * count),
    )(plan, *[block for _, block in blocks], *[w_out] * count, *([] if first else [total]))


SLOTS = 4


def weight_kernel(places, turn, plan_ref, left_ref, *refs):
    out_ref, held, sems = refs[-3:]
    copies = []
    for i, (place, block) in enumerate(zip(places, refs)):
        width = block.shape[1]
        slot = i % SLOTS
        if i >= SLOTS:
            copies[i - SLOTS].wait()
        if turn:
            turned = block[...].T
            for k in range(3):
                held[slot, k] = dot(turned, left_ref[k]).astype(jnp.bfloat16)
        else:
            held[slot] = dot(left_ref[...], block[...]).astype(jnp.bfloat16)
        start = pl.multiple_of(plan_ref[place] * width, 128)
        copy = pltpu.make_async_copy(
            held.at[slot], out_ref.at[:, pl.ds(start, width)], sems.at[slot]
        )
        copy.start()
        copies.append(copy)
    for copy in copies[-SLOTS:]:
        copy.wait()


def weight_grad(plan, left, blocks, shape, into=None):
    turn = left.ndim == 3
    seq, part = blocks[0][1].shape
    count = len(blocks)
    held = (3, part, left.shape[2]) if turn else (left.shape[0], part)
    vmem = pl.BlockSpec(memory_space=pltpu.VMEM)
    rest = pl.BlockSpec(memory_space=pl.ANY)
    size = math.prod(held) * count
    return pl.pallas_call(
        functools.partial(weight_kernel, [place for place, _ in blocks], turn),
        in_specs=[pl.BlockSpec(memory_space=pltpu.SMEM)]
        + [vmem] * (1 + count)
        + [rest] * (into is not None),
        out_specs=rest,
        out_shape=jax.ShapeDtypeStruct(shape, jnp.bfloat16),
        scratch_shapes=[
            pltpu.VMEM((SLOTS, *held), jnp.bfloat16),
            pltpu.SemaphoreType.DMA((SLOTS,)),
        ],
        input_output_aliases={} if into is None else {2 + count: 0},
        compiler_params=params(40),
        cost_estimate=cost(2 * seq * size, 3 * size),
    )(plan, left, *[block for _, block in blocks], *([] if into is None else [into]))


def terms_kernel(receivers, plan_ref, grad_ref, w_ref, *out_refs):
    total = dot(grad_ref[0], w_ref[0], NT)
    total += dot(grad_ref[1], w_ref[1], NT)
    total += dot(grad_ref[2], w_ref[2], NT)
    total = total.astype(jnp.bfloat16)
    part = total.shape[1] // 2
    step = pl.program_id(0)
    for i, out_ref in enumerate(out_refs):
        core = 1 - plan_ref[0] if receivers[i] else plan_ref[0]

        @pl.when((step == i) & (core == 0))
        def _():
            out_ref[0] = total[:, part:]
            out_ref[1] = total[:, :part]

        @pl.when((step == i) & (core == 1))
        def _():
            out_ref[0] = total[:, :part]
            out_ref[1] = total[:, part:]


def terms(plan, place, receivers, grad, w, part):
    _, seq, columns = grad.shape
    count = len(receivers)
    out = pl.BlockSpec((2, seq, part), lambda i, plan: (0, 0, 0))
    shape = jax.ShapeDtypeStruct((2, seq, part), jnp.bfloat16)
    return pl.pallas_call(
        functools.partial(terms_kernel, receivers),
        grid_spec=pltpu.PrefetchScalarGridSpec(
            num_scalar_prefetch=1,
            grid=(count,),
            in_specs=[
                pl.BlockSpec((3, seq, columns), lambda i, plan: (0, 0, 0)),
                pl.BlockSpec((3, 2 * part, columns), lambda i, plan: (0, plan[place + i], 0)),
            ],
            out_specs=[out] * count,
        ),
        out_shape=[shape] * count,
        compiler_params=params(48),
        cost_estimate=cost(12 * seq * columns * part * count, 5 * MIB * count),
    )(plan, grad, w)


def plain(n, inputs, out_grad, w_qkv, w_out, saved_qkv, positions):
    full_in = lax.all_gather(inputs, "gx", axis=1, tiled=True)
    full_grad = lax.all_gather(out_grad, "gx", axis=1, tiled=True)
    qkv = saved_qkv.transpose(1, 0, 2)
    attn, attended, _ = attend(positions, qkv)
    grad_h = dot(full_grad, w_out, NT).astype(jnp.bfloat16)
    grad_w_out = dot(attended, full_grad, TN).astype(jnp.bfloat16)
    grad = attend_back(qkv, attn, attended, grad_h)
    grad_w_qkv = jnp.stack([dot(full_in, grad[k], TN).astype(jnp.bfloat16) for k in range(3)], 1)
    partial = sum(dot(grad[k], w_qkv[:, k], NT) for k in range(3))
    input_grad = lax.psum_scatter(partial, "gx", scatter_dimension=1, tiled=True)
    return input_grad.astype(jnp.bfloat16), grad_w_qkv, grad_w_out


def ring_order(chips):
    if chips == 8:
        return [0, 2, 4, 6, 7, 5, 3, 1]
    return list(range(chips))


def plan_of(order, device):
    chips = len(order)
    at = order.index(device // 2)
    core = device % 2

    def chip(offset):
        return order[(at + offset) % chips]

    blocks = [2 * chip(0) + core, 2 * chip(0) + 1 - core]
    for step in range(1, chips // 2):
        behind, ahead = (-step, step) if core == 0 else (step, -step)
        blocks += [2 * chip(behind) + core, 2 * chip(behind) + 1 - core]
        blocks += [2 * chip(ahead) + 1 - core, 2 * chip(ahead) + core]
    blocks += [2 * chip(chips // 2) + core, 2 * chip(chips // 2) + 1 - core]
    summed = [chip(chips // 2)]
    for step in range(chips // 2 - 1, 0, -1):
        ahead = step if core == 0 else -step
        summed += [chip(-ahead), chip(ahead)]
    return [core] + blocks + summed + [chip(0)]


def after(x, *others):
    return lax.optimization_barrier((x, *others))[0]


def together(*arrays):
    return lax.optimization_barrier(arrays)


def f32(x):
    return x.astype(jnp.float32)


def on_device(n, inputs, out_grad, w_qkv, w_out, saved_qkv, positions):
    part = inputs.shape[1]
    if part % 128 or n != 16:
        return plain(n, inputs, out_grad, w_qkv, w_out, saved_qkv, positions)
    order = ring_order(n // 2)
    chips = range(n // 2)
    ring = [(2 * order[i], 2 * order[i - 1]) for i in chips]
    ring = [(j, i) for i, j in ring] + [(i + 1, j + 1) for i, j in ring]
    swap = [(i, i ^ 1) for i in range(n)]
    plans = [plan_of(order, i) for i in range(n)]
    size = len(plans[0])
    plan = lax.dynamic_slice(
        jnp.array(sum(plans, []), jnp.int32), (lax.axis_index("gx") * size,), (size,)
    )

    def send(x):
        return lax.ppermute(x, "gx", ring)

    def swapped(x):
        return lax.ppermute(x, "gx", swap)

    def blocks(step, *arrays):
        first = 1 if step == 0 else 4 * step - 1
        return [(first + i, array) for i, array in enumerate(arrays)]

    def grad_qkv(index, some, into=None):
        return weight_grad(index, grad, some, w.shape, into)

    def total(*values):
        return sum(f32(value) for value in values[1:]) + f32(values[0])

    def rounded_total(*values):
        return total(*values).astype(jnp.bfloat16)

    qkv = saved_qkv.transpose(1, 0, 2)
    w = w_qkv.transpose(1, 0, 2)

    a1 = send(out_grad)
    other = swapped(out_grad)
    b1 = send(other)
    attn, attended, attended_t = attend(positions, qkv)

    def grad_out_heads(index, some, so_far=None, last=False):
        return grad_heads(index, w_out, some, so_far, last)

    def grad_out(index, some, into=None):
        return weight_grad(index, attended_t, some, w_out.shape, into)

    a1 = after(a1, attended)
    a2, a1x = send(a1), swapped(a1)
    g0 = blocks(0, out_grad, other)
    grad_h = grad_out_heads(after(plan, a1), g0)

    b1 = after(b1, grad_h)
    b2, b1x = send(b1), swapped(b1)
    out = grad_out(after(plan, b1), g0)

    a2 = after(a2, out)
    a3, a2x = send(a2), swapped(a2)
    g1 = blocks(1, a1, b1, a1x, b1x)
    grad_h = grad_out_heads(after(plan, a2), g1, grad_h)

    b2 = after(b2, grad_h)
    b3, b2x = send(b2), swapped(b2)
    out = grad_out(after(plan, b2), g1, out)

    a3 = after(a3, out)
    a4, a3x = send(a3), swapped(a3)
    inputs = after(inputs, a3)
    other = swapped(inputs)
    i1 = send(inputs)
    g2 = blocks(2, a2, b2, a2x, b2x)
    grad_h = grad_out_heads(after(plan, a3), g2, grad_h)

    b3, grad_h, other, plan = together(b3, grad_h, other, plan)
    b3x = swapped(b3)
    j1 = send(other)
    f0 = blocks(0, inputs, other)
    out = grad_out(plan, g2, out)

    out, a3x, b3x, plan = together(out, a3x, b3x, plan)
    g3 = blocks(3, a3, b3, a3x, b3x)
    grad_h = grad_out_heads(plan, g3, grad_h)

    grad_h, a4, i1, plan = together(grad_h, a4, i1, plan)
    a4x = swapped(a4)
    i2, i1x = send(i1), swapped(i1)

    a4x, j1, plan = together(a4x, j1, plan)
    j2, j1x = send(j1), swapped(j1)
    g4 = blocks(4, a4, a4x)
    grad_h = grad_out_heads(plan, g4, grad_h, last=True)
    grad = attend_back(qkv, attn, attended, grad_h)

    grad, i2, plan = together(grad, i2, plan)
    i3, i2x = send(i2), swapped(i2)
    t4, theirs3, t3 = terms(plan, 17, (0, 1, 0), grad, w, part)

    t4, theirs3, t3, j2, i3, plan = together(t4, theirs3, t3, j2, i3, plan)
    theirs4 = swapped(t4[0])
    theirs3 = swapped(theirs3)
    j3, j2x = send(j2), swapped(j2)
    i4, i3x = send(i3), swapped(i3)
    out = grad_out(plan, g3 + g4, out)

    out, theirs4, theirs3, plan = together(out, theirs4, theirs3, plan)
    m4 = send(rounded_total(t4[1], theirs4))
    theirs2, t2 = terms(plan, 20, (1, 0), grad, w, part)

    theirs2, t2, m4, j3, i4, plan = together(theirs2, t2, m4, j3, i4, plan)
    o3 = send(rounded_total(t3[0], theirs3[0]))
    m3 = send(rounded_total(t3[1], theirs3[1], m4))
    theirs2 = swapped(theirs2)
    j3x = swapped(j3)
    i4x = swapped(i4)
    theirs1, t1, t0 = terms(plan, 22, (1, 0, 0), grad, w, part)

    theirs1, t1, t0, theirs2, m3, o3, plan = together(theirs1, t1, t0, theirs2, m3, o3, plan)
    o2 = send(rounded_total(t2[0], theirs2[0], o3))
    m2 = send(rounded_total(t2[1], theirs2[1], m3))
    theirs1 = swapped(theirs1)
    some = f0 + blocks(1, i1, j1, i1x, j1x) + blocks(4, i4, i4x)
    weight = grad_qkv(plan, some)

    weight, theirs1, o2, m2, plan = together(weight, theirs1, o2, m2, plan)
    o1 = send(rounded_total(t1[0], theirs1[0], o2))
    m1 = send(rounded_total(t1[1], theirs1[1], m2))
    some = blocks(2, i2, j2, i2x, j2x) + blocks(3, i3, j3, i3x, j3x)
    weight = grad_qkv(plan, some, weight)

    weight, o1, m1 = together(weight, o1, m1)
    theirs = swapped(rounded_total(t0[0], o1))
    return rounded_total(t0[1], m1, theirs), weight.transpose(1, 0, 2), out


def solution(mesh):
    placed = (
        P("runs", "gx"),
        P("runs", "gx"),
        P(None, None, "gx"),
        P("gx", None),
        P("runs", None, "gx"),
        P("runs"),
    )
    return jax.shard_map(
        functools.partial(on_device, mesh.shape["gx"]),
        mesh=mesh,
        in_specs=placed,
        out_specs=(P("runs", "gx"), P("runs", None, "gx"), P(("runs", "gx"), None)),
        check_vma=False,
    )
```

```python
import functools
import math

import jax
import jax.numpy as jnp
from jax import lax
from jax.experimental import pallas as pl
from jax.experimental.pallas import tpu as pltpu
from jax.sharding import PartitionSpec as P

HD = 128
FACTOR = 1.0 / math.sqrt(HD)
MIB = 1 << 20
NT = (((1,), (1,)), ((), ()))
TN = (((0,), (0,)), ((), ()))


def dot(a, b, dims=(((1,), (0,)), ((), ()))):
    return lax.dot_general(a, b, dims, preferred_element_type=jnp.float32)


def params(mib):
    return pltpu.CompilerParams(vmem_limit_bytes=mib * MIB)


def cost(flops, nbytes, transcendentals=0):
    flops, nbytes = flops // 4096, nbytes // 4096
    return pl.CostEstimate(flops=flops, bytes_accessed=nbytes, transcendentals=transcendentals)


def attend_kernel(row_ref, qkv_ref, attn_ref, out_ref, out_t_ref, column):
    row = row_ref[...]

    @pl.when(pl.program_id(0) == 0)
    def _():
        column[...] = jnp.broadcast_to(row, (HD, row.shape[1])).T

    scores = dot(qkv_ref[0], qkv_ref[1], NT) * FACTOR
    scores = jnp.where(row <= column[:, :1], scores, -1e30)
    expd = jnp.exp(scores - jnp.max(scores, axis=1, keepdims=True))
    attn = (expd / jnp.sum(expd, axis=1, keepdims=True)).astype(jnp.bfloat16)
    attn_ref[0] = attn
    attended = dot(attn, qkv_ref[2])
    out_ref[...] = attended.astype(jnp.bfloat16)
    out_t_ref[...] = attended.T.astype(jnp.bfloat16)


def attend(positions, qkv):
    _, seq, columns = qkv.shape
    heads = columns // HD
    return pl.pallas_call(
        attend_kernel,
        grid=(heads,),
        in_specs=[
            pl.BlockSpec((1, seq), lambda h: (0, 0)),
            pl.BlockSpec((3, seq, HD), lambda h: (0, 0, h)),
        ],
        out_specs=[
            pl.BlockSpec((1, seq, seq), lambda h: (h, 0, 0)),
            pl.BlockSpec((seq, HD), lambda h: (0, h)),
            pl.BlockSpec((HD, seq), lambda h: (h, 0)),
        ],
        out_shape=[
            jax.ShapeDtypeStruct((heads, seq, seq), jnp.bfloat16),
            jax.ShapeDtypeStruct((seq, columns), jnp.bfloat16),
            jax.ShapeDtypeStruct((columns, seq), jnp.bfloat16),
        ],
        scratch_shapes=[pltpu.VMEM((seq, HD), jnp.int32)],
        compiler_params=params(60),
        cost_estimate=cost(4 * seq * seq * columns, 5 * MIB, heads * seq * seq),
    )(positions[None, :], qkv)


def attend_back_kernel(qkv_ref, attn_ref, attended_ref, grad_ref, out_ref):
    grad = grad_ref[...]
    attn = attn_ref[0]
    row_dot = jnp.sum(
        grad.astype(jnp.float32) * attended_ref[...].astype(jnp.float32), axis=1, keepdims=True
    )
    grad_attn = dot(grad, qkv_ref[2], NT)
    grad_scores = (attn.astype(jnp.float32) * (grad_attn - row_dot) * FACTOR).astype(jnp.bfloat16)
    out_ref[0] = dot(grad_scores, qkv_ref[1]).astype(jnp.bfloat16)
    out_ref[1] = dot(grad_scores, qkv_ref[0], TN).astype(jnp.bfloat16)
    out_ref[2] = dot(attn, grad, TN).astype(jnp.bfloat16)


def attend_back(qkv, attn, attended, grad):
    _, seq, columns = qkv.shape
    planes = pl.BlockSpec((3, seq, HD), lambda h: (0, 0, h))
    one = pl.BlockSpec((seq, HD), lambda h: (0, h))
    return pl.pallas_call(
        attend_back_kernel,
        grid=(columns // HD,),
        in_specs=[planes, pl.BlockSpec((1, seq, seq), lambda h: (h, 0, 0)), one, one],
        out_specs=planes,
        out_shape=jax.ShapeDtypeStruct(qkv.shape, jnp.bfloat16),
        compiler_params=params(24),
        cost_estimate=cost(8 * seq * seq * columns, 6 * MIB),
    )(qkv, attn, attended, grad)


def grad_heads_kernel(count, first, last, plan_ref, *refs):
    blocks, (weight_ref, *rest) = refs[:count], refs[count:]
    out_ref, total = rest[-2:]
    for i, block in enumerate(blocks):

        @pl.when(pl.program_id(0) == i)
        def _():
            term = dot(block[...], weight_ref[...], NT)
            if i:
                total[...] += term
            else:
                total[...] = term if first else rest[0][...] + term
            if i == count - 1:
                out_ref[...] = total[...].astype(out_ref.dtype)


def grad_heads(plan, w_out, blocks, total=None, last=False):
    columns = w_out.shape[0]
    seq, part = blocks[0][1].shape
    count, place = len(blocks), blocks[0][0]

    def whole(shape):
        return pl.BlockSpec(shape, lambda step, plan: (0, 0))

    first = total is None
    return pl.pallas_call(
        functools.partial(grad_heads_kernel, count, first, last),
        grid_spec=pltpu.PrefetchScalarGridSpec(
            num_scalar_prefetch=1,
            grid=(count,),
            in_specs=[whole((seq, part))] * count
            + [pl.BlockSpec((columns, part), lambda step, plan: (0, plan[place + step]))]
            + [whole((seq, columns))] * (not first),
            out_specs=whole((seq, columns)),
            scratch_shapes=[pltpu.VMEM((seq, columns), jnp.float32)],
        ),
        out_shape=jax.ShapeDtypeStruct((seq, columns), jnp.bfloat16 if last else jnp.float32),
        compiler_params=params(48),
        cost_estimate=cost(2 * seq * columns * part * count, MIB * count),
    )(plan, *[block for _, block in blocks], w_out, *([] if first else [total]))


SLOTS = 4


def weight_kernel(places, turn, plan_ref, left_ref, *refs):
    out_ref, held, sems = refs[-3:]
    copies = []
    for i, (place, block) in enumerate(zip(places, refs)):
        width = block.shape[1]
        slot = i % SLOTS
        if i >= SLOTS:
            copies[i - SLOTS].wait()
        if turn:
            turned = block[...].T
            for k in range(3):
                held[slot, k] = dot(turned, left_ref[k]).astype(jnp.bfloat16)
        else:
            held[slot] = dot(left_ref[...], block[...]).astype(jnp.bfloat16)
        start = pl.multiple_of(plan_ref[place] * width, 128)
        copy = pltpu.make_async_copy(
            held.at[slot], out_ref.at[:, pl.ds(start, width)], sems.at[slot]
        )
        copy.start()
        copies.append(copy)
    for copy in copies[-SLOTS:]:
        copy.wait()


def weight_grad(plan, left, blocks, shape, into=None):
    turn = left.ndim == 3
    seq, part = blocks[0][1].shape
    count = len(blocks)
    held = (3, part, left.shape[2]) if turn else (left.shape[0], part)
    vmem = pl.BlockSpec(memory_space=pltpu.VMEM)
    rest = pl.BlockSpec(memory_space=pl.ANY)
    size = math.prod(held) * count
    return pl.pallas_call(
        functools.partial(weight_kernel, [place for place, _ in blocks], turn),
        in_specs=[pl.BlockSpec(memory_space=pltpu.SMEM)]
        + [vmem] * (1 + count)
        + [rest] * (into is not None),
        out_specs=rest,
        out_shape=jax.ShapeDtypeStruct(shape, jnp.bfloat16),
        scratch_shapes=[
            pltpu.VMEM((SLOTS, *held), jnp.bfloat16),
            pltpu.SemaphoreType.DMA((SLOTS,)),
        ],
        input_output_aliases={} if into is None else {2 + count: 0},
        compiler_params=params(40),
        cost_estimate=cost(2 * seq * size, 3 * size),
    )(plan, left, *[block for _, block in blocks], *([] if into is None else [into]))


def terms_kernel(plan_ref, grad_ref, w_ref, theirs_ref, mine_ref):
    total = dot(grad_ref[0], w_ref[0], NT)
    total += dot(grad_ref[1], w_ref[1], NT)
    total += dot(grad_ref[2], w_ref[2], NT)
    total = total.astype(jnp.bfloat16)
    part = total.shape[1] // 2

    @pl.when(plan_ref[0] == 0)
    def _():
        mine_ref[0] = total[:, :part]
        theirs_ref[0] = total[:, part:]

    @pl.when(plan_ref[0] == 1)
    def _():
        mine_ref[0] = total[:, part:]
        theirs_ref[0] = total[:, :part]


def terms(plan, place, count, grad, w, part):
    _, seq, columns = grad.shape
    out = pl.BlockSpec((1, seq, part), lambda i, plan: (i, 0, 0))
    shape = jax.ShapeDtypeStruct((count, seq, part), jnp.bfloat16)
    return pl.pallas_call(
        terms_kernel,
        grid_spec=pltpu.PrefetchScalarGridSpec(
            num_scalar_prefetch=1,
            grid=(count,),
            in_specs=[
                pl.BlockSpec((3, seq, columns), lambda i, plan: (0, 0, 0)),
                pl.BlockSpec((3, 2 * part, columns), lambda i, plan: (0, plan[place + i], 0)),
            ],
            out_specs=[out, out],
        ),
        out_shape=[shape, shape],
        compiler_params=params(48),
        cost_estimate=cost(12 * seq * columns * part * count, 5 * MIB * count),
    )(plan, grad, w)


def plain(n, inputs, out_grad, w_qkv, w_out, saved_qkv, positions):
    full_in = lax.all_gather(inputs, "gx", axis=1, tiled=True)
    full_grad = lax.all_gather(out_grad, "gx", axis=1, tiled=True)
    qkv = saved_qkv.transpose(1, 0, 2)
    attn, attended, _ = attend(positions, qkv)
    grad_h = dot(full_grad, w_out, NT).astype(jnp.bfloat16)
    grad_w_out = dot(attended, full_grad, TN).astype(jnp.bfloat16)
    grad = attend_back(qkv, attn, attended, grad_h)
    grad_w_qkv = jnp.stack([dot(full_in, grad[k], TN).astype(jnp.bfloat16) for k in range(3)], 1)
    partial = sum(dot(grad[k], w_qkv[:, k], NT) for k in range(3))
    input_grad = lax.psum_scatter(partial, "gx", scatter_dimension=1, tiled=True)
    return input_grad.astype(jnp.bfloat16), grad_w_qkv, grad_w_out


def ring_order(chips):
    if chips == 8:
        return [0, 2, 4, 6, 7, 5, 3, 1]
    return list(range(chips))


def plan_of(order, device):
    chips = len(order)
    at = order.index(device // 2)
    core = device % 2

    def chip(offset):
        return order[(at + offset) % chips]

    blocks = [2 * chip(0) + core, 2 * chip(0) + 1 - core]
    for step in range(1, chips // 2):
        for shard in (core, 1 - core):
            blocks += [2 * chip(-step) + shard, 2 * chip(step) + shard]
    blocks += [2 * chip(chips // 2) + core, 2 * chip(chips // 2) + 1 - core]
    summed = [chip(chips // 2)]
    for step in range(chips // 2 - 1, 0, -1):
        summed += [chip(step), chip(-step)]
    return [core] + blocks + summed + [chip(0)]


def after(x, *others):
    return lax.optimization_barrier((x, *others))[0]


def together(*arrays):
    return lax.optimization_barrier(arrays)


def f32(x):
    return x.astype(jnp.float32)


def on_device(n, inputs, out_grad, w_qkv, w_out, saved_qkv, positions):
    part = inputs.shape[1]
    if part % 128 or n != 16:
        return plain(n, inputs, out_grad, w_qkv, w_out, saved_qkv, positions)
    order = ring_order(n // 2)
    hops = [(2 * order[i - 1], 2 * order[i]) for i in range(n // 2)]
    ahead = [(i + core, j + core) for i, j in hops for core in range(2)]
    back = [(j, i) for i, j in ahead]
    apart = [(i, j) for i, j in hops] + [(j + 1, i + 1) for i, j in hops]
    swap = [(i, i ^ 1) for i in range(n)]
    plans = [plan_of(order, i) for i in range(n)]
    size = len(plans[0])
    plan = lax.dynamic_slice(
        jnp.array(sum(plans, []), jnp.int32), (lax.axis_index("gx") * size,), (size,)
    )
    on_first = lax.axis_index("gx") % 2 == 0

    def both_ways(right, left):
        return lax.ppermute(right, "gx", ahead), lax.ppermute(left, "gx", back)

    def one_way(right, left):
        return lax.ppermute(jnp.where(on_first, right, left), "gx", apart)

    def swapped(*arrays):
        found = [lax.ppermute(x, "gx", swap) for x in arrays]
        return found if len(found) > 1 else found[0]

    def blocks(step, *arrays):
        first = 1 if step == 0 else 4 * step - 1
        return [(first + i, array) for i, array in enumerate(arrays)]

    def grad_qkv(index, some, into=None):
        return weight_grad(index, grad, some, w.shape, into)

    def total(*values):
        return sum(f32(value) for value in values[1:]) + f32(values[0])

    def rounded_total(*values):
        return total(*values).astype(jnp.bfloat16)

    qkv = saved_qkv.transpose(1, 0, 2)
    w = w_qkv.transpose(1, 0, 2)

    def grad_out_heads(index, some, so_far=None, last=False):
        return grad_heads(index, w_out, some, so_far, last)

    def grad_out(index, some, into=None):
        return weight_grad(index, attended_t, some, w_out.shape, into)

    r1, l1 = both_ways(out_grad, out_grad)
    other = swapped(out_grad)
    attn, attended, attended_t = attend(positions, qkv)

    r1, l1, attended, plan = together(r1, l1, attended, plan)
    r2, l2 = both_ways(r1, l1)
    g1 = blocks(1, r1, l1, *swapped(r1, l1))
    g0 = blocks(0, out_grad, other)
    grad_h = grad_out_heads(plan, g0)
    out = grad_out(plan, g0)

    r2, l2, grad_h, out, plan = together(r2, l2, grad_h, out, plan)
    r3, l3 = both_ways(r2, l2)
    g2 = blocks(2, r2, l2, *swapped(r2, l2))
    grad_h = grad_out_heads(plan, g1, grad_h)
    out = grad_out(plan, g1, out)

    r3, l3, grad_h, out, plan = together(r3, l3, grad_h, out, plan)
    x4 = one_way(r3, l3)
    r3x, l3x = swapped(r3, l3)
    g3 = blocks(3, r3, l3, r3x, l3x)
    grad_h = grad_out_heads(plan, g2, grad_h)

    grad_h, r3x, l3x, inputs, plan = together(grad_h, r3x, l3x, inputs, plan)
    i1, j1 = both_ways(inputs, inputs)
    out = grad_out(plan, g2, out)
    grad_h = grad_out_heads(plan, g3, grad_h)

    x4, grad_h, out, plan = together(x4, grad_h, out, plan)
    x4x = swapped(x4)
    other = swapped(inputs)
    g4 = blocks(4, x4, x4x)
    grad_h = grad_out_heads(plan, g4, grad_h, last=True)
    grad = attend_back(qkv, attn, attended, grad_h)

    grad, i1, j1, other, plan = together(grad, i1, j1, other, plan)
    i2, j2 = both_ways(i1, j1)
    i1x, j1x = swapped(i1, j1)
    f0 = blocks(0, inputs, other)

    theirs3, mine3 = terms(plan, 17, 3, grad, w, part)

    theirs3, mine3, i2, j2, i1x, j1x, plan = together(theirs3, mine3, i2, j2, i1x, j1x, plan)
    theirs3 = swapped(theirs3)
    i3, j3 = both_ways(i2, j2)
    i2x, j2x = swapped(i2, j2)
    out = grad_out(plan, g3 + g4, out)

    out, theirs3, plan = together(out, theirs3, plan)
    low = rounded_total(mine3[0], theirs3[0])
    s4 = one_way(low, low)
    theirs2, mine2 = terms(plan, 20, 2, grad, w, part)

    theirs2, mine2, s4, i3, j3, i2x, j2x, plan = together(
        theirs2, mine2, s4, i3, j3, i2x, j2x, plan
    )
    nothing = jnp.zeros_like(s4)
    s3, u3 = both_ways(
        rounded_total(mine3[1], theirs3[1], jnp.where(on_first, s4, nothing)),
        rounded_total(mine3[2], theirs3[2], jnp.where(on_first, nothing, s4)),
    )
    theirs2 = swapped(theirs2)
    i4 = one_way(i3, j3)
    i3x, j3x = swapped(i3, j3)
    theirs1, mine1 = terms(plan, 22, 3, grad, w, part)

    theirs1, mine1, theirs2, s3, u3, i4, i3x, plan = together(
        theirs1, mine1, theirs2, s3, u3, i4, i3x, plan
    )
    s2, u2 = both_ways(
        rounded_total(mine2[0], theirs2[0], s3), rounded_total(mine2[1], theirs2[1], u3)
    )
    theirs1 = swapped(theirs1)
    i4x = swapped(i4)
    some = f0 + blocks(1, i1, j1, i1x, j1x) + blocks(2, i2, j2, i2x, j2x)[:2]
    weight = grad_qkv(plan, some)

    weight, theirs1, s2, u2, i4x, j3x, plan = together(
        weight, theirs1, s2, u2, i4x, j3x, plan
    )
    s1, u1 = both_ways(
        rounded_total(mine1[0], theirs1[0], s2), rounded_total(mine1[1], theirs1[1], u2)
    )
    some = blocks(2, i2, j2, i2x, j2x)[2:] + blocks(3, i3, j3, i3x, j3x) + blocks(4, i4, i4x)
    weight = grad_qkv(plan, some, weight)

    weight, s1, u1 = together(weight, s1, u1)
    input_grad = rounded_total(mine1[2], theirs1[2], s1, u1)
    return input_grad, weight.transpose(1, 0, 2), out


def solution(mesh):
    placed = (
        P("runs", "gx"),
        P("runs", "gx"),
        P(None, None, "gx"),
        P("gx", None),
        P("runs", None, "gx"),
        P("runs"),
    )
    return jax.shard_map(
        functools.partial(on_device, mesh.shape["gx"]),
        mesh=mesh,
        in_specs=placed,
        out_specs=(P("runs", "gx"), P("runs", None, "gx"), P(("runs", "gx"), None)),
        check_vma=False,
    )
```

```python
import functools
import math

import jax
import jax.numpy as jnp
from jax import lax
from jax.experimental import pallas as pl
from jax.experimental.pallas import tpu as pltpu
from jax.sharding import PartitionSpec as P

HD = 128
FACTOR = 1.0 / math.sqrt(HD)
MIB = 1 << 20
NT = (((1,), (1,)), ((), ()))
TN = (((0,), (0,)), ((), ()))


def dot(a, b, dims=(((1,), (0,)), ((), ()))):
    return lax.dot_general(a, b, dims, preferred_element_type=jnp.float32)


def params(mib):
    return pltpu.CompilerParams(vmem_limit_bytes=mib * MIB)


def cost(flops, nbytes, transcendentals=0):
    flops, nbytes = flops // 4096, nbytes // 4096
    return pl.CostEstimate(flops=flops, bytes_accessed=nbytes, transcendentals=transcendentals)


def attend_kernel(row_ref, qkv_ref, attn_ref, out_ref, out_t_ref, column):
    row = row_ref[...]

    @pl.when(pl.program_id(0) == 0)
    def _():
        column[...] = jnp.broadcast_to(row, (HD, row.shape[1])).T

    scores = dot(qkv_ref[0], qkv_ref[1], NT) * FACTOR
    scores = jnp.where(row <= column[:, :1], scores, -1e30)
    expd = jnp.exp(scores - jnp.max(scores, axis=1, keepdims=True))
    attn = (expd / jnp.sum(expd, axis=1, keepdims=True)).astype(jnp.bfloat16)
    attn_ref[0] = attn
    attended = dot(attn, qkv_ref[2])
    out_ref[...] = attended.astype(jnp.bfloat16)
    out_t_ref[...] = attended.T.astype(jnp.bfloat16)


def attend(positions, qkv):
    _, seq, columns = qkv.shape
    heads = columns // HD
    return pl.pallas_call(
        attend_kernel,
        grid=(heads,),
        in_specs=[
            pl.BlockSpec((1, seq), lambda h: (0, 0)),
            pl.BlockSpec((3, seq, HD), lambda h: (0, 0, h)),
        ],
        out_specs=[
            pl.BlockSpec((1, seq, seq), lambda h: (h, 0, 0)),
            pl.BlockSpec((seq, HD), lambda h: (0, h)),
            pl.BlockSpec((HD, seq), lambda h: (h, 0)),
        ],
        out_shape=[
            jax.ShapeDtypeStruct((heads, seq, seq), jnp.bfloat16),
            jax.ShapeDtypeStruct((seq, columns), jnp.bfloat16),
            jax.ShapeDtypeStruct((columns, seq), jnp.bfloat16),
        ],
        scratch_shapes=[pltpu.VMEM((seq, HD), jnp.int32)],
        compiler_params=params(60),
        cost_estimate=cost(4 * seq * seq * columns, 5 * MIB, heads * seq * seq),
    )(positions[None, :], qkv)


def attend_back_kernel(qkv_ref, attn_ref, attended_ref, grad_ref, out_ref):
    grad = grad_ref[...]
    attn = attn_ref[0]
    row_dot = jnp.sum(
        grad.astype(jnp.float32) * attended_ref[...].astype(jnp.float32), axis=1, keepdims=True
    )
    grad_attn = dot(grad, qkv_ref[2], NT)
    grad_scores = (attn.astype(jnp.float32) * (grad_attn - row_dot) * FACTOR).astype(jnp.bfloat16)
    out_ref[0] = dot(grad_scores, qkv_ref[1]).astype(jnp.bfloat16)
    out_ref[1] = dot(grad_scores, qkv_ref[0], TN).astype(jnp.bfloat16)
    out_ref[2] = dot(attn, grad, TN).astype(jnp.bfloat16)


def attend_back(qkv, attn, attended, grad):
    _, seq, columns = qkv.shape
    planes = pl.BlockSpec((3, seq, HD), lambda h: (0, 0, h))
    one = pl.BlockSpec((seq, HD), lambda h: (0, h))
    return pl.pallas_call(
        attend_back_kernel,
        grid=(columns // HD,),
        in_specs=[planes, pl.BlockSpec((1, seq, seq), lambda h: (h, 0, 0)), one, one],
        out_specs=planes,
        out_shape=jax.ShapeDtypeStruct(qkv.shape, jnp.bfloat16),
        compiler_params=params(24),
        cost_estimate=cost(8 * seq * seq * columns, 6 * MIB),
    )(qkv, attn, attended, grad)


def grad_heads_kernel(count, first, last, plan_ref, *refs):
    blocks, weights, rest = refs[:count], refs[count : 2 * count], refs[2 * count :]
    out_ref, total = rest[-2:]
    for i, (block, weight) in enumerate(zip(blocks, weights)):
        term = dot(block[...], weight[...], NT)
        if i:
            total[...] += term
        else:
            total[...] = term if first else rest[0][...] + term
    out_ref[...] = total[...].astype(jnp.bfloat16) if last else total[...]


def grad_heads(plan, w_out, blocks, total=None, last=False):
    columns = w_out.shape[0]
    seq, part = blocks[0][1].shape
    count = len(blocks)

    def weight(place):
        return pl.BlockSpec((columns, part), lambda step, plan: (0, plan[place]))

    def whole(shape):
        return pl.BlockSpec(shape, lambda step, plan: (0, 0))

    first = total is None
    return pl.pallas_call(
        functools.partial(grad_heads_kernel, count, first, last),
        grid_spec=pltpu.PrefetchScalarGridSpec(
            num_scalar_prefetch=1,
            grid=(1,),
            in_specs=[whole((seq, part))] * count
            + [weight(place) for place, _ in blocks]
            + [whole((seq, columns))] * (not first),
            out_specs=whole((seq, columns)),
            scratch_shapes=[pltpu.VMEM((seq, columns), jnp.float32)],
        ),
        out_shape=jax.ShapeDtypeStruct((seq, columns), jnp.bfloat16 if last else jnp.float32),
        compiler_params=params(40),
        cost_estimate=cost(2 * seq * columns * part * count, MIB * count),
    )(plan, *[block for _, block in blocks], *[w_out] * count, *([] if first else [total]))


SLOTS = 4


def weight_kernel(places, turn, plan_ref, left_ref, *refs):
    out_ref, held, sems = refs[-3:]
    copies = []
    for i, (place, block) in enumerate(zip(places, refs)):
        width = block.shape[1]
        slot = i % SLOTS
        if i >= SLOTS:
            copies[i - SLOTS].wait()
        if turn:
            turned = block[...].T
            for k in range(3):
                held[slot, k] = dot(turned, left_ref[k]).astype(jnp.bfloat16)
        else:
            held[slot] = dot(left_ref[...], block[...]).astype(jnp.bfloat16)
        start = pl.multiple_of(plan_ref[place] * width, 128)
        copy = pltpu.make_async_copy(
            held.at[slot], out_ref.at[:, pl.ds(start, width)], sems.at[slot]
        )
        copy.start()
        copies.append(copy)
    for copy in copies[-SLOTS:]:
        copy.wait()


def weight_grad(plan, left, blocks, shape, into=None):
    turn = left.ndim == 3
    seq, part = blocks[0][1].shape
    count = len(blocks)
    held = (3, part, left.shape[2]) if turn else (left.shape[0], part)
    vmem = pl.BlockSpec(memory_space=pltpu.VMEM)
    rest = pl.BlockSpec(memory_space=pl.ANY)
    size = math.prod(held) * count
    return pl.pallas_call(
        functools.partial(weight_kernel, [place for place, _ in blocks], turn),
        in_specs=[pl.BlockSpec(memory_space=pltpu.SMEM)]
        + [vmem] * (1 + count)
        + [rest] * (into is not None),
        out_specs=rest,
        out_shape=jax.ShapeDtypeStruct(shape, jnp.bfloat16),
        scratch_shapes=[
            pltpu.VMEM((SLOTS, *held), jnp.bfloat16),
            pltpu.SemaphoreType.DMA((SLOTS,)),
        ],
        input_output_aliases={} if into is None else {2 + count: 0},
        compiler_params=params(40),
        cost_estimate=cost(2 * seq * size, 3 * size),
    )(plan, left, *[block for _, block in blocks], *([] if into is None else [into]))


def terms_kernel(plan_ref, grad_ref, w_ref, theirs_ref, mine_ref):
    total = dot(grad_ref[0], w_ref[0], NT)
    total += dot(grad_ref[1], w_ref[1], NT)
    total += dot(grad_ref[2], w_ref[2], NT)
    total = total.astype(jnp.bfloat16)
    part = total.shape[1] // 2

    @pl.when(plan_ref[0] == 0)
    def _():
        mine_ref[0] = total[:, :part]
        theirs_ref[0] = total[:, part:]

    @pl.when(plan_ref[0] == 1)
    def _():
        mine_ref[0] = total[:, part:]
        theirs_ref[0] = total[:, :part]


def terms(plan, place, count, grad, w, part):
    _, seq, columns = grad.shape
    out = pl.BlockSpec((1, seq, part), lambda i, plan: (i, 0, 0))
    shape = jax.ShapeDtypeStruct((count, seq, part), jnp.bfloat16)
    return pl.pallas_call(
        terms_kernel,
        grid_spec=pltpu.PrefetchScalarGridSpec(
            num_scalar_prefetch=1,
            grid=(count,),
            in_specs=[
                pl.BlockSpec((3, seq, columns), lambda i, plan: (0, 0, 0)),
                pl.BlockSpec((3, 2 * part, columns), lambda i, plan: (0, plan[place + i], 0)),
            ],
            out_specs=[out, out],
        ),
        out_shape=[shape, shape],
        compiler_params=params(48),
        cost_estimate=cost(12 * seq * columns * part * count, 5 * MIB * count),
    )(plan, grad, w)


def plain(n, inputs, out_grad, w_qkv, w_out, saved_qkv, positions):
    full_in = lax.all_gather(inputs, "gx", axis=1, tiled=True)
    full_grad = lax.all_gather(out_grad, "gx", axis=1, tiled=True)
    qkv = saved_qkv.transpose(1, 0, 2)
    attn, attended, _ = attend(positions, qkv)
    grad_h = dot(full_grad, w_out, NT).astype(jnp.bfloat16)
    grad_w_out = dot(attended, full_grad, TN).astype(jnp.bfloat16)
    grad = attend_back(qkv, attn, attended, grad_h)
    grad_w_qkv = jnp.stack([dot(full_in, grad[k], TN).astype(jnp.bfloat16) for k in range(3)], 1)
    partial = sum(dot(grad[k], w_qkv[:, k], NT) for k in range(3))
    input_grad = lax.psum_scatter(partial, "gx", scatter_dimension=1, tiled=True)
    return input_grad.astype(jnp.bfloat16), grad_w_qkv, grad_w_out


def ring_order(chips):
    if chips == 8:
        return [0, 2, 4, 6, 7, 5, 3, 1]
    return list(range(chips))


def plan_of(order, device):
    chips = len(order)
    at = order.index(device // 2)
    core = device % 2

    def chip(offset):
        return order[(at + offset) % chips]

    blocks = [2 * chip(0) + core, 2 * chip(0) + 1 - core]
    for step in range(1, chips // 2):
        for shard in (core, 1 - core):
            blocks += [2 * chip(-step) + shard, 2 * chip(step) + shard]
    blocks += [2 * chip(chips // 2) + core, 2 * chip(chips // 2) + 1 - core]
    summed = [chip(chips // 2)]
    for step in range(chips // 2 - 1, 0, -1):
        summed += [chip(step), chip(-step)]
    apart = blocks[:2]
    for step in range(1, chips // 2):
        behind = step if core else -step
        for shard, first in ((core, behind), (1 - core, -behind)):
            apart += [2 * chip(first) + shard, 2 * chip(-first) + shard]
    return [core] + blocks + summed + [chip(0)] + apart + blocks[-2:]


def after(x, *others):
    return lax.optimization_barrier((x, *others))[0]


def together(*arrays):
    return lax.optimization_barrier(arrays)


def f32(x):
    return x.astype(jnp.float32)


def on_device(n, inputs, out_grad, w_qkv, w_out, saved_qkv, positions):
    part = inputs.shape[1]
    if part % 128 or n != 16:
        return plain(n, inputs, out_grad, w_qkv, w_out, saved_qkv, positions)
    order = ring_order(n // 2)
    hops = [(2 * order[i - 1], 2 * order[i]) for i in range(n // 2)]
    ahead = [(i + core, j + core) for i, j in hops for core in range(2)]
    back = [(j, i) for i, j in ahead]
    apart = [(i, j) for i, j in hops] + [(j + 1, i + 1) for i, j in hops]
    crossed = [(j, i) for i, j in apart]
    swap = [(i, i ^ 1) for i in range(n)]
    plans = [plan_of(order, i) for i in range(n)]
    size = len(plans[0])
    plan = lax.dynamic_slice(
        jnp.array(sum(plans, []), jnp.int32), (lax.axis_index("gx") * size,), (size,)
    )
    on_first = lax.axis_index("gx") % 2 == 0

    def both_ways(right, left):
        return lax.ppermute(right, "gx", ahead), lax.ppermute(left, "gx", back)

    def one_way(right, left):
        return lax.ppermute(jnp.where(on_first, right, left), "gx", apart)

    def first_chain(x):
        return lax.ppermute(x, "gx", apart)

    def second_chain(x):
        return lax.ppermute(x, "gx", crossed)

    def swapped(*arrays):
        found = [lax.ppermute(x, "gx", swap) for x in arrays]
        return found if len(found) > 1 else found[0]

    def blocks(step, *arrays):
        first = 1 if step == 0 else 4 * step - 1
        return [(first + i, array) for i, array in enumerate(arrays)]

    def in_blocks(step, *arrays):
        return [(place + 24, array) for place, array in blocks(step, *arrays)]

    def grad_qkv(index, some, into=None):
        return weight_grad(index, grad, some, w.shape, into)

    def total(*values):
        return sum(f32(value) for value in values[1:]) + f32(values[0])

    def rounded_total(*values):
        return total(*values).astype(jnp.bfloat16)

    qkv = saved_qkv.transpose(1, 0, 2)
    w = w_qkv.transpose(1, 0, 2)

    def grad_out_heads(index, some, so_far=None, last=False):
        return grad_heads(index, w_out, some, so_far, last)

    def grad_out(index, some, into=None):
        return weight_grad(index, attended_t, some, w_out.shape, into)

    r1, l1 = both_ways(out_grad, out_grad)
    other = swapped(out_grad)
    attn, attended, attended_t = attend(positions, qkv)

    r1, l1, attended, plan = together(r1, l1, attended, plan)
    r2, l2 = both_ways(r1, l1)
    g1 = blocks(1, r1, l1, *swapped(r1, l1))
    g0 = blocks(0, out_grad, other)
    grad_h = grad_out_heads(plan, g0)
    out = grad_out(plan, g0)

    r2, l2, grad_h, out, plan = together(r2, l2, grad_h, out, plan)
    r3, l3 = both_ways(r2, l2)
    g2 = blocks(2, r2, l2, *swapped(r2, l2))
    grad_h = grad_out_heads(plan, g1, grad_h)
    out = grad_out(plan, g1, out)

    r3, l3, grad_h, out, plan = together(r3, l3, grad_h, out, plan)
    x4 = one_way(r3, l3)
    i1 = first_chain(after(inputs, r3))
    r3x, l3x = swapped(r3, l3)
    g3 = blocks(3, r3, l3, r3x, l3x)
    grad_h = grad_out_heads(plan, g2, grad_h)

    grad_h, r3x, l3x, plan = together(grad_h, r3x, l3x, plan)
    out = grad_out(plan, g2, out)
    grad_h = grad_out_heads(plan, g3, grad_h)

    x4, i1, grad_h, out, plan = together(x4, i1, grad_h, out, plan)
    x4x, other = swapped(x4, inputs)
    i2, j1 = first_chain(i1), second_chain(inputs)
    f0 = in_blocks(0, inputs, other)
    g4 = blocks(4, x4, x4x)
    grad_h = grad_out_heads(plan, g4, grad_h, last=True)
    grad = attend_back(qkv, attn, attended, grad_h)

    grad, i2, j1, other, plan = together(grad, i2, j1, other, plan)
    i3, j2 = first_chain(i2), second_chain(j1)
    i1x, j1x = swapped(i1, j1)
    theirs3, mine3 = terms(plan, 17, 3, grad, w, part)

    theirs3, mine3, i3, j2, i1x, j1x, plan = together(theirs3, mine3, i3, j2, i1x, j1x, plan)
    theirs3 = swapped(theirs3)
    i4, j3 = first_chain(i3), second_chain(j2)
    i2x, j2x = swapped(i2, j2)
    out = grad_out(plan, g3 + g4, out)

    out, theirs3, plan = together(out, theirs3, plan)
    low = rounded_total(mine3[0], theirs3[0])
    s4 = first_chain(low)
    theirs2, mine2 = terms(plan, 20, 2, grad, w, part)

    theirs2, mine2, s4, i4, j3, i2x, j2x, plan = together(
        theirs2, mine2, s4, i4, j3, i2x, j2x, plan
    )
    nothing = jnp.zeros_like(s4)
    s3, u3 = both_ways(
        rounded_total(mine3[1], theirs3[1], jnp.where(on_first, s4, nothing)),
        rounded_total(mine3[2], theirs3[2], jnp.where(on_first, nothing, s4)),
    )
    theirs2, i3x = swapped(theirs2, i3)
    theirs1, mine1 = terms(plan, 22, 3, grad, w, part)

    theirs1, mine1, theirs2, s3, u3, i3x, plan = together(
        theirs1, mine1, theirs2, s3, u3, i3x, plan
    )
    s2, u2 = both_ways(
        rounded_total(mine2[0], theirs2[0], s3), rounded_total(mine2[1], theirs2[1], u3)
    )
    theirs1, i4x, j3x = swapped(theirs1, i4, j3)
    some = f0 + in_blocks(1, i1, j1, i1x, j1x) + in_blocks(2, i2, j2, i2x, j2x)[:2]
    weight = grad_qkv(plan, some)

    weight, theirs1, s2, u2, i4x, j3x, plan = together(weight, theirs1, s2, u2, i4x, j3x, plan)
    s1, u1 = both_ways(
        rounded_total(mine1[0], theirs1[0], s2), rounded_total(mine1[1], theirs1[1], u2)
    )
    some = in_blocks(2, i2, j2, i2x, j2x)[2:]
    some += in_blocks(3, i3, j3, i3x, j3x) + in_blocks(4, i4, i4x)
    weight = grad_qkv(plan, some, weight)

    weight, s1, u1 = together(weight, s1, u1)
    input_grad = rounded_total(mine1[2], theirs1[2], s1, u1)
    return input_grad, weight.transpose(1, 0, 2), out


def solution(mesh):
    placed = (
        P("runs", "gx"),
        P("runs", "gx"),
        P(None, None, "gx"),
        P("gx", None),
        P("runs", None, "gx"),
        P("runs"),
    )
    return jax.shard_map(
        functools.partial(on_device, mesh.shape["gx"]),
        mesh=mesh,
        in_specs=placed,
        out_specs=(P("runs", "gx"), P("runs", None, "gx"), P(("runs", "gx"), None)),
        check_vma=False,
    )
```

```python
import functools
import math

import jax
import jax.numpy as jnp
from jax import lax
from jax.experimental import pallas as pl
from jax.experimental.pallas import tpu as pltpu
from jax.sharding import PartitionSpec as P

HD = 128
FACTOR = 1.0 / math.sqrt(HD)
MIB = 1 << 20
NT = (((1,), (1,)), ((), ()))
TN = (((0,), (0,)), ((), ()))


def dot(a, b, dims=(((1,), (0,)), ((), ()))):
    return lax.dot_general(a, b, dims, preferred_element_type=jnp.float32)


def params(mib):
    return pltpu.CompilerParams(vmem_limit_bytes=mib * MIB)


def cost(flops, nbytes, transcendentals=0):
    flops, nbytes = flops // 4096, nbytes // 4096
    return pl.CostEstimate(flops=flops, bytes_accessed=nbytes, transcendentals=transcendentals)


def attend_kernel(row_ref, qkv_ref, attn_ref, out_ref, out_t_ref, column):
    row = row_ref[...]

    @pl.when(pl.program_id(0) == 0)
    def _():
        column[...] = jnp.broadcast_to(row, (HD, row.shape[1])).T

    scores = dot(qkv_ref[0], qkv_ref[1], NT) * FACTOR
    scores = jnp.where(row <= column[:, :1], scores, -1e30)
    expd = jnp.exp(scores - jnp.max(scores, axis=1, keepdims=True))
    attn = (expd / jnp.sum(expd, axis=1, keepdims=True)).astype(jnp.bfloat16)
    attn_ref[0] = attn
    attended = dot(attn, qkv_ref[2])
    out_ref[...] = attended.astype(jnp.bfloat16)
    out_t_ref[...] = attended.T.astype(jnp.bfloat16)


def attend(positions, qkv):
    _, seq, columns = qkv.shape
    heads = columns // HD
    return pl.pallas_call(
        attend_kernel,
        grid=(heads,),
        in_specs=[
            pl.BlockSpec((1, seq), lambda h: (0, 0)),
            pl.BlockSpec((3, seq, HD), lambda h: (0, 0, h)),
        ],
        out_specs=[
            pl.BlockSpec((1, seq, seq), lambda h: (h, 0, 0)),
            pl.BlockSpec((seq, HD), lambda h: (0, h)),
            pl.BlockSpec((HD, seq), lambda h: (h, 0)),
        ],
        out_shape=[
            jax.ShapeDtypeStruct((heads, seq, seq), jnp.bfloat16),
            jax.ShapeDtypeStruct((seq, columns), jnp.bfloat16),
            jax.ShapeDtypeStruct((columns, seq), jnp.bfloat16),
        ],
        scratch_shapes=[pltpu.VMEM((seq, HD), jnp.int32)],
        compiler_params=params(60),
        cost_estimate=cost(4 * seq * seq * columns, 5 * MIB, heads * seq * seq),
    )(positions[None, :], qkv)


def attend_back_kernel(qkv_ref, attn_ref, attended_ref, grad_ref, out_ref):
    grad = grad_ref[...]
    attn = attn_ref[0]
    row_dot = jnp.sum(
        grad.astype(jnp.float32) * attended_ref[...].astype(jnp.float32), axis=1, keepdims=True
    )
    grad_attn = dot(grad, qkv_ref[2], NT)
    grad_scores = (attn.astype(jnp.float32) * (grad_attn - row_dot) * FACTOR).astype(jnp.bfloat16)
    out_ref[0] = dot(grad_scores, qkv_ref[1]).astype(jnp.bfloat16)
    out_ref[1] = dot(grad_scores, qkv_ref[0], TN).astype(jnp.bfloat16)
    out_ref[2] = dot(attn, grad, TN).astype(jnp.bfloat16)


def attend_back(qkv, attn, attended, grad):
    _, seq, columns = qkv.shape
    planes = pl.BlockSpec((3, seq, HD), lambda h: (0, 0, h))
    one = pl.BlockSpec((seq, HD), lambda h: (0, h))
    return pl.pallas_call(
        attend_back_kernel,
        grid=(columns // HD,),
        in_specs=[planes, pl.BlockSpec((1, seq, seq), lambda h: (h, 0, 0)), one, one],
        out_specs=planes,
        out_shape=jax.ShapeDtypeStruct(qkv.shape, jnp.bfloat16),
        compiler_params=params(24),
        cost_estimate=cost(8 * seq * seq * columns, 6 * MIB),
    )(qkv, attn, attended, grad)


def grad_heads_kernel(count, first, last, plan_ref, *refs):
    blocks, weights, rest = refs[:count], refs[count : 2 * count], refs[2 * count :]
    out_ref, total = rest[-2:]
    for i, (block, weight) in enumerate(zip(blocks, weights)):
        term = dot(block[...], weight[...], NT)
        if i:
            total[...] += term
        else:
            total[...] = term if first else rest[0][...] + term
    out_ref[...] = total[...].astype(jnp.bfloat16) if last else total[...]


def grad_heads(plan, w_out, blocks, total=None, last=False):
    columns = w_out.shape[0]
    seq, part = blocks[0][1].shape
    count = len(blocks)

    def weight(place):
        return pl.BlockSpec((columns, part), lambda step, plan: (0, plan[place]))

    def whole(shape):
        return pl.BlockSpec(shape, lambda step, plan: (0, 0))

    first = total is None
    return pl.pallas_call(
        functools.partial(grad_heads_kernel, count, first, last),
        grid_spec=pltpu.PrefetchScalarGridSpec(
            num_scalar_prefetch=1,
            grid=(1,),
            in_specs=[whole((seq, part))] * count
            + [weight(place) for place, _ in blocks]
            + [whole((seq, columns))] * (not first),
            out_specs=whole((seq, columns)),
            scratch_shapes=[pltpu.VMEM((seq, columns), jnp.float32)],
        ),
        out_shape=jax.ShapeDtypeStruct((seq, columns), jnp.bfloat16 if last else jnp.float32),
        compiler_params=params(48),
        cost_estimate=cost(2 * seq * columns * part * count, MIB * count),
    )(plan, *[block for _, block in blocks], *[w_out] * count, *([] if first else [total]))


def weight_out_kernel(places, plan_ref, left_ref, *refs):
    out_ref, held, sems = refs[-3:]
    for i in range(len(places)):
        held[i] = dot(left_ref[...], refs[i][...]).astype(jnp.bfloat16)
    width = held.shape[2]
    copies = []
    for i, place in enumerate(places):
        start = pl.multiple_of(plan_ref[place] * width, 128)
        copies.append(
            pltpu.make_async_copy(held.at[i], out_ref.at[:, pl.ds(start, width)], sems.at[i])
        )
        copies[i].start()
    for copy in copies:
        copy.wait()


def weight_out(plan, left, blocks, shape, into=None):
    seq, part = blocks[0][1].shape
    count = len(blocks)
    vmem = pl.BlockSpec(memory_space=pltpu.VMEM)
    rest = pl.BlockSpec(memory_space=pl.ANY)
    size = left.shape[0] * part * count
    return pl.pallas_call(
        functools.partial(weight_out_kernel, [place for place, _ in blocks]),
        in_specs=[pl.BlockSpec(memory_space=pltpu.SMEM)]
        + [vmem] * (1 + count)
        + [rest] * (into is not None),
        out_specs=rest,
        out_shape=jax.ShapeDtypeStruct(shape, jnp.bfloat16),
        scratch_shapes=[
            pltpu.VMEM((count, left.shape[0], part), jnp.bfloat16),
            pltpu.SemaphoreType.DMA((count,)),
        ],
        input_output_aliases={} if into is None else {2 + count: 0},
        compiler_params=params(40),
        cost_estimate=cost(2 * seq * size, 3 * size),
    )(plan, left, *[block for _, block in blocks], *([] if into is None else [into]))


def weight_qkv_kernel(grad_ref, block_ref, *refs):
    turned = block_ref[...].T
    for k in range(3):
        refs[-1][k] = dot(turned, grad_ref[k]).astype(jnp.bfloat16)


def weight_qkv(grad, full_in, width, first, count, into=None):
    _, seq, columns = grad.shape
    features = full_in.shape[1]
    given = [] if into is None else [into]
    return pl.pallas_call(
        weight_qkv_kernel,
        grid=(count,),
        in_specs=[
            pl.BlockSpec((3, seq, columns), lambda i: (0, 0, 0)),
            pl.BlockSpec((seq, width), lambda i: (0, first + i)),
        ]
        + [pl.BlockSpec(memory_space=pl.ANY)] * len(given),
        out_specs=pl.BlockSpec((3, width, columns), lambda i: (0, first + i, 0)),
        out_shape=jax.ShapeDtypeStruct((3, features, columns), jnp.bfloat16),
        input_output_aliases={2: 0} if given else {},
        compiler_params=params(56),
        cost_estimate=cost(6 * seq * columns * width * count, 5 * MIB * count),
    )(grad, full_in, *given)


def terms_kernel(plan_ref, grad_ref, w_ref, theirs_ref, mine_ref):
    total = dot(grad_ref[0], w_ref[0], NT)
    total += dot(grad_ref[1], w_ref[1], NT)
    total += dot(grad_ref[2], w_ref[2], NT)
    total = total.astype(jnp.bfloat16)
    part = total.shape[1] // 2

    @pl.when(plan_ref[0] == 0)
    def _():
        mine_ref[0] = total[:, :part]
        theirs_ref[0] = total[:, part:]

    @pl.when(plan_ref[0] == 1)
    def _():
        mine_ref[0] = total[:, part:]
        theirs_ref[0] = total[:, :part]


def terms(plan, place, count, grad, w, part):
    _, seq, columns = grad.shape
    out = pl.BlockSpec((1, seq, part), lambda i, plan: (i, 0, 0))
    shape = jax.ShapeDtypeStruct((count, seq, part), jnp.bfloat16)
    return pl.pallas_call(
        terms_kernel,
        grid_spec=pltpu.PrefetchScalarGridSpec(
            num_scalar_prefetch=1,
            grid=(count,),
            in_specs=[
                pl.BlockSpec((3, seq, columns), lambda i, plan: (0, 0, 0)),
                pl.BlockSpec((3, 2 * part, columns), lambda i, plan: (0, plan[place + i], 0)),
            ],
            out_specs=[out, out],
        ),
        out_shape=[shape, shape],
        compiler_params=params(48),
        cost_estimate=cost(12 * seq * columns * part * count, 5 * MIB * count),
    )(plan, grad, w)


def plain(n, inputs, out_grad, w_qkv, w_out, saved_qkv, positions):
    full_in = lax.all_gather(inputs, "gx", axis=1, tiled=True)
    full_grad = lax.all_gather(out_grad, "gx", axis=1, tiled=True)
    qkv = saved_qkv.transpose(1, 0, 2)
    attn, attended, _ = attend(positions, qkv)
    grad_h = dot(full_grad, w_out, NT).astype(jnp.bfloat16)
    grad_w_out = dot(attended, full_grad, TN).astype(jnp.bfloat16)
    grad = attend_back(qkv, attn, attended, grad_h)
    grad_w_qkv = jnp.stack([dot(full_in, grad[k], TN).astype(jnp.bfloat16) for k in range(3)], 1)
    partial = sum(dot(grad[k], w_qkv[:, k], NT) for k in range(3))
    input_grad = lax.psum_scatter(partial, "gx", scatter_dimension=1, tiled=True)
    return input_grad.astype(jnp.bfloat16), grad_w_qkv, grad_w_out


def ring_order(chips):
    if chips == 8:
        return [0, 2, 4, 6, 7, 5, 3, 1]
    return list(range(chips))


def plan_of(order, device):
    chips = len(order)
    at = order.index(device // 2)
    core = device % 2

    def chip(offset):
        return order[(at + offset) % chips]

    blocks = [2 * chip(0) + core, 2 * chip(0) + 1 - core]
    for step in range(1, chips // 2):
        for shard in (core, 1 - core):
            blocks += [2 * chip(-step) + shard, 2 * chip(step) + shard]
    blocks += [2 * chip(chips // 2) + core, 2 * chip(chips // 2) + 1 - core]
    summed = [chip(chips // 2)]
    for step in range(chips // 2 - 1, 0, -1):
        summed += [chip(step), chip(-step)]
    return [core] + blocks + summed + [chip(0)]


def after(x, *others):
    return lax.optimization_barrier((x, *others))[0]


def together(*arrays):
    return lax.optimization_barrier(arrays)


def f32(x):
    return x.astype(jnp.float32)


def on_device(n, inputs, out_grad, w_qkv, w_out, saved_qkv, positions):
    part = inputs.shape[1]
    if part % 128 or n != 16:
        return plain(n, inputs, out_grad, w_qkv, w_out, saved_qkv, positions)
    order = ring_order(n // 2)
    hops = [(2 * order[i - 1], 2 * order[i]) for i in range(n // 2)]
    ahead = [(i + core, j + core) for i, j in hops for core in range(2)]
    back = [(j, i) for i, j in ahead]
    apart = [(i, j) for i, j in hops] + [(j + 1, i + 1) for i, j in hops]
    swap = [(i, i ^ 1) for i in range(n)]
    plans = [plan_of(order, i) for i in range(n)]
    size = len(plans[0])
    plan = lax.dynamic_slice(
        jnp.array(sum(plans, []), jnp.int32), (lax.axis_index("gx") * size,), (size,)
    )
    on_first = lax.axis_index("gx") % 2 == 0

    def both_ways(right, left):
        return lax.ppermute(right, "gx", ahead), lax.ppermute(left, "gx", back)

    def one_way(right, left):
        return lax.ppermute(jnp.where(on_first, right, left), "gx", apart)

    def both_apart(x):
        return lax.ppermute(x, "gx", apart)

    def swapped(*arrays):
        found = [lax.ppermute(x, "gx", swap) for x in arrays]
        return found if len(found) > 1 else found[0]

    def blocks(step, *arrays):
        first = 1 if step == 0 else 4 * step - 1
        return [(first + i, array) for i, array in enumerate(arrays)]

    def total(*values):
        return sum(f32(value) for value in values[1:]) + f32(values[0])

    def rounded_total(*values):
        return total(*values).astype(jnp.bfloat16)

    qkv = saved_qkv.transpose(1, 0, 2)
    w = w_qkv.transpose(1, 0, 2)

    def grad_out_heads(index, some, so_far=None, last=False):
        return grad_heads(index, w_out, some, so_far, last)

    def grad_out(index, some, into=None):
        return weight_out(index, attended_t, some, w_out.shape, into)

    r1, l1 = both_ways(out_grad, out_grad)
    other = swapped(out_grad)
    attn, attended, attended_t = attend(positions, qkv)

    r1, l1, attended, inputs, plan = together(r1, l1, attended, inputs, plan)
    r2, l2 = both_ways(r1, l1)
    full_in = lax.all_gather(inputs, "gx", axis=1, tiled=True)
    g1 = blocks(1, r1, l1, *swapped(r1, l1))
    g0 = blocks(0, out_grad, other)
    grad_h = grad_out_heads(plan, g0)
    out = grad_out(plan, g0)

    r2, l2, grad_h, out, plan = together(r2, l2, grad_h, out, plan)
    r3, l3 = both_ways(r2, l2)
    g2 = blocks(2, r2, l2, *swapped(r2, l2))
    grad_h = grad_out_heads(plan, g1, grad_h)
    out = grad_out(plan, g1, out)

    r3, l3, grad_h, out, plan = together(r3, l3, grad_h, out, plan)
    x4 = one_way(r3, l3)
    r3x, l3x = swapped(r3, l3)
    g3 = blocks(3, r3, l3, r3x, l3x)
    grad_h = grad_out_heads(plan, g2, grad_h)

    grad_h, r3x, l3x, plan = together(grad_h, r3x, l3x, plan)
    grad_h = grad_out_heads(plan, g3, grad_h)

    x4, grad_h, plan = together(x4, grad_h, plan)
    x4x = swapped(x4)
    out = grad_out(plan, g2, out)

    x4x, out, plan = together(x4x, out, plan)
    g4 = blocks(4, x4, x4x)
    grad_h = grad_out_heads(plan, g4, grad_h, last=True)
    grad = attend_back(qkv, attn, attended, grad_h)

    theirs3, mine3 = terms(plan, 17, 3, grad, w, part)

    theirs3, mine3, plan = together(theirs3, mine3, plan)
    theirs3 = swapped(theirs3)
    out = grad_out(plan, g3 + g4, out)

    out, theirs3, plan = together(out, theirs3, plan)
    s4 = both_apart(rounded_total(mine3[0], theirs3[0]))
    theirs2, mine2 = terms(plan, 20, 2, grad, w, part)

    theirs2, mine2, s4, plan = together(theirs2, mine2, s4, plan)
    nothing = jnp.zeros_like(s4)
    s3, u3 = both_ways(
        rounded_total(mine3[1], theirs3[1], jnp.where(on_first, s4, nothing)),
        rounded_total(mine3[2], theirs3[2], jnp.where(on_first, nothing, s4)),
    )
    theirs2 = swapped(theirs2)
    theirs1, mine1 = terms(plan, 22, 3, grad, w, part)

    theirs1, mine1, theirs2, s3, u3, full_in, plan = together(
        theirs1, mine1, theirs2, s3, u3, full_in, plan
    )
    s2, u2 = both_ways(
        rounded_total(mine2[0], theirs2[0], s3), rounded_total(mine2[1], theirs2[1], u3)
    )
    theirs1 = swapped(theirs1)
    half = n // 4
    weight = weight_qkv(grad, full_in, 2 * part, 0, half)

    weight, theirs1, s2, u2 = together(weight, theirs1, s2, u2)
    s1, u1 = both_ways(
        rounded_total(mine1[0], theirs1[0], s2), rounded_total(mine1[1], theirs1[1], u2)
    )
    weight = weight_qkv(grad, full_in, 2 * part, half, half, weight)

    weight, s1, u1 = together(weight, s1, u1)
    input_grad = rounded_total(mine1[2], theirs1[2], s1, u1)
    return input_grad, weight.transpose(1, 0, 2), out


def solution(mesh):
    placed = (
        P("runs", "gx"),
        P("runs", "gx"),
        P(None, None, "gx"),
        P("gx", None),
        P("runs", None, "gx"),
        P("runs"),
    )
    return jax.shard_map(
        functools.partial(on_device, mesh.shape["gx"]),
        mesh=mesh,
        in_specs=placed,
        out_specs=(P("runs", "gx"), P("runs", None, "gx"), P(("runs", "gx"), None)),
        check_vma=False,
    )
```

```python
import functools
import math

import jax
import jax.numpy as jnp
from jax import lax
from jax.experimental import pallas as pl
from jax.experimental.pallas import tpu as pltpu
from jax.sharding import PartitionSpec as P

HD = 128
FACTOR = 1.0 / math.sqrt(HD)
MIB = 1 << 20
NT = (((1,), (1,)), ((), ()))
TN = (((0,), (0,)), ((), ()))


def dot(a, b, dims=(((1,), (0,)), ((), ()))):
    return lax.dot_general(a, b, dims, preferred_element_type=jnp.float32)


def params(mib):
    return pltpu.CompilerParams(vmem_limit_bytes=mib * MIB)


def cost(flops, nbytes, transcendentals=0):
    flops, nbytes = flops // 4096, nbytes // 4096
    return pl.CostEstimate(flops=flops, bytes_accessed=nbytes, transcendentals=transcendentals)


def attend_kernel(row_ref, qkv_ref, attn_ref, out_ref, out_t_ref, column):
    row = row_ref[...]

    @pl.when(pl.program_id(0) == 0)
    def _():
        column[...] = jnp.broadcast_to(row, (HD, row.shape[1])).T

    scores = dot(qkv_ref[0], qkv_ref[1], NT) * FACTOR
    scores = jnp.where(row <= column[:, :1], scores, -1e30)
    expd = jnp.exp(scores - jnp.max(scores, axis=1, keepdims=True))
    attn = (expd / jnp.sum(expd, axis=1, keepdims=True)).astype(jnp.bfloat16)
    attn_ref[0] = attn
    attended = dot(attn, qkv_ref[2])
    out_ref[...] = attended.astype(jnp.bfloat16)
    out_t_ref[...] = attended.T.astype(jnp.bfloat16)


def attend(positions, qkv):
    _, seq, columns = qkv.shape
    heads = columns // HD
    return pl.pallas_call(
        attend_kernel,
        grid=(heads,),
        in_specs=[
            pl.BlockSpec((1, seq), lambda h: (0, 0)),
            pl.BlockSpec((3, seq, HD), lambda h: (0, 0, h)),
        ],
        out_specs=[
            pl.BlockSpec((1, seq, seq), lambda h: (h, 0, 0)),
            pl.BlockSpec((seq, HD), lambda h: (0, h)),
            pl.BlockSpec((HD, seq), lambda h: (h, 0)),
        ],
        out_shape=[
            jax.ShapeDtypeStruct((heads, seq, seq), jnp.bfloat16),
            jax.ShapeDtypeStruct((seq, columns), jnp.bfloat16),
            jax.ShapeDtypeStruct((columns, seq), jnp.bfloat16),
        ],
        scratch_shapes=[pltpu.VMEM((seq, HD), jnp.int32)],
        compiler_params=params(60),
        cost_estimate=cost(4 * seq * seq * columns, 5 * MIB, heads * seq * seq),
    )(positions[None, :], qkv)


def attend_back_kernel(qkv_ref, attn_ref, attended_ref, grad_ref, out_ref):
    grad = grad_ref[...]
    attn = attn_ref[0]
    row_dot = jnp.sum(
        grad.astype(jnp.float32) * attended_ref[...].astype(jnp.float32), axis=1, keepdims=True
    )
    grad_attn = dot(grad, qkv_ref[2], NT)
    grad_scores = (attn.astype(jnp.float32) * (grad_attn - row_dot) * FACTOR).astype(jnp.bfloat16)
    out_ref[0] = dot(grad_scores, qkv_ref[1]).astype(jnp.bfloat16)
    out_ref[1] = dot(grad_scores, qkv_ref[0], TN).astype(jnp.bfloat16)
    out_ref[2] = dot(attn, grad, TN).astype(jnp.bfloat16)


def attend_back(qkv, attn, attended, grad):
    _, seq, columns = qkv.shape
    planes = pl.BlockSpec((3, seq, HD), lambda h: (0, 0, h))
    one = pl.BlockSpec((seq, HD), lambda h: (0, h))
    return pl.pallas_call(
        attend_back_kernel,
        grid=(columns // HD,),
        in_specs=[planes, pl.BlockSpec((1, seq, seq), lambda h: (h, 0, 0)), one, one],
        out_specs=planes,
        out_shape=jax.ShapeDtypeStruct(qkv.shape, jnp.bfloat16),
        compiler_params=params(24),
        cost_estimate=cost(8 * seq * seq * columns, 6 * MIB),
    )(qkv, attn, attended, grad)


def grad_heads_kernel(count, first, last, plan_ref, *refs):
    blocks, weights, rest = refs[:count], refs[count : 2 * count], refs[2 * count :]
    out_ref, total = rest[-2:]
    for i, (block, weight) in enumerate(zip(blocks, weights)):
        term = dot(block[...], weight[...], NT)
        if i:
            total[...] += term
        else:
            total[...] = term if first else rest[0][...] + term
    out_ref[...] = total[...].astype(jnp.bfloat16) if last else total[...]


def grad_heads(plan, w_out, blocks, total=None, last=False):
    columns = w_out.shape[0]
    seq, part = blocks[0][1].shape
    count = len(blocks)

    def weight(place):
        return pl.BlockSpec((columns, part), lambda step, plan: (0, plan[place]))

    def whole(shape):
        return pl.BlockSpec(shape, lambda step, plan: (0, 0))

    first = total is None
    return pl.pallas_call(
        functools.partial(grad_heads_kernel, count, first, last),
        grid_spec=pltpu.PrefetchScalarGridSpec(
            num_scalar_prefetch=1,
            grid=(1,),
            in_specs=[whole((seq, part))] * count
            + [weight(place) for place, _ in blocks]
            + [whole((seq, columns))] * (not first),
            out_specs=whole((seq, columns)),
            scratch_shapes=[pltpu.VMEM((seq, columns), jnp.float32)],
        ),
        out_shape=jax.ShapeDtypeStruct((seq, columns), jnp.bfloat16 if last else jnp.float32),
        compiler_params=params(40),
        cost_estimate=cost(2 * seq * columns * part * count, MIB * count),
    )(plan, *[block for _, block in blocks], *[w_out] * count, *([] if first else [total]))


SLOTS = 4


def weight_kernel(places, turned, plan_ref, left_ref, *refs):
    out_ref, held, sems = refs[-3:]
    copies = []
    for i, (place, block) in enumerate(zip(places, refs)):
        width = block.shape[0 if turned else 1]
        slot = i % SLOTS
        if i >= SLOTS:
            copies[i - SLOTS].wait()
        if turned:
            for k in range(3):
                held[slot, k] = dot(block[...], left_ref[k]).astype(jnp.bfloat16)
        else:
            held[slot] = dot(left_ref[...], block[...]).astype(jnp.bfloat16)
        start = pl.multiple_of(plan_ref[place] * width, 128)
        copy = pltpu.make_async_copy(
            held.at[slot], out_ref.at[:, pl.ds(start, width)], sems.at[slot]
        )
        copy.start()
        copies.append(copy)
    for copy in copies[-SLOTS:]:
        copy.wait()


def weight_grad(plan, left, blocks, shape, into=None):
    turned = left.ndim == 3
    seq, part = blocks[0][1].shape[::-1] if turned else blocks[0][1].shape
    count = len(blocks)
    held = (3, part, left.shape[2]) if turned else (left.shape[0], part)
    vmem = pl.BlockSpec(memory_space=pltpu.VMEM)
    rest = pl.BlockSpec(memory_space=pl.ANY)
    size = math.prod(held) * count
    return pl.pallas_call(
        functools.partial(weight_kernel, [place for place, _ in blocks], turned),
        in_specs=[pl.BlockSpec(memory_space=pltpu.SMEM)]
        + [vmem] * (1 + count)
        + [rest] * (into is not None),
        out_specs=rest,
        out_shape=jax.ShapeDtypeStruct(shape, jnp.bfloat16),
        scratch_shapes=[
            pltpu.VMEM((SLOTS, *held), jnp.bfloat16),
            pltpu.SemaphoreType.DMA((SLOTS,)),
        ],
        input_output_aliases={} if into is None else {2 + count: 0},
        compiler_params=params(40),
        cost_estimate=cost(2 * seq * size, 3 * size),
    )(plan, left, *[block for _, block in blocks], *([] if into is None else [into]))


def terms_kernel(plan_ref, grad_ref, w_ref, theirs_ref, mine_ref):
    total = dot(grad_ref[0], w_ref[0], NT)
    total += dot(grad_ref[1], w_ref[1], NT)
    total += dot(grad_ref[2], w_ref[2], NT)
    total = total.astype(jnp.bfloat16)
    part = total.shape[1] // 2

    @pl.when(plan_ref[0] == 0)
    def _():
        mine_ref[0] = total[:, :part]
        theirs_ref[0] = total[:, part:]

    @pl.when(plan_ref[0] == 1)
    def _():
        mine_ref[0] = total[:, part:]
        theirs_ref[0] = total[:, :part]


def terms(plan, place, count, grad, w, part):
    _, seq, columns = grad.shape
    out = pl.BlockSpec((1, seq, part), lambda i, plan: (i, 0, 0))
    shape = jax.ShapeDtypeStruct((count, seq, part), jnp.bfloat16)
    return pl.pallas_call(
        terms_kernel,
        grid_spec=pltpu.PrefetchScalarGridSpec(
            num_scalar_prefetch=1,
            grid=(count,),
            in_specs=[
                pl.BlockSpec((3, seq, columns), lambda i, plan: (0, 0, 0)),
                pl.BlockSpec((3, 2 * part, columns), lambda i, plan: (0, plan[place + i], 0)),
            ],
            out_specs=[out, out],
        ),
        out_shape=[shape, shape],
        compiler_params=params(48),
        cost_estimate=cost(12 * seq * columns * part * count, 5 * MIB * count),
    )(plan, grad, w)


def plain(n, inputs, out_grad, w_qkv, w_out, saved_qkv, positions):
    full_in = lax.all_gather(inputs, "gx", axis=1, tiled=True)
    full_grad = lax.all_gather(out_grad, "gx", axis=1, tiled=True)
    qkv = saved_qkv.transpose(1, 0, 2)
    attn, attended, _ = attend(positions, qkv)
    grad_h = dot(full_grad, w_out, NT).astype(jnp.bfloat16)
    grad_w_out = dot(attended, full_grad, TN).astype(jnp.bfloat16)
    grad = attend_back(qkv, attn, attended, grad_h)
    grad_w_qkv = jnp.stack([dot(full_in, grad[k], TN).astype(jnp.bfloat16) for k in range(3)], 1)
    partial = sum(dot(grad[k], w_qkv[:, k], NT) for k in range(3))
    input_grad = lax.psum_scatter(partial, "gx", scatter_dimension=1, tiled=True)
    return input_grad.astype(jnp.bfloat16), grad_w_qkv, grad_w_out


def ring_order(chips):
    if chips == 8:
        return [0, 2, 4, 6, 7, 5, 3, 1]
    return list(range(chips))


def plan_of(order, device):
    chips = len(order)
    at = order.index(device // 2)
    core = device % 2

    def chip(offset):
        return order[(at + offset) % chips]

    blocks = [2 * chip(0) + core, 2 * chip(0) + 1 - core]
    for step in range(1, chips // 2):
        for shard in (core, 1 - core):
            blocks += [2 * chip(-step) + shard, 2 * chip(step) + shard]
    blocks += [2 * chip(chips // 2) + core, 2 * chip(chips // 2) + 1 - core]
    summed = [chip(chips // 2)]
    for step in range(chips // 2 - 1, 0, -1):
        summed += [chip(step), chip(-step)]
    apart = blocks[:2]
    for step in range(1, chips // 2):
        behind = step if core else -step
        for shard, first in ((core, behind), (1 - core, -behind)):
            apart += [2 * chip(first) + shard, 2 * chip(-first) + shard]
    return [core] + blocks + summed + [chip(0)] + apart + blocks[-2:]


def after(x, *others):
    return lax.optimization_barrier((x, *others))[0]


def together(*arrays):
    return lax.optimization_barrier(arrays)


def f32(x):
    return x.astype(jnp.float32)


def on_device(n, inputs, out_grad, w_qkv, w_out, saved_qkv, positions):
    part = inputs.shape[1]
    if part % 128 or n != 16:
        return plain(n, inputs, out_grad, w_qkv, w_out, saved_qkv, positions)
    order = ring_order(n // 2)
    hops = [(2 * order[i - 1], 2 * order[i]) for i in range(n // 2)]
    ahead = [(i + core, j + core) for i, j in hops for core in range(2)]
    back = [(j, i) for i, j in ahead]
    apart = [(i, j) for i, j in hops] + [(j + 1, i + 1) for i, j in hops]
    crossed = [(j, i) for i, j in apart]
    swap = [(i, i ^ 1) for i in range(n)]
    plans = [plan_of(order, i) for i in range(n)]
    size = len(plans[0])
    plan = lax.dynamic_slice(
        jnp.array(sum(plans, []), jnp.int32), (lax.axis_index("gx") * size,), (size,)
    )
    on_first = lax.axis_index("gx") % 2 == 0

    def both_ways(right, left):
        return lax.ppermute(right, "gx", ahead), lax.ppermute(left, "gx", back)

    def one_way(right, left):
        return lax.ppermute(jnp.where(on_first, right, left), "gx", apart)

    def first_chain(x):
        return lax.ppermute(x, "gx", apart)

    def second_chain(x):
        return lax.ppermute(x, "gx", crossed)

    def swapped(*arrays):
        found = [lax.ppermute(x, "gx", swap) for x in arrays]
        return found if len(found) > 1 else found[0]

    def blocks(step, *arrays):
        first = 1 if step == 0 else 4 * step - 1
        return [(first + i, array) for i, array in enumerate(arrays)]

    def in_blocks(step, *arrays):
        return [(place + 24, array) for place, array in blocks(step, *arrays)]

    def grad_qkv(index, some, into=None):
        return weight_grad(index, grad, some, w.shape, into)

    def total(*values):
        return sum(f32(value) for value in values[1:]) + f32(values[0])

    def rounded_total(*values):
        return total(*values).astype(jnp.bfloat16)

    qkv = saved_qkv.transpose(1, 0, 2)
    w = w_qkv.transpose(1, 0, 2)
    inputs = inputs.T

    def grad_out_heads(index, some, so_far=None, last=False):
        return grad_heads(index, w_out, some, so_far, last)

    def grad_out(index, some, into=None):
        return weight_grad(index, attended_t, some, w_out.shape, into)

    r1, l1 = both_ways(out_grad, out_grad)
    other = swapped(out_grad)
    attn, attended, attended_t = attend(positions, qkv)

    r1, l1, attended, plan = together(r1, l1, attended, plan)
    r2, l2 = both_ways(r1, l1)
    g1 = blocks(1, r1, l1, *swapped(r1, l1))
    g0 = blocks(0, out_grad, other)
    out = grad_out(plan, g0)

    r2, l2, out, plan = together(r2, l2, out, plan)
    r3, l3 = both_ways(r2, l2)
    g2 = blocks(2, r2, l2, *swapped(r2, l2))
    grad_h = grad_out_heads(plan, g0 + g1)
    out = grad_out(plan, g1, out)

    r3, l3, grad_h, out, plan = together(r3, l3, grad_h, out, plan)
    x4 = one_way(r3, l3)
    i1 = first_chain(after(inputs, r3))
    r3x, l3x = swapped(r3, l3)
    g3 = blocks(3, r3, l3, r3x, l3x)
    grad_h = grad_out_heads(plan, g2, grad_h)

    grad_h, r3x, l3x, plan = together(grad_h, r3x, l3x, plan)
    grad_h = grad_out_heads(plan, g3, grad_h)

    x4, i1, grad_h, plan = together(x4, i1, grad_h, plan)
    x4x, other = swapped(x4, inputs)
    i2, j1 = first_chain(i1), second_chain(inputs)
    f0 = in_blocks(0, inputs, other)
    g4 = blocks(4, x4, x4x)
    grad_h = grad_out_heads(plan, g4, grad_h, last=True)
    grad = attend_back(qkv, attn, attended, grad_h)

    grad, plan = together(grad, plan)
    out = grad_out(plan, g2, out)

    out, i2, j1, other, plan = together(out, i2, j1, other, plan)
    i3, j2 = first_chain(i2), second_chain(j1)
    i1x, j1x = swapped(i1, j1)
    theirs3, mine3 = terms(plan, 17, 3, grad, w, part)

    theirs3, mine3, i3, j2, i1x, j1x, plan = together(theirs3, mine3, i3, j2, i1x, j1x, plan)
    theirs3 = swapped(theirs3)
    i4, j3 = first_chain(i3), second_chain(j2)
    i2x, j2x = swapped(i2, j2)
    out = grad_out(plan, g3 + g4, out)

    out, theirs3, plan = together(out, theirs3, plan)
    low = rounded_total(mine3[0], theirs3[0])
    s4 = first_chain(low)
    theirs2, mine2 = terms(plan, 20, 2, grad, w, part)

    theirs2, mine2, s4, i4, j3, i2x, j2x, plan = together(
        theirs2, mine2, s4, i4, j3, i2x, j2x, plan
    )
    nothing = jnp.zeros_like(s4)
    s3, u3 = both_ways(
        rounded_total(mine3[1], theirs3[1], jnp.where(on_first, s4, nothing)),
        rounded_total(mine3[2], theirs3[2], jnp.where(on_first, nothing, s4)),
    )
    theirs2, i3x = swapped(theirs2, i3)
    theirs1, mine1 = terms(plan, 22, 3, grad, w, part)

    theirs1, mine1, theirs2, s3, u3, i3x, plan = together(
        theirs1, mine1, theirs2, s3, u3, i3x, plan
    )
    s2, u2 = both_ways(
        rounded_total(mine2[0], theirs2[0], s3), rounded_total(mine2[1], theirs2[1], u3)
    )
    theirs1, i4x, j3x = swapped(theirs1, i4, j3)
    some = f0 + in_blocks(1, i1, j1, i1x, j1x) + in_blocks(2, i2, j2, i2x, j2x)[:2]
    weight = grad_qkv(plan, some)

    weight, theirs1, s2, u2, i4x, j3x, plan = together(weight, theirs1, s2, u2, i4x, j3x, plan)
    s1, u1 = both_ways(
        rounded_total(mine1[0], theirs1[0], s2), rounded_total(mine1[1], theirs1[1], u2)
    )
    some = in_blocks(2, i2, j2, i2x, j2x)[2:]
    some += in_blocks(3, i3, j3, i3x, j3x) + in_blocks(4, i4, i4x)
    weight = grad_qkv(plan, some, weight)

    weight, s1, u1 = together(weight, s1, u1)
    input_grad = rounded_total(mine1[2], theirs1[2], s1, u1)
    return input_grad, weight.transpose(1, 0, 2), out


def solution(mesh):
    placed = (
        P("runs", "gx"),
        P("runs", "gx"),
        P(None, None, "gx"),
        P("gx", None),
        P("runs", None, "gx"),
        P("runs"),
    )
    return jax.shard_map(
        functools.partial(on_device, mesh.shape["gx"]),
        mesh=mesh,
        in_specs=placed,
        out_specs=(P("runs", "gx"), P("runs", None, "gx"), P(("runs", "gx"), None)),
        check_vma=False,
    )
```

```python
import functools
import math

import jax
import jax.numpy as jnp
from jax import lax
from jax.experimental import pallas as pl
from jax.experimental.pallas import tpu as pltpu
from jax.sharding import PartitionSpec as P

HD = 128
FACTOR = 1.0 / math.sqrt(HD)
MIB = 1 << 20
NT = (((1,), (1,)), ((), ()))
TN = (((0,), (0,)), ((), ()))


def dot(a, b, dims=(((1,), (0,)), ((), ()))):
    return lax.dot_general(a, b, dims, preferred_element_type=jnp.float32)


def params(mib):
    return pltpu.CompilerParams(vmem_limit_bytes=mib * MIB)


def cost(flops, nbytes, transcendentals=0):
    flops, nbytes = flops // 4096, nbytes // 4096
    return pl.CostEstimate(flops=flops, bytes_accessed=nbytes, transcendentals=transcendentals)


def attend_kernel(row_ref, qkv_ref, attn_ref, out_ref, out_t_ref, column):
    row = row_ref[...]

    @pl.when(pl.program_id(0) == 0)
    def _():
        column[...] = jnp.broadcast_to(row, (HD, row.shape[1])).T

    scores = dot(qkv_ref[0], qkv_ref[1], NT) * FACTOR
    scores = jnp.where(row <= column[:, :1], scores, -1e30)
    expd = jnp.exp(scores - jnp.max(scores, axis=1, keepdims=True))
    attn = (expd / jnp.sum(expd, axis=1, keepdims=True)).astype(jnp.bfloat16)
    attn_ref[0] = attn
    attended = dot(attn, qkv_ref[2])
    out_ref[...] = attended.astype(jnp.bfloat16)
    out_t_ref[...] = attended.T.astype(jnp.bfloat16)


def attend(positions, qkv):
    _, seq, columns = qkv.shape
    heads = columns // HD
    return pl.pallas_call(
        attend_kernel,
        grid=(heads,),
        in_specs=[
            pl.BlockSpec((1, seq), lambda h: (0, 0)),
            pl.BlockSpec((3, seq, HD), lambda h: (0, 0, h)),
        ],
        out_specs=[
            pl.BlockSpec((1, seq, seq), lambda h: (h, 0, 0)),
            pl.BlockSpec((seq, HD), lambda h: (0, h)),
            pl.BlockSpec((HD, seq), lambda h: (h, 0)),
        ],
        out_shape=[
            jax.ShapeDtypeStruct((heads, seq, seq), jnp.bfloat16),
            jax.ShapeDtypeStruct((seq, columns), jnp.bfloat16),
            jax.ShapeDtypeStruct((columns, seq), jnp.bfloat16),
        ],
        scratch_shapes=[pltpu.VMEM((seq, HD), jnp.int32)],
        compiler_params=params(60),
        cost_estimate=cost(4 * seq * seq * columns, 5 * MIB, heads * seq * seq),
    )(positions[None, :], qkv)


def attend_back_kernel(qkv_ref, attn_ref, attended_ref, grad_ref, out_ref):
    grad = grad_ref[...]
    attn = attn_ref[0]
    row_dot = jnp.sum(
        grad.astype(jnp.float32) * attended_ref[...].astype(jnp.float32), axis=1, keepdims=True
    )
    grad_attn = dot(grad, qkv_ref[2], NT)
    grad_scores = (attn.astype(jnp.float32) * (grad_attn - row_dot) * FACTOR).astype(jnp.bfloat16)
    out_ref[0] = dot(grad_scores, qkv_ref[1]).astype(jnp.bfloat16)
    out_ref[1] = dot(grad_scores, qkv_ref[0], TN).astype(jnp.bfloat16)
    out_ref[2] = dot(attn, grad, TN).astype(jnp.bfloat16)


def attend_back(qkv, attn, attended, grad):
    _, seq, columns = qkv.shape
    planes = pl.BlockSpec((3, seq, HD), lambda h: (0, 0, h))
    one = pl.BlockSpec((seq, HD), lambda h: (0, h))
    return pl.pallas_call(
        attend_back_kernel,
        grid=(columns // HD,),
        in_specs=[planes, pl.BlockSpec((1, seq, seq), lambda h: (h, 0, 0)), one, one],
        out_specs=planes,
        out_shape=jax.ShapeDtypeStruct(qkv.shape, jnp.bfloat16),
        compiler_params=params(24),
        cost_estimate=cost(8 * seq * seq * columns, 6 * MIB),
    )(qkv, attn, attended, grad)


def grad_heads_kernel(count, first, last, plan_ref, *refs):
    blocks, weights, rest = refs[:count], refs[count : 2 * count], refs[2 * count :]
    out_ref, total = rest[-2:]
    for i, (block, weight) in enumerate(zip(blocks, weights)):
        term = dot(block[...], weight[...], NT)
        if i:
            total[...] += term
        else:
            total[...] = term if first else rest[0][...] + term
    out_ref[...] = total[...].astype(jnp.bfloat16) if last else total[...]


def grad_heads(plan, w_out, blocks, total=None, last=False):
    columns = w_out.shape[0]
    seq, part = blocks[0][1].shape
    count = len(blocks)

    def weight(place):
        return pl.BlockSpec((columns, part), lambda step, plan: (0, plan[place]))

    def whole(shape):
        return pl.BlockSpec(shape, lambda step, plan: (0, 0))

    first = total is None
    return pl.pallas_call(
        functools.partial(grad_heads_kernel, count, first, last),
        grid_spec=pltpu.PrefetchScalarGridSpec(
            num_scalar_prefetch=1,
            grid=(1,),
            in_specs=[whole((seq, part))] * count
            + [weight(place) for place, _ in blocks]
            + [whole((seq, columns))] * (not first),
            out_specs=whole((seq, columns)),
            scratch_shapes=[pltpu.VMEM((seq, columns), jnp.float32)],
        ),
        out_shape=jax.ShapeDtypeStruct((seq, columns), jnp.bfloat16 if last else jnp.float32),
        compiler_params=params(40),
        cost_estimate=cost(2 * seq * columns * part * count, MIB * count),
    )(plan, *[block for _, block in blocks], *[w_out] * count, *([] if first else [total]))


SLOTS = 4


def weight_kernel(places, turn, plan_ref, left_ref, *refs):
    out_ref, held, sems = refs[-3:]
    copies = []
    for i, (place, block) in enumerate(zip(places, refs)):
        width = block.shape[1]
        slot = i % SLOTS
        if i >= SLOTS:
            copies[i - SLOTS].wait()
        if turn:
            turned = block[...].T
            for k in range(3):
                held[slot, k] = dot(turned, left_ref[k]).astype(jnp.bfloat16)
        else:
            held[slot] = dot(left_ref[...], block[...]).astype(jnp.bfloat16)
        start = pl.multiple_of(plan_ref[place] * width, 128)
        copy = pltpu.make_async_copy(
            held.at[slot], out_ref.at[:, pl.ds(start, width)], sems.at[slot]
        )
        copy.start()
        copies.append(copy)
    for copy in copies[-SLOTS:]:
        copy.wait()


def weight_grad(plan, left, blocks, shape, into=None):
    turn = left.ndim == 3
    seq, part = blocks[0][1].shape
    count = len(blocks)
    held = (3, part, left.shape[2]) if turn else (left.shape[0], part)
    vmem = pl.BlockSpec(memory_space=pltpu.VMEM)
    rest = pl.BlockSpec(memory_space=pl.ANY)
    size = math.prod(held) * count
    return pl.pallas_call(
        functools.partial(weight_kernel, [place for place, _ in blocks], turn),
        in_specs=[pl.BlockSpec(memory_space=pltpu.SMEM)]
        + [vmem] * (1 + count)
        + [rest] * (into is not None),
        out_specs=rest,
        out_shape=jax.ShapeDtypeStruct(shape, jnp.bfloat16),
        scratch_shapes=[
            pltpu.VMEM((SLOTS, *held), jnp.bfloat16),
            pltpu.SemaphoreType.DMA((SLOTS,)),
        ],
        input_output_aliases={} if into is None else {2 + count: 0},
        compiler_params=params(40),
        cost_estimate=cost(2 * seq * size, 3 * size),
    )(plan, left, *[block for _, block in blocks], *([] if into is None else [into]))


def terms_kernel(plan_ref, grad_ref, w_ref, theirs_ref, mine_ref):
    total = dot(grad_ref[0], w_ref[0], NT)
    total += dot(grad_ref[1], w_ref[1], NT)
    total += dot(grad_ref[2], w_ref[2], NT)
    total = total.astype(jnp.bfloat16)
    part = total.shape[1] // 2

    @pl.when(plan_ref[0] == 0)
    def _():
        mine_ref[0] = total[:, :part]
        theirs_ref[0] = total[:, part:]

    @pl.when(plan_ref[0] == 1)
    def _():
        mine_ref[0] = total[:, part:]
        theirs_ref[0] = total[:, :part]


def terms(plan, place, count, grad, w, part):
    _, seq, columns = grad.shape
    out = pl.BlockSpec((1, seq, part), lambda i, plan: (i, 0, 0))
    shape = jax.ShapeDtypeStruct((count, seq, part), jnp.bfloat16)
    return pl.pallas_call(
        terms_kernel,
        grid_spec=pltpu.PrefetchScalarGridSpec(
            num_scalar_prefetch=1,
            grid=(count,),
            in_specs=[
                pl.BlockSpec((3, seq, columns), lambda i, plan: (0, 0, 0)),
                pl.BlockSpec((3, 2 * part, columns), lambda i, plan: (0, plan[place + i], 0)),
            ],
            out_specs=[out, out],
        ),
        out_shape=[shape, shape],
        compiler_params=params(48),
        cost_estimate=cost(12 * seq * columns * part * count, 5 * MIB * count),
    )(plan, grad, w)


def plain(n, inputs, out_grad, w_qkv, w_out, saved_qkv, positions):
    full_in = lax.all_gather(inputs, "gx", axis=1, tiled=True)
    full_grad = lax.all_gather(out_grad, "gx", axis=1, tiled=True)
    qkv = saved_qkv.transpose(1, 0, 2)
    attn, attended, _ = attend(positions, qkv)
    grad_h = dot(full_grad, w_out, NT).astype(jnp.bfloat16)
    grad_w_out = dot(attended, full_grad, TN).astype(jnp.bfloat16)
    grad = attend_back(qkv, attn, attended, grad_h)
    grad_w_qkv = jnp.stack([dot(full_in, grad[k], TN).astype(jnp.bfloat16) for k in range(3)], 1)
    partial = sum(dot(grad[k], w_qkv[:, k], NT) for k in range(3))
    input_grad = lax.psum_scatter(partial, "gx", scatter_dimension=1, tiled=True)
    return input_grad.astype(jnp.bfloat16), grad_w_qkv, grad_w_out


def ring_order(chips):
    if chips == 8:
        return [0, 2, 4, 6, 7, 5, 3, 1]
    return list(range(chips))


def plan_of(order, device):
    chips = len(order)
    at = order.index(device // 2)
    core = device % 2

    def chip(offset):
        return order[(at + offset) % chips]

    blocks = [2 * chip(0) + core, 2 * chip(0) + 1 - core]
    for step in range(1, chips // 2):
        for shard in (core, 1 - core):
            blocks += [2 * chip(-step) + shard, 2 * chip(step) + shard]
    blocks += [2 * chip(chips // 2) + core, 2 * chip(chips // 2) + 1 - core]
    summed = [chip(chips // 2)]
    for step in range(chips // 2 - 1, 0, -1):
        summed += [chip(step), chip(-step)]
    apart = blocks[:2]
    for step in range(1, chips // 2):
        behind = step if core else -step
        for shard, first in ((core, behind), (1 - core, -behind)):
            apart += [2 * chip(first) + shard, 2 * chip(-first) + shard]
    return [core] + blocks + summed + [chip(0)] + apart + blocks[-2:]


def after(x, *others):
    return lax.optimization_barrier((x, *others))[0]


def together(*arrays):
    return lax.optimization_barrier(arrays)


def f32(x):
    return x.astype(jnp.float32)


def on_device(n, inputs, out_grad, w_qkv, w_out, saved_qkv, positions):
    part = inputs.shape[1]
    if part % 128 or n != 16:
        return plain(n, inputs, out_grad, w_qkv, w_out, saved_qkv, positions)
    order = ring_order(n // 2)
    hops = [(2 * order[i - 1], 2 * order[i]) for i in range(n // 2)]
    ahead = [(i + core, j + core) for i, j in hops for core in range(2)]
    back = [(j, i) for i, j in ahead]
    apart = [(i, j) for i, j in hops] + [(j + 1, i + 1) for i, j in hops]
    crossed = [(j, i) for i, j in apart]
    swap = [(i, i ^ 1) for i in range(n)]
    plans = [plan_of(order, i) for i in range(n)]
    size = len(plans[0])
    plan = lax.dynamic_slice(
        jnp.array(sum(plans, []), jnp.int32), (lax.axis_index("gx") * size,), (size,)
    )
    on_first = lax.axis_index("gx") % 2 == 0

    def both_ways(right, left):
        return lax.ppermute(right, "gx", ahead), lax.ppermute(left, "gx", back)

    def one_way(right, left):
        return lax.ppermute(jnp.where(on_first, right, left), "gx", apart)

    def first_chain(x):
        return lax.ppermute(x, "gx", apart)

    def second_chain(x):
        return lax.ppermute(x, "gx", crossed)

    def swapped(*arrays):
        found = [lax.ppermute(x, "gx", swap) for x in arrays]
        return found if len(found) > 1 else found[0]

    def blocks(step, *arrays):
        first = 1 if step == 0 else 4 * step - 1
        return [(first + i, array) for i, array in enumerate(arrays)]

    def in_blocks(step, *arrays):
        return [(place + 24, array) for place, array in blocks(step, *arrays)]

    def grad_qkv(index, some, into=None):
        return weight_grad(index, grad, some, w.shape, into)

    def total(*values):
        return sum(f32(value) for value in values[1:]) + f32(values[0])

    def rounded_total(*values):
        return total(*values).astype(jnp.bfloat16)

    qkv = saved_qkv.transpose(1, 0, 2)
    w = w_qkv.transpose(1, 0, 2)

    def grad_out_heads(index, some, so_far=None, last=False):
        return grad_heads(index, w_out, some, so_far, last)

    def grad_out(index, some, into=None):
        return weight_grad(index, attended_t, some, w_out.shape, into)

    r1, l1 = both_ways(out_grad, out_grad)
    i1 = first_chain(inputs)
    other = swapped(out_grad)
    attn, attended, attended_t = attend(positions, qkv)

    r1, l1, i1, attended, plan = together(r1, l1, i1, attended, plan)
    r2, l2 = both_ways(r1, l1)
    i2 = first_chain(i1)
    g1 = blocks(1, r1, l1, *swapped(r1, l1))
    g0 = blocks(0, out_grad, other)
    out = grad_out(plan, g0)

    r2, l2, i2, out, plan = together(r2, l2, i2, out, plan)
    r3, l3 = both_ways(r2, l2)
    i3 = first_chain(i2)
    g2 = blocks(2, r2, l2, *swapped(r2, l2))
    grad_h = grad_out_heads(plan, g0 + g1)
    out = grad_out(plan, g1, out)

    r3, l3, i3, grad_h, out, plan = together(r3, l3, i3, grad_h, out, plan)
    x4 = one_way(r3, l3)
    j1 = second_chain(after(inputs, r3))
    r3x, l3x = swapped(r3, l3)
    g3 = blocks(3, r3, l3, r3x, l3x)
    grad_h = grad_out_heads(plan, g2, grad_h)

    grad_h, r3x, l3x, plan = together(grad_h, r3x, l3x, plan)
    out = grad_out(plan, g2, out)
    grad_h = grad_out_heads(plan, g3, grad_h)

    x4, j1, grad_h, out, plan = together(x4, j1, grad_h, out, plan)
    x4x, other = swapped(x4, inputs)
    i4, j2 = first_chain(i3), second_chain(j1)
    f0 = in_blocks(0, inputs, other)
    g4 = blocks(4, x4, x4x)
    grad_h = grad_out_heads(plan, g4, grad_h, last=True)
    grad = attend_back(qkv, attn, attended, grad_h)

    grad, plan = together(grad, plan)
    out = grad_out(plan, g3, out)

    out, i4, j2, other, plan = together(out, i4, j2, other, plan)
    j3 = second_chain(j2)
    i1x, i2x = swapped(i1, i2)
    theirs3, mine3 = terms(plan, 17, 3, grad, w, part)

    theirs3, mine3, j3, i1x, i2x, plan = together(theirs3, mine3, j3, i1x, i2x, plan)
    theirs3 = swapped(theirs3)
    i3x, j1x = swapped(i3, j1)
    out = grad_out(plan, g4, out)

    out, theirs3, i3x, j1x, plan = together(out, theirs3, i3x, j1x, plan)
    low = rounded_total(mine3[0], theirs3[0])
    s4 = first_chain(low)
    i4x, j2x = swapped(i4, j2)
    theirs2, mine2 = terms(plan, 20, 2, grad, w, part)

    theirs2, mine2, s4, i4x, j2x, plan = together(theirs2, mine2, s4, i4x, j2x, plan)
    nothing = jnp.zeros_like(s4)
    s3, u3 = both_ways(
        rounded_total(mine3[1], theirs3[1], jnp.where(on_first, s4, nothing)),
        rounded_total(mine3[2], theirs3[2], jnp.where(on_first, nothing, s4)),
    )
    theirs2, j3x = swapped(theirs2, j3)
    theirs1, mine1 = terms(plan, 22, 3, grad, w, part)

    theirs1, mine1, theirs2, s3, u3, j3x, plan = together(
        theirs1, mine1, theirs2, s3, u3, j3x, plan
    )
    s2, u2 = both_ways(
        rounded_total(mine2[0], theirs2[0], s3), rounded_total(mine2[1], theirs2[1], u3)
    )
    theirs1 = swapped(theirs1)
    some = f0 + in_blocks(1, i1, j1, i1x, j1x) + in_blocks(2, i2, j2, i2x, j2x)[:2]
    weight = grad_qkv(plan, some)

    weight, theirs1, s2, u2, plan = together(weight, theirs1, s2, u2, plan)
    s1, u1 = both_ways(
        rounded_total(mine1[0], theirs1[0], s2), rounded_total(mine1[1], theirs1[1], u2)
    )
    some = in_blocks(2, i2, j2, i2x, j2x)[2:]
    some += in_blocks(3, i3, j3, i3x, j3x) + in_blocks(4, i4, i4x)
    weight = grad_qkv(plan, some, weight)

    weight, s1, u1 = together(weight, s1, u1)
    input_grad = rounded_total(mine1[2], theirs1[2], s1, u1)
    return input_grad, weight.transpose(1, 0, 2), out


def solution(mesh):
    placed = (
        P("runs", "gx"),
        P("runs", "gx"),
        P(None, None, "gx"),
        P("gx", None),
        P("runs", None, "gx"),
        P("runs"),
    )
    return jax.shard_map(
        functools.partial(on_device, mesh.shape["gx"]),
        mesh=mesh,
        in_specs=placed,
        out_specs=(P("runs", "gx"), P("runs", None, "gx"), P(("runs", "gx"), None)),
        check_vma=False,
    )
```

```python
import functools
import math

import jax
import jax.numpy as jnp
from jax import lax
from jax.experimental import pallas as pl
from jax.experimental.pallas import tpu as pltpu
from jax.sharding import PartitionSpec as P

HD = 128
FACTOR = 1.0 / math.sqrt(HD)
MIB = 1 << 20
NT = (((1,), (1,)), ((), ()))
TN = (((0,), (0,)), ((), ()))


def dot(a, b, dims=(((1,), (0,)), ((), ()))):
    return lax.dot_general(a, b, dims, preferred_element_type=jnp.float32)


def params(mib):
    return pltpu.CompilerParams(vmem_limit_bytes=mib * MIB)


def cost(flops, nbytes, transcendentals=0):
    flops, nbytes = flops // 4096, nbytes // 4096
    return pl.CostEstimate(flops=flops, bytes_accessed=nbytes, transcendentals=transcendentals)


def attend_kernel(row_ref, qkv_ref, attn_ref, out_ref, out_t_ref, column):
    row = row_ref[...]

    @pl.when(pl.program_id(0) == 0)
    def _():
        column[...] = jnp.broadcast_to(row, (HD, row.shape[1])).T

    scores = dot(qkv_ref[0], qkv_ref[1], NT) * FACTOR
    scores = jnp.where(row <= column[:, :1], scores, -1e30)
    expd = jnp.exp(scores - jnp.max(scores, axis=1, keepdims=True))
    attn = (expd / jnp.sum(expd, axis=1, keepdims=True)).astype(jnp.bfloat16)
    attn_ref[0] = attn
    attended = dot(attn, qkv_ref[2])
    out_ref[...] = attended.astype(jnp.bfloat16)
    out_t_ref[...] = attended.T.astype(jnp.bfloat16)


def attend(positions, qkv):
    _, seq, columns = qkv.shape
    heads = columns // HD
    return pl.pallas_call(
        attend_kernel,
        grid=(heads,),
        in_specs=[
            pl.BlockSpec((1, seq), lambda h: (0, 0)),
            pl.BlockSpec((3, seq, HD), lambda h: (0, 0, h)),
        ],
        out_specs=[
            pl.BlockSpec((1, seq, seq), lambda h: (h, 0, 0)),
            pl.BlockSpec((seq, HD), lambda h: (0, h)),
            pl.BlockSpec((HD, seq), lambda h: (h, 0)),
        ],
        out_shape=[
            jax.ShapeDtypeStruct((heads, seq, seq), jnp.bfloat16),
            jax.ShapeDtypeStruct((seq, columns), jnp.bfloat16),
            jax.ShapeDtypeStruct((columns, seq), jnp.bfloat16),
        ],
        scratch_shapes=[pltpu.VMEM((seq, HD), jnp.int32)],
        compiler_params=params(60),
        cost_estimate=cost(4 * seq * seq * columns, 5 * MIB, heads * seq * seq),
    )(positions[None, :], qkv)


def attend_back_kernel(qkv_ref, attn_ref, attended_ref, grad_ref, out_ref):
    grad = grad_ref[...]
    attn = attn_ref[0]
    row_dot = jnp.sum(
        grad.astype(jnp.float32) * attended_ref[...].astype(jnp.float32), axis=1, keepdims=True
    )
    grad_attn = dot(grad, qkv_ref[2], NT)
    grad_scores = (attn.astype(jnp.float32) * (grad_attn - row_dot) * FACTOR).astype(jnp.bfloat16)
    out_ref[0] = dot(grad_scores, qkv_ref[1]).astype(jnp.bfloat16)
    out_ref[1] = dot(grad_scores, qkv_ref[0], TN).astype(jnp.bfloat16)
    out_ref[2] = dot(attn, grad, TN).astype(jnp.bfloat16)


def attend_back(qkv, attn, attended, grad):
    _, seq, columns = qkv.shape
    planes = pl.BlockSpec((3, seq, HD), lambda h: (0, 0, h))
    one = pl.BlockSpec((seq, HD), lambda h: (0, h))
    return pl.pallas_call(
        attend_back_kernel,
        grid=(columns // HD,),
        in_specs=[planes, pl.BlockSpec((1, seq, seq), lambda h: (h, 0, 0)), one, one],
        out_specs=planes,
        out_shape=jax.ShapeDtypeStruct(qkv.shape, jnp.bfloat16),
        compiler_params=params(24),
        cost_estimate=cost(8 * seq * seq * columns, 6 * MIB),
    )(qkv, attn, attended, grad)


def grad_heads_kernel(count, first, last, plan_ref, *refs):
    blocks, weights, rest = refs[:count], refs[count : 2 * count], refs[2 * count :]
    out_ref, total = rest[-2:]
    for i, (block, weight) in enumerate(zip(blocks, weights)):
        term = dot(block[...], weight[...], NT)
        if i:
            total[...] += term
        else:
            total[...] = term if first else rest[0][...] + term
    out_ref[...] = total[...].astype(jnp.bfloat16) if last else total[...]


def grad_heads(plan, w_out, blocks, total=None, last=False):
    columns = w_out.shape[0]
    seq, part = blocks[0][1].shape
    count = len(blocks)

    def weight(place):
        return pl.BlockSpec((columns, part), lambda step, plan: (0, plan[place]))

    def whole(shape):
        return pl.BlockSpec(shape, lambda step, plan: (0, 0))

    first = total is None
    return pl.pallas_call(
        functools.partial(grad_heads_kernel, count, first, last),
        grid_spec=pltpu.PrefetchScalarGridSpec(
            num_scalar_prefetch=1,
            grid=(1,),
            in_specs=[whole((seq, part))] * count
            + [weight(place) for place, _ in blocks]
            + [whole((seq, columns))] * (not first),
            out_specs=whole((seq, columns)),
            scratch_shapes=[pltpu.VMEM((seq, columns), jnp.float32)],
        ),
        out_shape=jax.ShapeDtypeStruct((seq, columns), jnp.bfloat16 if last else jnp.float32),
        compiler_params=params(40),
        cost_estimate=cost(2 * seq * columns * part * count, MIB * count),
    )(plan, *[block for _, block in blocks], *[w_out] * count, *([] if first else [total]))


SLOTS = 4


def weight_kernel(places, turn, plan_ref, left_ref, *refs):
    out_ref, held, sems = refs[-3:]
    copies = []
    for i, (place, block) in enumerate(zip(places, refs)):
        width = block.shape[1]
        slot = i % SLOTS
        if i >= SLOTS:
            copies[i - SLOTS].wait()
        if turn:
            turned = block[...].T
            for k in range(3):
                held[slot, k] = dot(turned, left_ref[k]).astype(jnp.bfloat16)
        else:
            held[slot] = dot(left_ref[...], block[...]).astype(jnp.bfloat16)
        start = pl.multiple_of(plan_ref[place] * width, 128)
        copy = pltpu.make_async_copy(
            held.at[slot], out_ref.at[:, pl.ds(start, width)], sems.at[slot]
        )
        copy.start()
        copies.append(copy)
    for copy in copies[-SLOTS:]:
        copy.wait()


def weight_grad(plan, left, blocks, shape, into=None):
    turn = left.ndim == 3
    seq, part = blocks[0][1].shape
    count = len(blocks)
    held = (3, part, left.shape[2]) if turn else (left.shape[0], part)
    vmem = pl.BlockSpec(memory_space=pltpu.VMEM)
    rest = pl.BlockSpec(memory_space=pl.ANY)
    size = math.prod(held) * count
    return pl.pallas_call(
        functools.partial(weight_kernel, [place for place, _ in blocks], turn),
        in_specs=[pl.BlockSpec(memory_space=pltpu.SMEM)]
        + [vmem] * (1 + count)
        + [rest] * (into is not None),
        out_specs=rest,
        out_shape=jax.ShapeDtypeStruct(shape, jnp.bfloat16),
        scratch_shapes=[
            pltpu.VMEM((SLOTS, *held), jnp.bfloat16),
            pltpu.SemaphoreType.DMA((SLOTS,)),
        ],
        input_output_aliases={} if into is None else {2 + count: 0},
        compiler_params=params(40),
        cost_estimate=cost(2 * seq * size, 3 * size),
    )(plan, left, *[block for _, block in blocks], *([] if into is None else [into]))


def terms_kernel(plan_ref, grad_ref, w_ref, theirs_ref, mine_ref):
    total = dot(grad_ref[0], w_ref[0], NT)
    total += dot(grad_ref[1], w_ref[1], NT)
    total += dot(grad_ref[2], w_ref[2], NT)
    total = total.astype(jnp.bfloat16)
    part = total.shape[1] // 2

    @pl.when(plan_ref[0] == 0)
    def _():
        mine_ref[0] = total[:, :part]
        theirs_ref[0] = total[:, part:]

    @pl.when(plan_ref[0] == 1)
    def _():
        mine_ref[0] = total[:, part:]
        theirs_ref[0] = total[:, :part]


def terms(plan, place, count, grad, w, part):
    _, seq, columns = grad.shape
    out = pl.BlockSpec((1, seq, part), lambda i, plan: (i, 0, 0))
    shape = jax.ShapeDtypeStruct((count, seq, part), jnp.bfloat16)
    return pl.pallas_call(
        terms_kernel,
        grid_spec=pltpu.PrefetchScalarGridSpec(
            num_scalar_prefetch=1,
            grid=(count,),
            in_specs=[
                pl.BlockSpec((3, seq, columns), lambda i, plan: (0, 0, 0)),
                pl.BlockSpec((3, 2 * part, columns), lambda i, plan: (0, plan[place + i], 0)),
            ],
            out_specs=[out, out],
        ),
        out_shape=[shape, shape],
        compiler_params=params(48),
        cost_estimate=cost(12 * seq * columns * part * count, 5 * MIB * count),
    )(plan, grad, w)


def plain(n, inputs, out_grad, w_qkv, w_out, saved_qkv, positions):
    full_in = lax.all_gather(inputs, "gx", axis=1, tiled=True)
    full_grad = lax.all_gather(out_grad, "gx", axis=1, tiled=True)
    qkv = saved_qkv.transpose(1, 0, 2)
    attn, attended, _ = attend(positions, qkv)
    grad_h = dot(full_grad, w_out, NT).astype(jnp.bfloat16)
    grad_w_out = dot(attended, full_grad, TN).astype(jnp.bfloat16)
    grad = attend_back(qkv, attn, attended, grad_h)
    grad_w_qkv = jnp.stack([dot(full_in, grad[k], TN).astype(jnp.bfloat16) for k in range(3)], 1)
    partial = sum(dot(grad[k], w_qkv[:, k], NT) for k in range(3))
    input_grad = lax.psum_scatter(partial, "gx", scatter_dimension=1, tiled=True)
    return input_grad.astype(jnp.bfloat16), grad_w_qkv, grad_w_out


def ring_order(chips):
    if chips == 8:
        return [0, 2, 4, 6, 7, 5, 3, 1]
    return list(range(chips))


def plan_of(order, device):
    chips = len(order)
    at = order.index(device // 2)
    core = device % 2

    def chip(offset):
        return order[(at + offset) % chips]

    blocks = [2 * chip(0) + core, 2 * chip(0) + 1 - core]
    for step in range(1, chips // 2):
        for shard in (core, 1 - core):
            blocks += [2 * chip(-step) + shard, 2 * chip(step) + shard]
    blocks += [2 * chip(chips // 2) + core, 2 * chip(chips // 2) + 1 - core]
    summed = [chip(chips // 2)]
    for step in range(chips // 2 - 1, 0, -1):
        summed += [chip(step), chip(-step)]
    apart = blocks[:2]
    for step in range(1, chips // 2):
        behind = step if core else -step
        for shard, first in ((core, behind), (1 - core, -behind)):
            apart += [2 * chip(first) + shard, 2 * chip(-first) + shard]
    return [core] + blocks + summed + [chip(0)] + apart + blocks[-2:]


def after(x, *others):
    return lax.optimization_barrier((x, *others))[0]


def together(*arrays):
    return lax.optimization_barrier(arrays)


def f32(x):
    return x.astype(jnp.float32)


def on_device(n, inputs, out_grad, w_qkv, w_out, saved_qkv, positions):
    part = inputs.shape[1]
    if part % 128 or n != 16:
        return plain(n, inputs, out_grad, w_qkv, w_out, saved_qkv, positions)
    order = ring_order(n // 2)
    hops = [(2 * order[i - 1], 2 * order[i]) for i in range(n // 2)]
    ahead = [(i + core, j + core) for i, j in hops for core in range(2)]
    back = [(j, i) for i, j in ahead]
    apart = [(i, j) for i, j in hops] + [(j + 1, i + 1) for i, j in hops]
    crossed = [(j, i) for i, j in apart]
    swap = [(i, i ^ 1) for i in range(n)]
    plans = [plan_of(order, i) for i in range(n)]
    size = len(plans[0])
    plan = lax.dynamic_slice(
        jnp.array(sum(plans, []), jnp.int32), (lax.axis_index("gx") * size,), (size,)
    )
    on_first = lax.axis_index("gx") % 2 == 0
    half = inputs.shape[0] // 2

    def both_ways(right, left):
        return lax.ppermute(right, "gx", ahead), lax.ppermute(left, "gx", back)

    def one_way(right, left):
        return lax.ppermute(jnp.where(on_first, right, left), "gx", apart)

    def first_chain(x):
        return lax.ppermute(x, "gx", apart)

    def second_chain(x):
        return lax.ppermute(x, "gx", crossed)

    def swapped(*arrays):
        found = [lax.ppermute(x, "gx", swap) for x in arrays]
        return found if len(found) > 1 else found[0]

    def blocks(step, *arrays):
        first = 1 if step == 0 else 4 * step - 1
        return [(first + i, array) for i, array in enumerate(arrays)]

    def in_blocks(step, *arrays):
        return [(place + 24, array) for place, array in blocks(step, *arrays)]

    def grad_qkv(index, some, into=None):
        return weight_grad(index, grad, some, w.shape, into)

    def total(*values):
        return sum(f32(value) for value in values[1:]) + f32(values[0])

    def rounded_total(*values):
        return total(*values).astype(jnp.bfloat16)

    qkv = saved_qkv.transpose(1, 0, 2)
    w = w_qkv.transpose(1, 0, 2)

    def grad_out_heads(index, some, so_far=None, last=False):
        return grad_heads(index, w_out, some, so_far, last)

    def grad_out(index, some, into=None):
        return weight_grad(index, attended_t, some, w_out.shape, into)

    r1, l1 = both_ways(out_grad, out_grad)
    other = swapped(out_grad)
    attn, attended, attended_t = attend(positions, qkv)

    r1, l1, attended, plan = together(r1, l1, attended, plan)
    r2, l2 = both_ways(r1, l1)
    g1 = blocks(1, r1, l1, *swapped(r1, l1))
    g0 = blocks(0, out_grad, other)
    out = grad_out(plan, g0)

    r2, l2, out, plan = together(r2, l2, out, plan)
    r3, l3 = both_ways(r2, l2)
    g2 = blocks(2, r2, l2, *swapped(r2, l2))
    grad_h = grad_out_heads(plan, g0 + g1)
    out = grad_out(plan, g1, out)

    r3, l3, grad_h, out, plan = together(r3, l3, grad_h, out, plan)
    x4 = one_way(r3, l3)
    i1 = first_chain(after(inputs, r3))
    r3x, l3x = swapped(r3, l3)
    g3 = blocks(3, r3, l3, r3x, l3x)
    grad_h = grad_out_heads(plan, g2, grad_h)

    grad_h, r3x, l3x, plan = together(grad_h, r3x, l3x, plan)
    out = grad_out(plan, g2, out)
    grad_h = grad_out_heads(plan, g3, grad_h)

    x4, i1, grad_h, out, plan = together(x4, i1, grad_h, out, plan)
    x4x, other = swapped(x4, inputs)
    i2, j1 = first_chain(i1), second_chain(inputs)
    f0 = in_blocks(0, inputs, other)
    g4 = blocks(4, x4, x4x)
    grad_h = grad_out_heads(plan, g4, grad_h, last=True)
    grad = attend_back(qkv, attn, attended, grad_h)

    grad, plan = together(grad, plan)
    out = grad_out(plan, g3, out)

    out, i2, j1, other, plan = together(out, i2, j1, other, plan)
    i3, j2 = first_chain(i2), second_chain(j1)
    i1x, j1x = swapped(i1, j1)
    theirs3, mine3 = terms(plan, 17, 3, grad, w, part)

    theirs3, mine3, i3, j2, i1x, j1x, plan = together(theirs3, mine3, i3, j2, i1x, j1x, plan)
    theirs3 = swapped(theirs3)
    i4, j3 = first_chain(i3), second_chain(j2)
    i2x, j2x = swapped(i2, j2)
    out = grad_out(plan, g4, out)

    out, theirs3, plan = together(out, theirs3, plan)
    low = rounded_total(mine3[0], theirs3[0])
    s4, u4 = both_ways(low[:half], low[half:])
    theirs2, mine2 = terms(plan, 20, 2, grad, w, part)

    theirs2, mine2, s4, u4, i4, j3, i2x, j2x, plan = together(
        theirs2, mine2, s4, u4, i4, j3, i2x, j2x, plan
    )
    s4 = jnp.pad(s4, ((0, half), (0, 0)))
    u4 = jnp.pad(u4, ((half, 0), (0, 0)))
    s3, u3 = both_ways(
        rounded_total(mine3[1], theirs3[1], s4), rounded_total(mine3[2], theirs3[2], u4)
    )
    theirs2, i3x = swapped(theirs2, i3)
    theirs1, mine1 = terms(plan, 22, 3, grad, w, part)

    theirs1, mine1, theirs2, s3, u3, i3x, plan = together(
        theirs1, mine1, theirs2, s3, u3, i3x, plan
    )
    s2, u2 = both_ways(
        rounded_total(mine2[0], theirs2[0], s3), rounded_total(mine2[1], theirs2[1], u3)
    )
    theirs1, i4x, j3x = swapped(theirs1, i4, j3)
    some = f0 + in_blocks(1, i1, j1, i1x, j1x) + in_blocks(2, i2, j2, i2x, j2x)[:2]
    weight = grad_qkv(plan, some)

    weight, theirs1, s2, u2, i4x, j3x, plan = together(weight, theirs1, s2, u2, i4x, j3x, plan)
    s1, u1 = both_ways(
        rounded_total(mine1[0], theirs1[0], s2), rounded_total(mine1[1], theirs1[1], u2)
    )
    some = in_blocks(2, i2, j2, i2x, j2x)[2:]
    some += in_blocks(3, i3, j3, i3x, j3x) + in_blocks(4, i4, i4x)
    weight = grad_qkv(plan, some, weight)

    weight, s1, u1 = together(weight, s1, u1)
    input_grad = rounded_total(mine1[2], theirs1[2], s1, u1)
    return input_grad, weight.transpose(1, 0, 2), out


def solution(mesh):
    placed = (
        P("runs", "gx"),
        P("runs", "gx"),
        P(None, None, "gx"),
        P("gx", None),
        P("runs", None, "gx"),
        P("runs"),
    )
    return jax.shard_map(
        functools.partial(on_device, mesh.shape["gx"]),
        mesh=mesh,
        in_specs=placed,
        out_specs=(P("runs", "gx"), P("runs", None, "gx"), P(("runs", "gx"), None)),
        check_vma=False,
    )
```

```python
import functools
import math

import jax
import jax.numpy as jnp
from jax import lax
from jax.experimental import pallas as pl
from jax.experimental.pallas import tpu as pltpu
from jax.sharding import PartitionSpec as P

HD = 128
FACTOR = 1.0 / math.sqrt(HD)
MIB = 1 << 20
NT = (((1,), (1,)), ((), ()))
TN = (((0,), (0,)), ((), ()))


def dot(a, b, dims=(((1,), (0,)), ((), ()))):
    return lax.dot_general(a, b, dims, preferred_element_type=jnp.float32)


def params(mib):
    return pltpu.CompilerParams(vmem_limit_bytes=mib * MIB)


def cost(flops, nbytes, transcendentals=0):
    flops, nbytes = flops // 4096, nbytes // 4096
    return pl.CostEstimate(flops=flops, bytes_accessed=nbytes, transcendentals=transcendentals)


def attend_kernel(row_ref, qkv_ref, attn_ref, out_ref, out_t_ref, column):
    row = row_ref[...]

    @pl.when(pl.program_id(0) == 0)
    def _():
        column[...] = jnp.broadcast_to(row, (HD, row.shape[1])).T

    scores = dot(qkv_ref[0], qkv_ref[1], NT) * FACTOR
    scores = jnp.where(row <= column[:, :1], scores, -1e30)
    expd = jnp.exp(scores - jnp.max(scores, axis=1, keepdims=True))
    attn = (expd / jnp.sum(expd, axis=1, keepdims=True)).astype(jnp.bfloat16)
    attn_ref[0] = attn
    attended = dot(attn, qkv_ref[2])
    out_ref[...] = attended.astype(jnp.bfloat16)
    out_t_ref[...] = attended.T.astype(jnp.bfloat16)


def attend(positions, qkv):
    _, seq, columns = qkv.shape
    heads = columns // HD
    return pl.pallas_call(
        attend_kernel,
        grid=(heads,),
        in_specs=[
            pl.BlockSpec((1, seq), lambda h: (0, 0)),
            pl.BlockSpec((3, seq, HD), lambda h: (0, 0, h)),
        ],
        out_specs=[
            pl.BlockSpec((1, seq, seq), lambda h: (h, 0, 0)),
            pl.BlockSpec((seq, HD), lambda h: (0, h)),
            pl.BlockSpec((HD, seq), lambda h: (h, 0)),
        ],
        out_shape=[
            jax.ShapeDtypeStruct((heads, seq, seq), jnp.bfloat16),
            jax.ShapeDtypeStruct((seq, columns), jnp.bfloat16),
            jax.ShapeDtypeStruct((columns, seq), jnp.bfloat16),
        ],
        scratch_shapes=[pltpu.VMEM((seq, HD), jnp.int32)],
        compiler_params=params(60),
        cost_estimate=cost(4 * seq * seq * columns, 5 * MIB, heads * seq * seq),
    )(positions[None, :], qkv)


def attend_back_kernel(qkv_ref, attn_ref, attended_ref, grad_ref, out_ref):
    grad = grad_ref[...]
    attn = attn_ref[0]
    row_dot = jnp.sum(
        grad.astype(jnp.float32) * attended_ref[...].astype(jnp.float32), axis=1, keepdims=True
    )
    grad_attn = dot(grad, qkv_ref[2], NT)
    grad_scores = (attn.astype(jnp.float32) * (grad_attn - row_dot) * FACTOR).astype(jnp.bfloat16)
    out_ref[0] = dot(grad_scores, qkv_ref[1]).astype(jnp.bfloat16)
    out_ref[1] = dot(grad_scores, qkv_ref[0], TN).astype(jnp.bfloat16)
    out_ref[2] = dot(attn, grad, TN).astype(jnp.bfloat16)


def attend_back(qkv, attn, attended, grad):
    _, seq, columns = qkv.shape
    planes = pl.BlockSpec((3, seq, HD), lambda h: (0, 0, h))
    one = pl.BlockSpec((seq, HD), lambda h: (0, h))
    return pl.pallas_call(
        attend_back_kernel,
        grid=(columns // HD,),
        in_specs=[planes, pl.BlockSpec((1, seq, seq), lambda h: (h, 0, 0)), one, one],
        out_specs=planes,
        out_shape=jax.ShapeDtypeStruct(qkv.shape, jnp.bfloat16),
        compiler_params=params(24),
        cost_estimate=cost(8 * seq * seq * columns, 6 * MIB),
    )(qkv, attn, attended, grad)


def grad_heads_kernel(count, first, last, plan_ref, *refs):
    blocks, weights, rest = refs[:count], refs[count : 2 * count], refs[2 * count :]
    out_ref, total = rest[-2:]
    for i, (block, weight) in enumerate(zip(blocks, weights)):
        term = dot(block[...], weight[...], NT)
        if i:
            total[...] += term
        else:
            total[...] = term if first else rest[0][...] + term
    out_ref[...] = total[...].astype(jnp.bfloat16) if last else total[...]


def grad_heads(plan, w_out, blocks, total=None, last=False):
    columns = w_out.shape[0]
    seq, part = blocks[0][1].shape
    count = len(blocks)

    def weight(place):
        return pl.BlockSpec((columns, part), lambda step, plan: (0, plan[place]))

    def whole(shape):
        return pl.BlockSpec(shape, lambda step, plan: (0, 0))

    first = total is None
    return pl.pallas_call(
        functools.partial(grad_heads_kernel, count, first, last),
        grid_spec=pltpu.PrefetchScalarGridSpec(
            num_scalar_prefetch=1,
            grid=(1,),
            in_specs=[whole((seq, part))] * count
            + [weight(place) for place, _ in blocks]
            + [whole((seq, columns))] * (not first),
            out_specs=whole((seq, columns)),
            scratch_shapes=[pltpu.VMEM((seq, columns), jnp.float32)],
        ),
        out_shape=jax.ShapeDtypeStruct((seq, columns), jnp.bfloat16 if last else jnp.float32),
        compiler_params=params(40),
        cost_estimate=cost(2 * seq * columns * part * count, MIB * count),
    )(plan, *[block for _, block in blocks], *[w_out] * count, *([] if first else [total]))


SLOTS = 4


def weight_kernel(places, turn, plan_ref, left_ref, *refs):
    out_ref, held, sems = refs[-3:]
    copies = []
    for i, (place, block) in enumerate(zip(places, refs)):
        width = block.shape[1]
        slot = i % SLOTS
        if i >= SLOTS:
            copies[i - SLOTS].wait()
        if turn:
            turned = block[...].T
            for k in range(3):
                held[slot, k] = dot(turned, left_ref[k]).astype(jnp.bfloat16)
        else:
            held[slot] = dot(left_ref[...], block[...]).astype(jnp.bfloat16)
        start = pl.multiple_of(plan_ref[place] * width, 128)
        copy = pltpu.make_async_copy(
            held.at[slot], out_ref.at[:, pl.ds(start, width)], sems.at[slot]
        )
        copy.start()
        copies.append(copy)
    for copy in copies[-SLOTS:]:
        copy.wait()


def weight_grad(plan, left, blocks, shape, into=None):
    turn = left.ndim == 3
    seq, part = blocks[0][1].shape
    count = len(blocks)
    held = (3, part, left.shape[2]) if turn else (left.shape[0], part)
    vmem = pl.BlockSpec(memory_space=pltpu.VMEM)
    rest = pl.BlockSpec(memory_space=pl.ANY)
    size = math.prod(held) * count
    return pl.pallas_call(
        functools.partial(weight_kernel, [place for place, _ in blocks], turn),
        in_specs=[pl.BlockSpec(memory_space=pltpu.SMEM)]
        + [vmem] * (1 + count)
        + [rest] * (into is not None),
        out_specs=rest,
        out_shape=jax.ShapeDtypeStruct(shape, jnp.bfloat16),
        scratch_shapes=[
            pltpu.VMEM((SLOTS, *held), jnp.bfloat16),
            pltpu.SemaphoreType.DMA((SLOTS,)),
        ],
        input_output_aliases={} if into is None else {2 + count: 0},
        compiler_params=params(40),
        cost_estimate=cost(2 * seq * size, 3 * size),
    )(plan, left, *[block for _, block in blocks], *([] if into is None else [into]))


def terms_kernel(plan_ref, grad_ref, w_ref, theirs_ref, mine_ref):
    total = dot(grad_ref[0], w_ref[0], NT)
    total += dot(grad_ref[1], w_ref[1], NT)
    total += dot(grad_ref[2], w_ref[2], NT)
    total = total.astype(jnp.bfloat16)
    part = total.shape[1] // 2

    @pl.when(plan_ref[0] == 0)
    def _():
        mine_ref[0] = total[:, :part]
        theirs_ref[0] = total[:, part:]

    @pl.when(plan_ref[0] == 1)
    def _():
        mine_ref[0] = total[:, part:]
        theirs_ref[0] = total[:, :part]


def terms(plan, place, count, grad, w, part):
    _, seq, columns = grad.shape
    out = pl.BlockSpec((1, seq, part), lambda i, plan: (i, 0, 0))
    shape = jax.ShapeDtypeStruct((count, seq, part), jnp.bfloat16)
    return pl.pallas_call(
        terms_kernel,
        grid_spec=pltpu.PrefetchScalarGridSpec(
            num_scalar_prefetch=1,
            grid=(count,),
            in_specs=[
                pl.BlockSpec((3, seq, columns), lambda i, plan: (0, 0, 0)),
                pl.BlockSpec((3, 2 * part, columns), lambda i, plan: (0, plan[place + i], 0)),
            ],
            out_specs=[out, out],
        ),
        out_shape=[shape, shape],
        compiler_params=params(48),
        cost_estimate=cost(12 * seq * columns * part * count, 5 * MIB * count),
    )(plan, grad, w)


def plain(n, inputs, out_grad, w_qkv, w_out, saved_qkv, positions):
    full_in = lax.all_gather(inputs, "gx", axis=1, tiled=True)
    full_grad = lax.all_gather(out_grad, "gx", axis=1, tiled=True)
    qkv = saved_qkv.transpose(1, 0, 2)
    attn, attended, _ = attend(positions, qkv)
    grad_h = dot(full_grad, w_out, NT).astype(jnp.bfloat16)
    grad_w_out = dot(attended, full_grad, TN).astype(jnp.bfloat16)
    grad = attend_back(qkv, attn, attended, grad_h)
    grad_w_qkv = jnp.stack([dot(full_in, grad[k], TN).astype(jnp.bfloat16) for k in range(3)], 1)
    partial = sum(dot(grad[k], w_qkv[:, k], NT) for k in range(3))
    input_grad = lax.psum_scatter(partial, "gx", scatter_dimension=1, tiled=True)
    return input_grad.astype(jnp.bfloat16), grad_w_qkv, grad_w_out


def ring_order(chips):
    if chips == 8:
        return [0, 2, 4, 6, 7, 5, 3, 1]
    return list(range(chips))


def plan_of(order, device):
    chips = len(order)
    at = order.index(device // 2)
    core = device % 2

    def chip(offset):
        return order[(at + offset) % chips]

    blocks = [2 * chip(0) + core, 2 * chip(0) + 1 - core]
    for step in range(1, chips // 2):
        for shard in (core, 1 - core):
            blocks += [2 * chip(-step) + shard, 2 * chip(step) + shard]
    blocks += [2 * chip(chips // 2) + core, 2 * chip(chips // 2) + 1 - core]
    summed = [chip(chips // 2)]
    for step in range(chips // 2 - 1, 0, -1):
        summed += [chip(step), chip(-step)]
    apart = blocks[:2]
    for step in range(1, chips // 2):
        behind = step if core else -step
        for shard, first in ((core, behind), (1 - core, -behind)):
            apart += [2 * chip(first) + shard, 2 * chip(-first) + shard]
    return [core] + blocks + summed + [chip(0)] + apart + blocks[-2:]


def after(x, *others):
    return lax.optimization_barrier((x, *others))[0]


def together(*arrays):
    return lax.optimization_barrier(arrays)


def f32(x):
    return x.astype(jnp.float32)


def on_device(n, inputs, out_grad, w_qkv, w_out, saved_qkv, positions):
    part = inputs.shape[1]
    if part % 128 or n != 16:
        return plain(n, inputs, out_grad, w_qkv, w_out, saved_qkv, positions)
    order = ring_order(n // 2)
    hops = [(2 * order[i - 1], 2 * order[i]) for i in range(n // 2)]
    ahead = [(i + core, j + core) for i, j in hops for core in range(2)]
    back = [(j, i) for i, j in ahead]
    apart = [(i, j) for i, j in hops] + [(j + 1, i + 1) for i, j in hops]
    crossed = [(j, i) for i, j in apart]
    swap = [(i, i ^ 1) for i in range(n)]
    plans = [plan_of(order, i) for i in range(n)]
    size = len(plans[0])
    plan = lax.dynamic_slice(
        jnp.array(sum(plans, []), jnp.int32), (lax.axis_index("gx") * size,), (size,)
    )
    on_first = lax.axis_index("gx") % 2 == 0
    half = inputs.shape[0] // 2

    def both_ways(right, left):
        return lax.ppermute(right, "gx", ahead), lax.ppermute(left, "gx", back)

    def one_way(right, left):
        return lax.ppermute(jnp.where(on_first, right, left), "gx", apart)

    def first_chain(x):
        return lax.ppermute(x, "gx", apart)

    def second_chain(x):
        return lax.ppermute(x, "gx", crossed)

    def swapped(*arrays):
        found = [lax.ppermute(x, "gx", swap) for x in arrays]
        return found if len(found) > 1 else found[0]

    def blocks(step, *arrays):
        first = 1 if step == 0 else 4 * step - 1
        return [(first + i, array) for i, array in enumerate(arrays)]

    def in_blocks(step, *arrays):
        return [(place + 24, array) for place, array in blocks(step, *arrays)]

    def grad_qkv(index, some, into=None):
        return weight_grad(index, grad, some, w.shape, into)

    def total(*values):
        return sum(f32(value) for value in values[1:]) + f32(values[0])

    def rounded_total(*values):
        return total(*values).astype(jnp.bfloat16)

    qkv = saved_qkv.transpose(1, 0, 2)
    w = w_qkv.transpose(1, 0, 2)

    def grad_out_heads(index, some, so_far=None, last=False):
        return grad_heads(index, w_out, some, so_far, last)

    def grad_out(index, some, into=None):
        return weight_grad(index, attended_t, some, w_out.shape, into)

    r1, l1 = both_ways(out_grad, out_grad)
    other = swapped(out_grad)
    attn, attended, attended_t = attend(positions, qkv)

    r1, l1, attended, plan = together(r1, l1, attended, plan)
    r2, l2 = both_ways(r1, l1)
    g1 = blocks(1, r1, l1, *swapped(r1, l1))
    g0 = blocks(0, out_grad, other)
    out = grad_out(plan, g0 + g1)

    r2, l2, out, plan = together(r2, l2, out, plan)
    r3, l3 = both_ways(r2, l2)
    g2 = blocks(2, r2, l2, *swapped(r2, l2))
    out = grad_out(plan, g2, out)
    grad_h = grad_out_heads(after(plan, out), g0 + g1)

    r3, l3, grad_h, out, plan = together(r3, l3, grad_h, out, plan)
    x4 = one_way(r3, l3)
    i1 = first_chain(after(inputs, r3))
    r3x, l3x = swapped(r3, l3)
    g3 = blocks(3, r3, l3, r3x, l3x)
    grad_h = grad_out_heads(plan, g2, grad_h)

    grad_h, r3x, l3x, plan = together(grad_h, r3x, l3x, plan)
    grad_h = grad_out_heads(plan, g3, grad_h)
    out = grad_out(plan, g3, out)

    x4, i1, grad_h, out, plan = together(x4, i1, grad_h, out, plan)
    x4x, other = swapped(x4, inputs)
    i2, j1 = first_chain(i1), second_chain(inputs)
    f0 = in_blocks(0, inputs, other)
    g4 = blocks(4, x4, x4x)
    grad_h = grad_out_heads(plan, g4, grad_h, last=True)
    grad = attend_back(qkv, attn, attended, grad_h)

    grad, plan = together(grad, plan)
    theirs4, mine4 = terms(plan, 17, 1, grad, w, part)

    theirs4, mine4, i2, j1, other, plan = together(theirs4, mine4, i2, j1, other, plan)
    i3, j2 = first_chain(i2), second_chain(j1)
    theirs4 = swapped(theirs4)
    i1x, j1x = swapped(i1, j1)
    theirs3, mine3 = terms(plan, 18, 2, grad, w, part)
    out = grad_out(after(plan, mine3), g4, out)

    theirs3, mine3, theirs4, out, i3, j2, i1x, j1x, plan = together(
        theirs3, mine3, theirs4, out, i3, j2, i1x, j1x, plan
    )
    low = rounded_total(mine4[0], theirs4[0])
    s4, u4 = both_ways(low[:half], low[half:])
    theirs3 = swapped(theirs3)
    i4, j3 = first_chain(i3), second_chain(j2)
    theirs2, mine2 = terms(plan, 20, 2, grad, w, part)

    theirs2, mine2, theirs3, s4, u4, i4, j3, plan = together(
        theirs2, mine2, theirs3, s4, u4, i4, j3, plan
    )
    s4 = jnp.pad(s4, ((0, half), (0, 0)))
    u4 = jnp.pad(u4, ((half, 0), (0, 0)))
    s3, u3 = both_ways(
        rounded_total(mine3[0], theirs3[0], s4), rounded_total(mine3[1], theirs3[1], u4)
    )
    theirs2, i2x, j2x = swapped(theirs2, i2, j2)
    theirs1, mine1 = terms(plan, 22, 3, grad, w, part)

    theirs1, mine1, theirs2, s3, u3, i2x, j2x, plan = together(
        theirs1, mine1, theirs2, s3, u3, i2x, j2x, plan
    )
    s2, u2 = both_ways(
        rounded_total(mine2[0], theirs2[0], s3), rounded_total(mine2[1], theirs2[1], u3)
    )
    theirs1, i3x = swapped(theirs1, i3)
    i4x, j3x = swapped(i4, j3)
    some = f0 + in_blocks(1, i1, j1, i1x, j1x) + in_blocks(2, i2, j2, i2x, j2x)[:2]
    weight = grad_qkv(plan, some)

    weight, theirs1, s2, u2, i3x, i4x, j3x, plan = together(
        weight, theirs1, s2, u2, i3x, i4x, j3x, plan
    )
    s1, u1 = both_ways(
        rounded_total(mine1[0], theirs1[0], s2), rounded_total(mine1[1], theirs1[1], u2)
    )
    some = in_blocks(2, i2, j2, i2x, j2x)[2:]
    some += in_blocks(3, i3, j3, i3x, j3x) + in_blocks(4, i4, i4x)
    weight = grad_qkv(plan, some, weight)

    weight, s1, u1 = together(weight, s1, u1)
    input_grad = rounded_total(mine1[2], theirs1[2], s1, u1)
    return input_grad, weight.transpose(1, 0, 2), out


def solution(mesh):
    placed = (
        P("runs", "gx"),
        P("runs", "gx"),
        P(None, None, "gx"),
        P("gx", None),
        P("runs", None, "gx"),
        P("runs"),
    )
    return jax.shard_map(
        functools.partial(on_device, mesh.shape["gx"]),
        mesh=mesh,
        in_specs=placed,
        out_specs=(P("runs", "gx"), P("runs", None, "gx"), P(("runs", "gx"), None)),
        check_vma=False,
    )
```

```python
import functools
import math

import jax
import jax.numpy as jnp
from jax import lax
from jax.experimental import pallas as pl
from jax.experimental.pallas import tpu as pltpu
from jax.sharding import PartitionSpec as P

HD = 128
FACTOR = 1.0 / math.sqrt(HD)
MIB = 1 << 20
NT = (((1,), (1,)), ((), ()))
TN = (((0,), (0,)), ((), ()))


def dot(a, b, dims=(((1,), (0,)), ((), ()))):
    return lax.dot_general(a, b, dims, preferred_element_type=jnp.float32)


def params(mib):
    return pltpu.CompilerParams(vmem_limit_bytes=mib * MIB)


def cost(flops, nbytes, transcendentals=0):
    flops, nbytes = flops // 4096, nbytes // 4096
    return pl.CostEstimate(flops=flops, bytes_accessed=nbytes, transcendentals=transcendentals)


def attend_kernel(row_ref, qkv_ref, attn_ref, out_ref, out_t_ref, column):
    row = row_ref[...]

    @pl.when(pl.program_id(0) == 0)
    def _():
        column[...] = jnp.broadcast_to(row, (HD, row.shape[1])).T

    scores = dot(qkv_ref[0], qkv_ref[1], NT) * FACTOR
    scores = jnp.where(row <= column[:, :1], scores, -1e30)
    expd = jnp.exp(scores - jnp.max(scores, axis=1, keepdims=True))
    attn = (expd / jnp.sum(expd, axis=1, keepdims=True)).astype(jnp.bfloat16)
    attn_ref[0] = attn
    attended = dot(attn, qkv_ref[2])
    out_ref[...] = attended.astype(jnp.bfloat16)
    out_t_ref[...] = attended.T.astype(jnp.bfloat16)


def attend(positions, qkv):
    _, seq, columns = qkv.shape
    heads = columns // HD
    return pl.pallas_call(
        attend_kernel,
        grid=(heads,),
        in_specs=[
            pl.BlockSpec((1, seq), lambda h: (0, 0)),
            pl.BlockSpec((3, seq, HD), lambda h: (0, 0, h)),
        ],
        out_specs=[
            pl.BlockSpec((1, seq, seq), lambda h: (h, 0, 0)),
            pl.BlockSpec((seq, HD), lambda h: (0, h)),
            pl.BlockSpec((HD, seq), lambda h: (h, 0)),
        ],
        out_shape=[
            jax.ShapeDtypeStruct((heads, seq, seq), jnp.bfloat16),
            jax.ShapeDtypeStruct((seq, columns), jnp.bfloat16),
            jax.ShapeDtypeStruct((columns, seq), jnp.bfloat16),
        ],
        scratch_shapes=[pltpu.VMEM((seq, HD), jnp.int32)],
        compiler_params=params(60),
        cost_estimate=cost(4 * seq * seq * columns, 5 * MIB, heads * seq * seq),
    )(positions[None, :], qkv)


def attend_back_kernel(qkv_ref, attn_ref, attended_ref, grad_ref, out_ref):
    grad = grad_ref[...]
    attn = attn_ref[0]
    row_dot = jnp.sum(
        grad.astype(jnp.float32) * attended_ref[...].astype(jnp.float32), axis=1, keepdims=True
    )
    grad_attn = dot(grad, qkv_ref[2], NT)
    grad_scores = (attn.astype(jnp.float32) * (grad_attn - row_dot) * FACTOR).astype(jnp.bfloat16)
    out_ref[0] = dot(grad_scores, qkv_ref[1]).astype(jnp.bfloat16)
    out_ref[1] = dot(grad_scores, qkv_ref[0], TN).astype(jnp.bfloat16)
    out_ref[2] = dot(attn, grad, TN).astype(jnp.bfloat16)


def attend_back(qkv, attn, attended, grad):
    _, seq, columns = qkv.shape
    planes = pl.BlockSpec((3, seq, HD), lambda h: (0, 0, h))
    one = pl.BlockSpec((seq, HD), lambda h: (0, h))
    return pl.pallas_call(
        attend_back_kernel,
        grid=(columns // HD,),
        in_specs=[planes, pl.BlockSpec((1, seq, seq), lambda h: (h, 0, 0)), one, one],
        out_specs=planes,
        out_shape=jax.ShapeDtypeStruct(qkv.shape, jnp.bfloat16),
        compiler_params=params(24),
        cost_estimate=cost(8 * seq * seq * columns, 6 * MIB),
    )(qkv, attn, attended, grad)


def grad_heads_kernel(count, first, last, plan_ref, *refs):
    blocks, weights, rest = refs[:count], refs[count : 2 * count], refs[2 * count :]
    out_ref, total = rest[-2:]
    for i, (block, weight) in enumerate(zip(blocks, weights)):
        term = dot(block[...], weight[...], NT)
        if i:
            total[...] += term
        else:
            total[...] = term if first else rest[0][...] + term
    out_ref[...] = total[...].astype(jnp.bfloat16) if last else total[...]


def grad_heads(plan, w_out, blocks, total=None, last=False):
    columns = w_out.shape[0]
    seq, part = blocks[0][1].shape
    count = len(blocks)

    def weight(place):
        return pl.BlockSpec((columns, part), lambda step, plan: (0, plan[place]))

    def whole(shape):
        return pl.BlockSpec(shape, lambda step, plan: (0, 0))

    first = total is None
    return pl.pallas_call(
        functools.partial(grad_heads_kernel, count, first, last),
        grid_spec=pltpu.PrefetchScalarGridSpec(
            num_scalar_prefetch=1,
            grid=(1,),
            in_specs=[whole((seq, part))] * count
            + [weight(place) for place, _ in blocks]
            + [whole((seq, columns))] * (not first),
            out_specs=whole((seq, columns)),
            scratch_shapes=[pltpu.VMEM((seq, columns), jnp.float32)],
        ),
        out_shape=jax.ShapeDtypeStruct((seq, columns), jnp.bfloat16 if last else jnp.float32),
        compiler_params=params(40),
        cost_estimate=cost(2 * seq * columns * part * count, MIB * count),
    )(plan, *[block for _, block in blocks], *[w_out] * count, *([] if first else [total]))


SLOTS = 4


def weight_kernel(places, turn, plan_ref, left_ref, *refs):
    out_ref, held, sems = refs[-3:]
    copies = []
    for i, (place, block) in enumerate(zip(places, refs)):
        width = block.shape[1]
        slot = i % SLOTS
        if i >= SLOTS:
            copies[i - SLOTS].wait()
        if turn:
            turned = block[...].T
            for k in range(3):
                held[slot, k] = dot(turned, left_ref[k]).astype(jnp.bfloat16)
        else:
            held[slot] = dot(left_ref[...], block[...]).astype(jnp.bfloat16)
        start = pl.multiple_of(plan_ref[place] * width, 128)
        copy = pltpu.make_async_copy(
            held.at[slot], out_ref.at[:, pl.ds(start, width)], sems.at[slot]
        )
        copy.start()
        copies.append(copy)
    for copy in copies[-SLOTS:]:
        copy.wait()


def weight_grad(plan, left, blocks, shape, into=None):
    turn = left.ndim == 3
    seq, part = blocks[0][1].shape
    count = len(blocks)
    held = (3, part, left.shape[2]) if turn else (left.shape[0], part)
    vmem = pl.BlockSpec(memory_space=pltpu.VMEM)
    rest = pl.BlockSpec(memory_space=pl.ANY)
    size = math.prod(held) * count
    return pl.pallas_call(
        functools.partial(weight_kernel, [place for place, _ in blocks], turn),
        in_specs=[pl.BlockSpec(memory_space=pltpu.SMEM)]
        + [vmem] * (1 + count)
        + [rest] * (into is not None),
        out_specs=rest,
        out_shape=jax.ShapeDtypeStruct(shape, jnp.bfloat16),
        scratch_shapes=[
            pltpu.VMEM((SLOTS, *held), jnp.bfloat16),
            pltpu.SemaphoreType.DMA((SLOTS,)),
        ],
        input_output_aliases={} if into is None else {2 + count: 0},
        compiler_params=params(40),
        cost_estimate=cost(2 * seq * size, 3 * size),
    )(plan, left, *[block for _, block in blocks], *([] if into is None else [into]))


def terms_kernel(plan_ref, grad_ref, w_ref, theirs_ref, mine_ref):
    total = dot(grad_ref[0], w_ref[0], NT)
    total += dot(grad_ref[1], w_ref[1], NT)
    total += dot(grad_ref[2], w_ref[2], NT)
    total = total.astype(jnp.bfloat16)
    part = total.shape[1] // 2

    @pl.when(plan_ref[0] == 0)
    def _():
        mine_ref[0] = total[:, :part]
        theirs_ref[0] = total[:, part:]

    @pl.when(plan_ref[0] == 1)
    def _():
        mine_ref[0] = total[:, part:]
        theirs_ref[0] = total[:, :part]


def terms(plan, place, count, grad, w, part):
    _, seq, columns = grad.shape
    out = pl.BlockSpec((1, seq, part), lambda i, plan: (i, 0, 0))
    shape = jax.ShapeDtypeStruct((count, seq, part), jnp.bfloat16)
    return pl.pallas_call(
        terms_kernel,
        grid_spec=pltpu.PrefetchScalarGridSpec(
            num_scalar_prefetch=1,
            grid=(count,),
            in_specs=[
                pl.BlockSpec((3, seq, columns), lambda i, plan: (0, 0, 0)),
                pl.BlockSpec((3, 2 * part, columns), lambda i, plan: (0, plan[place + i], 0)),
            ],
            out_specs=[out, out],
        ),
        out_shape=[shape, shape],
        compiler_params=params(48),
        cost_estimate=cost(12 * seq * columns * part * count, 5 * MIB * count),
    )(plan, grad, w)


def plain(n, inputs, out_grad, w_qkv, w_out, saved_qkv, positions):
    full_in = lax.all_gather(inputs, "gx", axis=1, tiled=True)
    full_grad = lax.all_gather(out_grad, "gx", axis=1, tiled=True)
    qkv = saved_qkv.transpose(1, 0, 2)
    attn, attended, _ = attend(positions, qkv)
    grad_h = dot(full_grad, w_out, NT).astype(jnp.bfloat16)
    grad_w_out = dot(attended, full_grad, TN).astype(jnp.bfloat16)
    grad = attend_back(qkv, attn, attended, grad_h)
    grad_w_qkv = jnp.stack([dot(full_in, grad[k], TN).astype(jnp.bfloat16) for k in range(3)], 1)
    partial = sum(dot(grad[k], w_qkv[:, k], NT) for k in range(3))
    input_grad = lax.psum_scatter(partial, "gx", scatter_dimension=1, tiled=True)
    return input_grad.astype(jnp.bfloat16), grad_w_qkv, grad_w_out


def ring_order(chips):
    if chips == 8:
        return [0, 2, 4, 6, 7, 5, 3, 1]
    return list(range(chips))


def plan_of(order, device):
    chips = len(order)
    at = order.index(device // 2)
    core = device % 2

    def chip(offset):
        return order[(at + offset) % chips]

    blocks = [2 * chip(0) + core, 2 * chip(0) + 1 - core]
    for step in range(1, chips // 2):
        for shard in (core, 1 - core):
            blocks += [2 * chip(-step) + shard, 2 * chip(step) + shard]
    blocks += [2 * chip(chips // 2) + core, 2 * chip(chips // 2) + 1 - core]
    summed = [chip(chips // 2)]
    for step in range(chips // 2 - 1, 0, -1):
        summed += [chip(step), chip(-step)]
    apart = blocks[:2]
    for step in range(1, chips // 2):
        behind = step if core else -step
        for shard, first in ((core, behind), (1 - core, -behind)):
            apart += [2 * chip(first) + shard, 2 * chip(-first) + shard]
    return [core] + blocks + summed + [chip(0)] + apart + blocks[-2:]


def after(x, *others):
    return lax.optimization_barrier((x, *others))[0]


def together(*arrays):
    return lax.optimization_barrier(arrays)


def f32(x):
    return x.astype(jnp.float32)


def on_device(n, inputs, out_grad, w_qkv, w_out, saved_qkv, positions):
    part = inputs.shape[1]
    if part % 128 or n != 16:
        return plain(n, inputs, out_grad, w_qkv, w_out, saved_qkv, positions)
    order = ring_order(n // 2)
    hops = [(2 * order[i - 1], 2 * order[i]) for i in range(n // 2)]
    ahead = [(i + core, j + core) for i, j in hops for core in range(2)]
    back = [(j, i) for i, j in ahead]
    apart = [(i, j) for i, j in hops] + [(j + 1, i + 1) for i, j in hops]
    crossed = [(j, i) for i, j in apart]
    swap = [(i, i ^ 1) for i in range(n)]
    plans = [plan_of(order, i) for i in range(n)]
    size = len(plans[0])
    plan = lax.dynamic_slice(
        jnp.array(sum(plans, []), jnp.int32), (lax.axis_index("gx") * size,), (size,)
    )
    on_first = lax.axis_index("gx") % 2 == 0
    half = inputs.shape[0] // 2

    def both_ways(right, left):
        return lax.ppermute(right, "gx", ahead), lax.ppermute(left, "gx", back)

    def one_way(right, left):
        return lax.ppermute(jnp.where(on_first, right, left), "gx", apart)

    def first_chain(x):
        return lax.ppermute(x, "gx", apart)

    def second_chain(x):
        return lax.ppermute(x, "gx", crossed)

    def swapped(*arrays):
        found = [lax.ppermute(x, "gx", swap) for x in arrays]
        return found if len(found) > 1 else found[0]

    def blocks(step, *arrays):
        first = 1 if step == 0 else 4 * step - 1
        return [(first + i, array) for i, array in enumerate(arrays)]

    def in_blocks(step, *arrays):
        return [(place + 24, array) for place, array in blocks(step, *arrays)]

    def grad_qkv(index, some, into=None):
        return weight_grad(index, grad, some, w.shape, into)

    def total(*values):
        return sum(f32(value) for value in values[1:]) + f32(values[0])

    def rounded_total(*values):
        return total(*values).astype(jnp.bfloat16)

    qkv = saved_qkv.transpose(1, 0, 2)
    w = w_qkv.transpose(1, 0, 2)

    def grad_out_heads(index, some, so_far=None, last=False):
        return grad_heads(index, w_out, some, so_far, last)

    def grad_out(index, some, into=None):
        return weight_grad(index, attended_t, some, w_out.shape, into)

    r1, l1 = both_ways(out_grad, out_grad)
    other = swapped(out_grad)
    attn, attended, attended_t = attend(positions, qkv)

    r1, l1, attended, plan = together(r1, l1, attended, plan)
    r2, l2 = both_ways(r1, l1)
    g1 = blocks(1, r1, l1, *swapped(r1, l1))
    g0 = blocks(0, out_grad, other)
    out = grad_out(plan, g0)

    r2, l2, out, plan = together(r2, l2, out, plan)
    r3, l3 = both_ways(r2, l2)
    g2 = blocks(2, r2, l2, *swapped(r2, l2))
    grad_h = grad_out_heads(plan, g0 + g1)
    out = grad_out(plan, g1, out)

    r3, l3, grad_h, out, plan = together(r3, l3, grad_h, out, plan)
    x4 = one_way(r3, l3)
    i1 = first_chain(after(inputs, r3))
    r3x, l3x = swapped(r3, l3)
    g3 = blocks(3, r3, l3, r3x, l3x)
    grad_h = grad_out_heads(plan, g2, grad_h)

    grad_h, r3x, l3x, plan = together(grad_h, r3x, l3x, plan)
    out = grad_out(plan, g2, out)
    grad_h = grad_out_heads(plan, g3, grad_h)

    x4, i1, grad_h, out, plan = together(x4, i1, grad_h, out, plan)
    x4x = swapped(x4)
    i2, j1 = first_chain(i1), second_chain(inputs)
    g4 = blocks(4, x4, x4x)
    grad_h = grad_out_heads(plan, g4, grad_h, last=True)
    grad = attend_back(qkv, attn, attended, grad_h)

    grad, inputs, plan = together(grad, inputs, plan)
    other = swapped(inputs)
    f0 = in_blocks(0, inputs, other)
    out = grad_out(plan, g3, out)

    out, i2, j1, other, plan = together(out, i2, j1, other, plan)
    i3, j2 = first_chain(i2), second_chain(j1)
    i1x, j1x, i2x = swapped(i1, j1, i2)
    theirs3, mine3 = terms(plan, 17, 3, grad, w, part)

    theirs3, mine3, i3, j2, i1x, j1x, plan = together(theirs3, mine3, i3, j2, i1x, j1x, plan)
    theirs3 = swapped(theirs3)
    i4, j3 = first_chain(i3), second_chain(j2)
    j2x = swapped(j2)
    out = grad_out(plan, g4, out)

    out, theirs3, plan = together(out, theirs3, plan)
    low = rounded_total(mine3[0], theirs3[0])
    s4, u4 = both_ways(low[:half], low[half:])
    theirs2, mine2 = terms(plan, 20, 2, grad, w, part)

    theirs2, mine2, s4, u4, i4, j3, i2x, j2x, plan = together(
        theirs2, mine2, s4, u4, i4, j3, i2x, j2x, plan
    )
    s4 = jnp.pad(s4, ((0, half), (0, 0)))
    u4 = jnp.pad(u4, ((half, 0), (0, 0)))
    s3, u3 = both_ways(
        rounded_total(mine3[1], theirs3[1], s4), rounded_total(mine3[2], theirs3[2], u4)
    )
    theirs2, i3x = swapped(theirs2, i3)
    theirs1, mine1 = terms(plan, 22, 3, grad, w, part)

    theirs1, mine1, theirs2, s3, u3, i3x, plan = together(
        theirs1, mine1, theirs2, s3, u3, i3x, plan
    )
    s2, u2 = both_ways(
        rounded_total(mine2[0], theirs2[0], s3), rounded_total(mine2[1], theirs2[1], u3)
    )
    theirs1, i4x, j3x = swapped(theirs1, i4, j3)
    some = f0 + in_blocks(1, i1, j1, i1x, j1x) + in_blocks(2, i2, j2, i2x, j2x)[:2]
    weight = grad_qkv(plan, some)

    weight, theirs1, s2, u2, i4x, j3x, plan = together(weight, theirs1, s2, u2, i4x, j3x, plan)
    s1, u1 = both_ways(
        rounded_total(mine1[0], theirs1[0], s2), rounded_total(mine1[1], theirs1[1], u2)
    )
    some = in_blocks(2, i2, j2, i2x, j2x)[2:]
    some += in_blocks(3, i3, j3, i3x, j3x) + in_blocks(4, i4, i4x)
    weight = grad_qkv(plan, some, weight)

    weight, s1, u1 = together(weight, s1, u1)
    input_grad = rounded_total(mine1[2], theirs1[2], s1, u1)
    return input_grad, weight.transpose(1, 0, 2), out


def solution(mesh):
    placed = (
        P("runs", "gx"),
        P("runs", "gx"),
        P(None, None, "gx"),
        P("gx", None),
        P("runs", None, "gx"),
        P("runs"),
    )
    return jax.shard_map(
        functools.partial(on_device, mesh.shape["gx"]),
        mesh=mesh,
        in_specs=placed,
        out_specs=(P("runs", "gx"), P("runs", None, "gx"), P(("runs", "gx"), None)),
        check_vma=False,
    )
```
